32 devices in a mesh: groups: 2 (over x), dp: 16 (over z, y, core).
Axes of the slice: x: 2, y: 2, z: 4, core: 2. Of those that a mesh axis runs over, the one named last changes fastest.
Arguments:
- acts: bfloat16 [5120, 8192], P(('groups', 'dp')), parts along dimension 0, may hold values from -6 to 6
- grads: bfloat16 [5120, 32768], P(('groups', 'dp')), parts along dimension 0, may hold values from -6 to 6
- out_factors: bfloat16 [65536, 256], P(('groups', 'dp')), parts along dimension 0, may hold values from -0.03125 to 0.03125
- in_factors: bfloat16 [16384, 256], P(('groups', 'dp')), parts along dimension 0, may hold values from -0.0625 to 0.0625
- seq_slot: int32 [64], P(('groups', 'dp')), parts along dimension 0, may hold values from 0 to 31, each once
- lengths: int32 [64], P(('groups', 'dp')), parts along dimension 0, may hold values from 1 to 80, 2240 in all
Outputs:
- influence: float32 [64, 8], P(('groups', 'dp')), parts along dimension 0
The draws below stay inside these ranges and needn't reach their ends.
There are 2 independent parts, one for each index of `groups`. The reference program is written for one: setup_inputs(seed, part) draws one part's arguments, and reference() takes and returns one part's arrays. A program takes and returns all parts, laid end to end along the dimension named above; each array names one. Nothing has to cross between parts.
Inputs may be any that keep to these rules, and one draw needn't show every extreme that they name: seq_slot is a permutation of 0 to 31. `lengths`: some slot has exactly 80 tokens.
All inputs are finite; a program needn't handle non-finite values. No bound on the sum of `lengths` on one device may be relied on, other than what follows from the above.
Results may differ from the reference program's by a relative error of at most 0.0003.
Values may be sent and summed in bfloat16 or wider, within the bound.
No kernel may reach another device: no remote copies, remote signals or barrier semaphores. Data moves between devices by JAX's collectives and lax.ppermute only.
A program may use at most 128 MiB of HBM per device.

```python
import math
import jax
import jax.numpy as jnp
import numpy as np
from jax import lax

D_IN = 8192
D_OUT = 32768
RANK = 32
NQ = 8
LEN = 80
NSEQ = 32
TOKENS = 2560


def steps_of(stream_key, extent, pieces, least, high):
    def one(dim, blocks):
        draws = jax.random.uniform(jax.random.fold_in(jax.random.fold_in(stream_key, 6), dim), (blocks,), jnp.float32, least / len(pieces), high / len(pieces))
        return jnp.repeat(jnp.exp(draws), extent[dim] // blocks).reshape((-1,) + (1,) * (len(extent) - dim - 1))

    level = one(*pieces[0])
    for cut in pieces[1:]:
        level = level * one(*cut)
    return level


def profile(amount, total, bound, skew):
    weights = [(1 << 20) // math.isqrt(grade ** skew) + 1 for grade in range(2, amount + 1)]
    spare, counts = total - bound - (amount - 1), [1] * (amount - 1)
    while spare > 0:
        free = [i for i in range(amount - 1) if counts[i] < bound]
        whole, budget = sum([weights[i] for i in free]), spare
        for i in free:
            more = min(bound - counts[i], max(1, budget * weights[i] // whole), spare)
            counts[i] = counts[i] + more
            spare = spare - more
    return np.array([bound] + counts)


def ragged(own_key, number_of, total, most, lean):
    if number_of == 2:
        one = jax.random.randint(own_key, (), max(1, total - most), min(most, total - 1) + 1)
        return jnp.stack([one, total - one])
    sizes = jnp.asarray(profile(number_of, total, most, lean), jnp.int32)
    pairs = (number_of - 1) // 2
    donor, taker = sizes[1:1 + 2 * pairs:2], sizes[2:2 + 2 * pairs:2]
    margin = jnp.minimum(donor - 1, most - taker)
    moved = jax.random.randint(jax.random.fold_in(own_key, 1), (pairs,), 0, 1 << 20) % (margin + 1)
    sizes = sizes.at[1:1 + 2 * pairs:2].set(donor - moved).at[2:2 + 2 * pairs:2].set(taker + moved)
    return sizes[jax.random.permutation(jax.random.fold_in(own_key, 2), number_of)]


def noise(own_key, extent, scale, limit, split=(), kind=jnp.bfloat16):
    drawn = jax.random.normal(own_key, extent, jnp.float32) * scale
    if len(split) > 0:
        drawn = steps_of(own_key, extent, split, -0.22, 0.18) * drawn
    return jnp.clip(drawn, min=-limit, max=limit).astype(kind)


def setup_inputs(seed: int = 0, part: int = 0) -> dict:
    splits = jax.random.split(jax.random.key(seed), 7)
    part_splits = jax.random.split(jax.random.fold_in(splits[6], part), 7)
    return {
        "acts": noise(part_splits[0], (TOKENS, D_IN), 1.0, 6.0, ((0, 16),)),
        "grads": noise(part_splits[1], (TOKENS, D_OUT), 1.0, 6.0, ((0, 16),)),
        "out_factors": noise(part_splits[2], (D_OUT, NQ * RANK), D_OUT ** -0.5, 0.03125, ((0, 16),)),
        "in_factors": noise(part_splits[3], (D_IN, NQ * RANK), D_IN ** -0.5, 0.0625, ((0, 16),)),
        "seq_slot": jax.random.permutation(part_splits[4], NSEQ).astype(jnp.int32),
        "lengths": ragged(part_splits[5], NSEQ, (7 * NSEQ * LEN) // 8, LEN, 1).astype(jnp.int32),
    }


def reference(acts, grads, out_factors, in_factors, seq_slot, lengths):
    proj_out = jnp.dot(grads, out_factors, preferred_element_type=jnp.float32)
    proj_in = jnp.dot(acts, in_factors, preferred_element_type=jnp.float32)
    contrib = (proj_out * proj_in).reshape(NSEQ, LEN, NQ, RANK).sum(axis=3)
    position = jnp.arange(LEN, dtype=jnp.int32)
    keep = (position[None, :] < lengths[:, None]).astype(jnp.float32)
    slot_score = lax.optimization_barrier(jnp.sum(contrib * keep[:, :, None], axis=1)) / math.sqrt(RANK * LEN)
    influence = jnp.zeros((NSEQ, NQ), jnp.float32).at[seq_slot].set(slot_score)
    return influence
```

```python
import functools
import math

import jax
import jax.numpy as jnp
import numpy as np
from jax import lax
from jax.experimental import pallas as pl
from jax.experimental.pallas import tpu as pltpu
from jax.sharding import PartitionSpec as P

RANK = 32
LEN = 80
F32 = jnp.float32


def ring_of(chips):
    cols = max([d for d in range(1, math.isqrt(chips) + 1) if chips % d == 0 and d % 2 == 0] or [1])
    rows = chips // cols
    if cols == 1 or rows % 2:
        return list(range(chips))
    walk = []
    for r in range(rows):
        line = range(1, cols) if r % 2 == 0 else range(cols - 1, 0, -1)
        walk += [r * cols + c for c in line]
    return walk + [r * cols for r in reversed(range(rows))]


def block_orders(chips):
    ring = ring_of(chips)
    order = np.zeros((2 * chips, chips), np.int32)
    for p, chip in enumerate(ring):
        for s in range(chips):
            order[2 * chip, s] = 2 * ring[(p - s) % chips]
            order[2 * chip + 1, s] = 2 * ring[(p + s) % chips] + 1
    return order


def ring_pairs(chips):
    ring = ring_of(chips)
    pairs = []
    for p, chip in enumerate(ring):
        pairs.append((2 * chip, 2 * ring[(p + 1) % chips]))
        pairs.append((2 * chip + 1, 2 * ring[(p - 1) % chips] + 1))
    return pairs


def pack_kernel(order_ref, own_ref, out_ref):
    out_ref[...] = own_ref[...]


def pack(order, own, rows):
    tokens, steps = own.shape[0], order.shape[0]
    return pl.pallas_call(
        pack_kernel,
        grid_spec=pltpu.PrefetchScalarGridSpec(
            num_scalar_prefetch=1,
            grid=(steps,),
            in_specs=[pl.BlockSpec((tokens, rows), lambda s, o: (0, o[s]))],
            out_specs=pl.BlockSpec((tokens, rows), lambda s, o: (0, s)),
        ),
        out_shape=jax.ShapeDtypeStruct((tokens, steps * rows), own.dtype),
        cost_estimate=pl.CostEstimate(
            flops=0, bytes_accessed=4 * tokens * steps * rows, transcendentals=0
        ),
        name="pack",
    )(order, own)


def step_kernel(first, order_ref, own_ref, sib_ref, block_ref, *refs):
    out_ref = refs[-1]
    tokens = own_ref.shape[0]
    block = block_ref[...]
    own = jnp.dot(own_ref[...], block, preferred_element_type=F32)
    sib = jnp.dot(sib_ref[...], block, preferred_element_type=F32)
    if first:
        out_ref[:tokens] = own
        out_ref[tokens:] = sib
    else:
        out_ref[:tokens] = refs[0][:tokens] + own
        out_ref[tokens:] = refs[0][tokens:] + sib


def step(order, own, sib, block, total, s, part, parts):
    tokens, columns = own.shape[0], block.shape[1]
    depth = block.shape[0]
    whole = pl.BlockSpec((2 * tokens, columns), lambda i, o: (0, 0))
    in_specs = [
        pl.BlockSpec((tokens, depth), lambda i, o: (0, o[s] * parts + part)),
        pl.BlockSpec((tokens, depth), lambda i, o: (0, s * parts + part)),
        pl.BlockSpec((depth, columns), lambda i, o: (0, 0)),
    ]
    args = [order, own, sib, block]
    if total is not None:
        in_specs.append(whole)
        args.append(total)
    return pl.pallas_call(
        functools.partial(step_kernel, total is None),
        grid_spec=pltpu.PrefetchScalarGridSpec(
            num_scalar_prefetch=1, grid=(1,), in_specs=in_specs, out_specs=whole
        ),
        out_shape=jax.ShapeDtypeStruct((2 * tokens, columns), F32),
        cost_estimate=pl.CostEstimate(
            flops=4 * tokens * depth * columns,
            bytes_accessed=2 * depth * (2 * tokens + columns),
            transcendentals=0,
        ),
        name="step",
    )(*args)


def score_kernel(terms, seq_ref, len_ref, *refs):
    outs, inns, table_ref = refs[:terms], refs[terms:-1], refs[-1]
    tokens, columns = outs[-1].shape
    slots = tokens // LEN
    queries = columns // RANK
    contrib = sum(r[:tokens] for r in outs) * sum(r[:tokens] for r in inns)
    column = lax.broadcasted_iota(jnp.int32, (columns, queries), 0) // RANK
    query = lax.broadcasted_iota(jnp.int32, (columns, queries), 1)
    fold = (column == query).astype(F32)
    position = lax.broadcasted_iota(jnp.int32, (LEN, columns), 0)
    row = lax.broadcasted_iota(jnp.int32, table_ref.shape, 0)
    table = jnp.zeros(table_ref.shape, F32)
    for i in range(slots):
        kept = jnp.where(position < len_ref[i], contrib[i * LEN:(i + 1) * LEN], 0.0)
        summed = jnp.sum(kept, axis=0, keepdims=True)
        score = jnp.dot(
            summed, fold, precision=lax.Precision.HIGHEST, preferred_element_type=F32
        ) * (1.0 / math.sqrt(RANK * LEN))
        table = jnp.where(row == seq_ref[i], score, table)
    table_ref[...] = table


def score_table(seq_slot, lengths, outs, inns, rows, queries):
    vmem = pl.BlockSpec(memory_space=pltpu.VMEM)
    smem = pl.BlockSpec(memory_space=pltpu.SMEM)
    return pl.pallas_call(
        functools.partial(score_kernel, len(outs)),
        in_specs=[smem, smem] + [vmem] * (len(outs) + len(inns)),
        out_specs=vmem,
        out_shape=jax.ShapeDtypeStruct((rows, queries), F32),
        name="score",
    )(seq_slot, lengths, *outs, *inns)


def shards(acts, grads, out_factors, in_factors, seq_slot, lengths):
    devices = lax.axis_size("dp")
    chips = devices // 2
    me = lax.axis_index("dp")
    tokens = grads.shape[0]
    rows, columns = out_factors.shape
    rows_in = in_factors.shape[0]
    orders = jnp.asarray(block_orders(chips))
    mine = lax.dynamic_index_in_dim(orders, me, keepdims=False)
    theirs = lax.dynamic_index_in_dim(orders, me ^ 1, keepdims=False)
    pairs = ring_pairs(chips)
    swap = [(d, d ^ 1) for d in range(devices)]

    parts = 2 if rows >= 1024 else 1
    depth = rows // parts
    held = [out_factors[i * depth:(i + 1) * depth] for i in range(parts)]

    ring_in = rows_in % 128 == 0
    sib_grads = lax.ppermute(pack(theirs, grads, rows), "dp", swap)
    if ring_in:
        sib_acts = lax.ppermute(pack(theirs, acts, rows_in), "dp", swap)
        held.append(in_factors)

    out = inn = None
    for s in range(chips):
        coming = [lax.ppermute(b, "dp", pairs) for b in held] if s < chips - 1 else None
        for i in range(parts):
            out = step(mine, grads, sib_grads, held[i], out, s, i, parts)
        if ring_in:
            inn = step(mine, acts, sib_acts, held[parts], inn, s, 0, 1)
        held = coming

    if ring_in:
        inns = [inn, lax.ppermute(inn[tokens:], "dp", swap)]
    else:
        every = lax.all_gather(in_factors, "dp", axis=0, tiled=True)
        inns = [jnp.dot(acts, every, preferred_element_type=F32)]
    outs = [out, lax.ppermute(out[tokens:], "dp", swap)]
    slots = lengths.shape[0]
    queries = columns // RANK
    table = score_table(seq_slot, lengths, outs, inns, slots * devices, queries)
    got = lax.all_to_all(table.reshape(devices, slots, queries), "dp", 0, 0, tiled=True)
    return jnp.sum(got, axis=0)


def solution(mesh):
    return jax.shard_map(
        shards,
        mesh=mesh,
        in_specs=(
            P(("groups", "dp"), None),
            P(("groups", "dp"), None),
            P(("groups", "dp"), None),
            P(("groups", "dp"), None),
            P(("groups", "dp")),
            P(("groups", "dp")),
        ),
        out_specs=P(("groups", "dp"), None),
        check_vma=False,
    )
```

```python
import functools
import math

import jax
import jax.numpy as jnp
import numpy as np
from jax import lax
from jax.experimental import pallas as pl
from jax.experimental.pallas import tpu as pltpu
from jax.sharding import PartitionSpec as P

RANK = 32
LEN = 80
F32 = jnp.float32
VMEM = 20 << 20


def ring_of(chips):
    cols = max([d for d in range(1, math.isqrt(chips) + 1) if chips % d == 0 and d % 2 == 0] or [1])
    rows = chips // cols
    if cols == 1 or rows % 2:
        return list(range(chips))
    walk = []
    for r in range(rows):
        line = range(1, cols) if r % 2 == 0 else range(cols - 1, 0, -1)
        walk += [r * cols + c for c in line]
    return walk + [r * cols for r in reversed(range(rows))]


def block_orders(chips):
    ring = ring_of(chips)
    order = np.zeros((2 * chips, chips), np.int32)
    for p, chip in enumerate(ring):
        for s in range(chips):
            order[2 * chip, s] = 2 * ring[(p - s) % chips]
            order[2 * chip + 1, s] = 2 * ring[(p + s) % chips] + 1
    return order


def ring_pairs(chips):
    ring = ring_of(chips)
    pairs = []
    for p, chip in enumerate(ring):
        pairs.append((2 * chip, 2 * ring[(p + 1) % chips]))
        pairs.append((2 * chip + 1, 2 * ring[(p - 1) % chips] + 1))
    return pairs


def dot(a, b):
    return jnp.dot(a, b, preferred_element_type=F32)


def call(kernel, order, windows, whole, scalars, out_shape, flops, name):
    in_specs = [pl.BlockSpec((x.shape[0], w), at) for x, w, at in windows]
    in_specs += [pl.BlockSpec(x.shape, lambda i, o: (0, 0)) for x in whole]
    in_specs += [pl.BlockSpec(memory_space=pltpu.SMEM) for _ in scalars]
    size = sum(2 * x.shape[0] * w for x, w, _ in windows)
    size += sum(x.size * x.dtype.itemsize for x in list(whole) + list(out_shape))
    return pl.pallas_call(
        kernel,
        grid_spec=pltpu.PrefetchScalarGridSpec(
            num_scalar_prefetch=1,
            grid=(1,),
            in_specs=in_specs,
            out_specs=[pl.BlockSpec(x.shape, lambda i, o: (0, 0)) for x in out_shape],
        ),
        out_shape=out_shape,
        cost_estimate=pl.CostEstimate(flops=flops, bytes_accessed=size, transcendentals=0),
        compiler_params=pltpu.CompilerParams(vmem_limit_bytes=VMEM),
        name=name,
    )(order, *[x for x, _, _ in windows], *whole, *scalars)


def step_kernel(lead, rows_in, with_b, summed, order_ref, *refs):
    refs = list(refs)
    own_g, sib_g = refs.pop(0), refs.pop(0)
    own_a, sib_a = (refs.pop(0), refs.pop(0)) if rows_in else (None, None)
    a_ref = refs.pop(0)
    b_ref = refs.pop(0) if with_b else None
    tokens = own_g.shape[0]
    for k, (g, a) in enumerate(((own_g, own_a), (sib_g, sib_a))):
        at = pl.ds(k * tokens, tokens)
        out = dot(g[:, :lead], a_ref[rows_in:])
        if with_b:
            out += dot(g[:, lead:], b_ref[...])
        if summed:
            out += refs[0][at]
        if rows_in:
            inn = dot(a[...], a_ref[:rows_in])
            if summed:
                inn += refs[1][at]
            refs[-1][at] = inn
            refs[-2][at] = out
        else:
            refs[-1][at] = out


def step(order, own, sib, blocks, totals, s, lead, rows, rows_in):
    here = lambda i, o: (0, o[s])
    windows = [(own[0], rows, here), (sib[0], rows, here)]
    if rows_in:
        windows += [(own[1], rows_in, here), (sib[1], rows_in, here)]
    tokens, columns = own[0].shape[0], blocks[0].shape[1]
    depth = sum(b.shape[0] for b in blocks)
    shape = jax.ShapeDtypeStruct((2 * tokens, columns), F32)
    return call(
        functools.partial(step_kernel, lead, rows_in, len(blocks) > 1, bool(totals)),
        order, windows, list(blocks) + list(totals), [],
        [shape] * (2 if rows_in else 1), 4 * tokens * depth * columns, "step",
    )


def score_kernel(lead, order_ref, own_g, sib_g, b_ref, out_ref, inn_ref, got_ref,
                 seq_ref, len_ref, seq_sib, len_sib, table_ref):
    tokens = own_g.shape[0]
    columns = b_ref.shape[1]
    queries = columns // RANK
    column = lax.broadcasted_iota(jnp.int32, (columns, queries), 0) // RANK
    query = lax.broadcasted_iota(jnp.int32, (columns, queries), 1)
    fold = (column == query).astype(F32)
    position = lax.broadcasted_iota(jnp.int32, (LEN, columns), 0)
    row = lax.broadcasted_iota(jnp.int32, table_ref.shape, 0)
    table = jnp.zeros(table_ref.shape, F32)
    for k, (g, seq, lens) in enumerate(((own_g, seq_ref, len_ref), (sib_g, seq_sib, len_sib))):
        mine, other = pl.ds(k * tokens, tokens), pl.ds((1 - k) * tokens, tokens)
        out = out_ref[mine] + dot(g[:, lead:], b_ref[...])
        contrib = out * (inn_ref[mine] + got_ref[other])
        for i in range(tokens // LEN):
            kept = jnp.where(position < lens[i], contrib[i * LEN:(i + 1) * LEN], 0.0)
            summed = jnp.sum(kept, axis=0, keepdims=True)
            score = jnp.dot(
                summed, fold, precision=lax.Precision.HIGHEST, preferred_element_type=F32
            ) * (1.0 / math.sqrt(RANK * LEN))
            table = jnp.where(row == seq[i], score, table)
    table_ref[...] = table


def shards(acts, grads, out_factors, in_factors, seq_slot, lengths):
    devices = lax.axis_size("dp")
    chips = devices // 2
    me = lax.axis_index("dp")
    tokens = grads.shape[0]
    rows, columns = out_factors.shape
    rows_in = in_factors.shape[0]
    orders = jnp.asarray(block_orders(chips))
    mine = lax.dynamic_index_in_dim(orders, me, keepdims=False)
    pairs = ring_pairs(chips)
    swap = [(d, d ^ 1) for d in range(devices)]

    own = [grads, acts]
    every = None
    if rows_in % 128:
        every = lax.all_gather(in_factors, "dp", axis=0, tiled=True)
        own, rows_in = own[:1], 0
    lead = (rows - rows_in) // 2
    first = out_factors[:lead]
    if rows_in:
        first = jnp.concatenate([in_factors, first])
    held = [(first, out_factors[lead:])]

    seq_sib, len_sib = lax.ppermute(jnp.stack([seq_slot, lengths]), "dp", swap)
    sib = [lax.ppermute(x, "dp", swap) for x in own]

    totals, summed = [], 0

    def sum_to(k, totals, summed):
        for j in range(summed, k):
            totals = step(mine, own, sib, held[j], totals, j, lead, rows, rows_in)
        return totals, max(k, summed)

    for s in range(chips - 1):
        a, b = held[s]
        if s >= 3:
            totals, summed = sum_to(min(2 * s - 5, s), totals, summed)
            a, *totals = lax.optimization_barrier((a, *totals))
            b, *totals = lax.optimization_barrier((b, *totals))
        held.append((lax.ppermute(a, "dp", pairs), lax.ppermute(b, "dp", pairs)))
    totals, summed = sum_to(chips - 1, totals, summed)
    s = chips - 1
    a, b = held[s]
    totals = step(mine, own, sib, [a], totals, s, lead, rows, rows_in)
    if every is not None:
        inn = dot(acts, every)
        totals = [totals[0], jnp.concatenate([inn, jnp.zeros_like(inn)])]
    got = lax.ppermute(totals[1], "dp", swap)

    slots = lengths.shape[0]
    queries = columns // RANK
    windows = [(x, rows, lambda i, o: (0, o[s])) for x in (grads, sib[0])]
    table = call(
        functools.partial(score_kernel, lead), mine, windows, [b, *totals, got],
        [seq_slot, lengths, seq_sib, len_sib],
        [jax.ShapeDtypeStruct((slots * devices, queries), F32)],
        4 * tokens * rows * columns, "score",
    )[0]
    got = lax.all_to_all(table.reshape(devices, slots, queries), "dp", 0, 0, tiled=True)
    return jnp.sum(got, axis=0)


def solution(mesh):
    return jax.shard_map(
        shards,
        mesh=mesh,
        in_specs=(
            P(("groups", "dp"), None),
            P(("groups", "dp"), None),
            P(("groups", "dp"), None),
            P(("groups", "dp"), None),
            P(("groups", "dp")),
            P(("groups", "dp")),
        ),
        out_specs=P(("groups", "dp"), None),
        check_vma=False,
    )
```

```python
import functools
import math

import jax
import jax.numpy as jnp
import numpy as np
from jax import lax
from jax.experimental import pallas as pl
from jax.experimental.pallas import tpu as pltpu
from jax.sharding import PartitionSpec as P

RANK = 32
LEN = 80
F32 = jnp.float32
VMEM = 26 << 20


def ring_of(chips):
    cols = max([d for d in range(1, math.isqrt(chips) + 1) if chips % d == 0 and d % 2 == 0] or [1])
    rows = chips // cols
    if cols == 1 or rows % 2:
        return list(range(chips))
    walk = []
    for r in range(rows):
        line = range(1, cols) if r % 2 == 0 else range(cols - 1, 0, -1)
        walk += [r * cols + c for c in line]
    return walk + [r * cols for r in reversed(range(rows))]


def block_orders(chips):
    ring = ring_of(chips)
    order = np.zeros((2 * chips, chips), np.int32)
    for p, chip in enumerate(ring):
        for s in range(chips):
            order[2 * chip, s] = 2 * ring[(p - s) % chips]
            order[2 * chip + 1, s] = 2 * ring[(p + s) % chips] + 1
    return order


def ring_pairs(chips):
    ring = ring_of(chips)
    pairs = []
    for p, chip in enumerate(ring):
        pairs.append((2 * chip, 2 * ring[(p + 1) % chips]))
        pairs.append((2 * chip + 1, 2 * ring[(p - 1) % chips] + 1))
    return pairs


def dot(a, b):
    return jnp.dot(a, b, preferred_element_type=F32)


def call(kernel, order, windows, whole, scalars, out_shape, flops, name):
    in_specs = [pl.BlockSpec((x.shape[0], w), at) for x, w, at in windows]
    in_specs += [pl.BlockSpec(x.shape, lambda i, o: (0, 0)) for x in whole]
    in_specs += [pl.BlockSpec(memory_space=pltpu.SMEM) for _ in scalars]
    size = sum(2 * x.shape[0] * w for x, w, _ in windows)
    size += sum(x.size * x.dtype.itemsize for x in list(whole) + list(out_shape))
    return pl.pallas_call(
        kernel,
        grid_spec=pltpu.PrefetchScalarGridSpec(
            num_scalar_prefetch=1,
            grid=(1,),
            in_specs=in_specs,
            out_specs=[pl.BlockSpec(x.shape, lambda i, o: (0, 0)) for x in out_shape],
        ),
        out_shape=out_shape,
        cost_estimate=pl.CostEstimate(flops=flops, bytes_accessed=size, transcendentals=0),
        compiler_params=pltpu.CompilerParams(vmem_limit_bytes=VMEM),
        name=name,
    )(order, *[x for x, _, _ in windows], *whole, *scalars)


def step_kernel(lead, rows_in, with_b, summed, order_ref, *refs):
    refs = list(refs)
    own_g, sib_g = refs.pop(0), refs.pop(0)
    own_a, sib_a = (refs.pop(0), refs.pop(0)) if rows_in else (None, None)
    a_ref = refs.pop(0)
    b_ref = refs.pop(0) if with_b else None
    tokens = own_g.shape[0]
    for k, (g, a) in enumerate(((own_g, own_a), (sib_g, sib_a))):
        at = pl.ds(k * tokens, tokens)
        out = dot(g[:, :lead], a_ref[rows_in:])
        if with_b:
            out += dot(g[:, lead:], b_ref[...])
        if summed:
            out += refs[0][at]
        if rows_in:
            inn = dot(a[...], a_ref[:rows_in])
            if summed:
                inn += refs[1][at]
            refs[-1][at] = inn
            refs[-2][at] = out
        else:
            refs[-1][at] = out


def step(order, own, sib, blocks, totals, s, lead, rows, rows_in):
    here = lambda i, o: (0, o[s])
    windows = [(own[0], rows, here), (sib[0], rows, here)]
    if rows_in:
        windows += [(own[1], rows_in, here), (sib[1], rows_in, here)]
    tokens, columns = own[0].shape[0], blocks[0].shape[1]
    depth = sum(b.shape[0] for b in blocks)
    shape = jax.ShapeDtypeStruct((2 * tokens, columns), F32)
    return call(
        functools.partial(step_kernel, lead, rows_in, len(blocks) > 1, bool(totals)),
        order, windows, list(blocks) + list(totals), [],
        [shape] * (2 if rows_in else 1), 4 * tokens * depth * columns, "step",
    )


def score_kernel(lead, order_ref, own_g, sib_g, b_ref, out_ref, inn_ref, got_ref,
                 seq_ref, len_ref, seq_sib, len_sib, table_ref):
    tokens = own_g.shape[0]
    columns = b_ref.shape[1]
    queries = columns // RANK
    column = lax.broadcasted_iota(jnp.int32, (columns, queries), 0) // RANK
    query = lax.broadcasted_iota(jnp.int32, (columns, queries), 1)
    fold = (column == query).astype(F32)
    position = lax.broadcasted_iota(jnp.int32, (LEN, columns), 0)
    row = lax.broadcasted_iota(jnp.int32, table_ref.shape, 0)
    table = jnp.zeros(table_ref.shape, F32)
    for k, (g, seq, lens) in enumerate(((own_g, seq_ref, len_ref), (sib_g, seq_sib, len_sib))):
        mine, other = pl.ds(k * tokens, tokens), pl.ds((1 - k) * tokens, tokens)
        out = out_ref[mine] + dot(g[:, lead:], b_ref[...])
        contrib = out * (inn_ref[mine] + got_ref[other])
        for i in range(tokens // LEN):
            kept = jnp.where(position < lens[i], contrib[i * LEN:(i + 1) * LEN], 0.0)
            summed = jnp.sum(kept, axis=0, keepdims=True)
            score = jnp.dot(
                summed, fold, precision=lax.Precision.HIGHEST, preferred_element_type=F32
            ) * (1.0 / math.sqrt(RANK * LEN))
            table = jnp.where(row == seq[i], score, table)
    table_ref[...] = table


def ring_shards(acts, grads, out_factors, in_factors, seq_slot, lengths):
    devices = lax.axis_size("dp")
    chips = devices // 2
    me = lax.axis_index("dp")
    tokens = grads.shape[0]
    rows, columns = out_factors.shape
    rows_in = in_factors.shape[0]
    orders = jnp.asarray(block_orders(chips))
    mine = lax.dynamic_index_in_dim(orders, me, keepdims=False)
    pairs = ring_pairs(chips)
    swap = [(d, d ^ 1) for d in range(devices)]

    own = [grads, acts]
    every = None
    if rows_in % 128:
        every = lax.all_gather(in_factors, "dp", axis=0, tiled=True)
        own, rows_in = own[:1], 0
    lead = (rows - rows_in) // 2
    first = out_factors[:lead]
    if rows_in:
        first = jnp.concatenate([in_factors, first])
    held = [(first, out_factors[lead:])]

    seq_sib, len_sib = lax.ppermute(jnp.stack([seq_slot, lengths]), "dp", swap)
    sib = [lax.ppermute(x, "dp", swap) for x in own]

    totals, summed = [], 0

    def sum_to(k, totals, summed):
        for j in range(summed, k):
            totals = step(mine, own, sib, held[j], totals, j, lead, rows, rows_in)
        return totals, max(k, summed)

    for s in range(chips - 1):
        a, b = held[s]
        if s >= 3:
            totals, summed = sum_to(min(2 * s - 5, s), totals, summed)
            a, *totals = lax.optimization_barrier((a, *totals))
            b, *totals = lax.optimization_barrier((b, *totals))
        held.append((lax.ppermute(a, "dp", pairs), lax.ppermute(b, "dp", pairs)))
    totals, summed = sum_to(chips - 1, totals, summed)
    s = chips - 1
    a, b = held[s]
    totals = step(mine, own, sib, [a], totals, s, lead, rows, rows_in)
    if every is not None:
        inn = dot(acts, every)
        totals = [totals[0], jnp.concatenate([inn, jnp.zeros_like(inn)])]
    got = lax.ppermute(totals[1], "dp", swap)

    slots = lengths.shape[0]
    queries = columns // RANK
    windows = [(x, rows, lambda i, o: (0, o[s])) for x in (grads, sib[0])]
    table = call(
        functools.partial(score_kernel, lead), mine, windows, [b, *totals, got],
        [seq_slot, lengths, seq_sib, len_sib],
        [jax.ShapeDtypeStruct((slots * devices, queries), F32)],
        4 * tokens * rows * columns, "score",
    )[0]
    got = lax.all_to_all(table.reshape(devices, slots, queries), "dp", 0, 0, tiled=True)
    return jnp.sum(got, axis=0)


FORWARD = {1: 2, 2: 5, 5: 6, 6: 1}
MIDDLE = {0: 1, 7: 6, 3: 2, 4: 5}
ACROSS = {0: 7, 7: 0, 3: 4, 4: 3}
LANE = {0: 0, 7: 1, 3: 1, 4: 0}


class Grid:
    def __init__(self):
        ring = ring_of(8)
        at = lambda place, core: 2 * ring[place] + core
        self.inner = [(at(m, 0), at(n, 0)) for m, n in FORWARD.items()]
        self.inner += [(at(n, 1), at(m, 1)) for m, n in FORWARD.items()]
        feed = [(at(m, LANE[q]), at(q, LANE[q])) for q, m in MIDDLE.items()]
        self.feed = feed
        self.other = [(at(m, 1 - LANE[q]), at(q, 1 - LANE[q])) for q, m in MIDDLE.items()]
        self.relay = [(at(q, LANE[q]), at(n, LANE[q])) for q, n in ACROSS.items()]
        cross = [(at(q, 1 - LANE[q]), at(n, 1 - LANE[q])) for q, n in ACROSS.items()]
        self.inward = [(at(q, c), at(m, c)) for q, m in MIDDLE.items() for c in (0, 1)]
        self.first = self.inner + self.relay + cross
        self.second = self.inward + feed
        self.third = self.inner + self.relay

        def sent(ids, pairs):
            got = np.full(16, -1)
            for i, j in pairs:
                got[j] = ids[i]
            return got

        stages = []
        last, early = self.flow(np.arange(16), sent, lambda *arrays: stages.append(arrays))
        stages.append(last)
        table = np.stack([np.max(np.stack(x), axis=0) for x in stages], axis=1)
        late = [src for src, _ in feed]
        skipped = np.zeros(16, int)
        for q, m in self.inward:
            skipped[q] = (last[0] if m in late else early)[m]
        places = [ring.index(d // 2) for d in range(16)]
        own_in = []
        for d in range(16):
            core = d % 2
            turn = -1 if core == 0 else 1
            row = [d]
            for k in (1, 2, 3):
                chip = ring[(places[d] + turn * k) % 8]
                row += [2 * chip + core, 2 * chip + 1 - core]
            own_in.append(row + [2 * ring[(places[d] + 4) % 8] + core])
        flag = np.array([d in late for d in range(16)], int)
        for d in range(16):
            blocks = sorted(x for x in table[d] if x >= 0)
            extra = [skipped[d]] if len(blocks) == 7 else []
            lane = sorted(set(range(16)) - set(blocks) - set(extra))
            assert len(blocks) + len(extra) == 8
            assert [x % 2 for x in lane] == [1 - d % 2] * 8
        table = np.maximum(table, 0)
        self.table = np.concatenate(
            [table, skipped[:, None], flag[:, None], np.array(own_in)], axis=1
        ).astype(np.int32)

    def flow(self, own, send, sums=lambda *arrays: None, tie=lambda x: x):
        m0 = send(own, self.first)
        m1 = send(own, self.second)
        r1 = send(m0, self.inner)
        z1 = send(m0, self.feed)
        m2 = send(m1, self.third)
        r3 = send(r1, self.inner)
        z2 = send(r1, self.feed)
        y2 = send(z1, self.relay)
        sums(own)
        sums(m0)
        r4 = send(tie(m2), self.inner)
        w = send(m2, self.other)
        y3 = send(z2, self.relay)
        z4 = send(r3, self.feed)
        sums(m1)
        sums(m2)
        r5 = send(tie(r4), self.inner)
        z5 = send(r4, self.feed)
        sums(r1, z1, y2)
        y5 = send(tie(z4), self.relay)
        sums(r3, z2, y3)
        sums(r4, z4, w)
        return (r5, z5, y5), r4


SKIPPED, LATE, OWN_IN = 8, 9, 10


def joined(refs):
    block = refs[0][...]
    for ref in refs[1:]:
        block = block + ref[...]
    return block


def stage_kernel(count, summed, order_ref, own_ref, sib_ref, *refs):
    block = joined(refs[:count])
    tokens = own_ref.shape[0]
    for k, ref in enumerate((own_ref, sib_ref)):
        at = pl.ds(k * tokens, tokens)
        new = dot(ref[...], block)
        refs[-1][at] = refs[count][at] + new if summed else new


def stage(order, pair, arrays, total, j):
    rows, columns = arrays[0].shape
    tokens = pair[0].shape[0]
    windows = [(x, rows, lambda i, o: (0, o[j])) for x in pair]
    return call(
        functools.partial(stage_kernel, len(arrays), total is not None),
        order, windows, list(arrays) + ([] if total is None else [total]), [],
        [jax.ShapeDtypeStruct((2 * tokens, columns), F32)],
        4 * tokens * rows * columns, "stage",
    )[0]


def inside_kernel(sizes, summed, order_ref, *refs):
    windows, refs = refs[:2 * sum(sizes)], refs[2 * sum(sizes):]
    blocks, refs = refs[:len(sizes)], refs[len(sizes):]
    tokens = windows[0].shape[0]
    rows = windows[0].shape[1]
    for k in range(2):
        at = pl.ds(k * tokens, tokens)
        new = refs[0][at] if summed else 0.0
        w = 0
        for block, size in zip(blocks, sizes):
            for i in range(size):
                new += dot(windows[2 * w + k][...], block[i * rows:(i + 1) * rows])
                w += 1
        refs[-1][at] = new


def inside(order, pair, rows, arrays, total, first):
    tokens, columns = pair[0].shape[0], arrays[0].shape[1]
    sizes = [x.shape[0] // rows for x in arrays]
    windows = []
    for w in range(sum(sizes)):
        pick = functools.partial(lambda i, o, col: (0, o[col]), col=first + w)
        windows += [(x, rows, pick) for x in pair]
    return call(
        functools.partial(inside_kernel, sizes, total is not None),
        order, windows, list(arrays) + ([] if total is None else [total]), [],
        [jax.ShapeDtypeStruct((2 * tokens, columns), F32)],
        4 * tokens * rows * sum(sizes) * columns, "inside",
    )[0]


def window_kernel(order_ref, own_ref, sib_ref, out_ref):
    tokens = own_ref.shape[0]
    out_ref[:tokens] = own_ref[...]
    out_ref[tokens:] = sib_ref[...]


def finish_kernel(count, order_ref, own_ref, sib_ref, *refs):
    arrays, refs = refs[:count], refs[count:]
    early_ref, total_ref, inn_ref, job_ref, job_inn_ref, slots_ref, job_slots_ref, table_ref = refs
    tokens, columns = own_ref.shape[0], total_ref.shape[1]
    queries = columns // RANK
    column = lax.broadcasted_iota(jnp.int32, (columns, queries), 0) // RANK
    query = lax.broadcasted_iota(jnp.int32, (columns, queries), 1)
    fold = (column == query).astype(F32)
    position = lax.broadcasted_iota(jnp.int32, (LEN, columns), 0)
    row = lax.broadcasted_iota(jnp.int32, table_ref.shape, 0)
    late = jnp.full(early_ref.shape, order_ref[LATE], jnp.int32) == 1
    block = joined(arrays)
    skipped = jnp.where(late, arrays[0][...], early_ref[...])
    sums, slots = [], []
    parts = [
        (total_ref[:tokens] + dot(own_ref[...], block), inn_ref[:tokens], slots_ref, 0),
        (total_ref[tokens:] + dot(sib_ref[...], block), inn_ref[tokens:], slots_ref, 1),
        (dot(job_ref[:tokens], skipped), job_inn_ref[:tokens], job_slots_ref, 0),
        (dot(job_ref[tokens:], skipped), job_inn_ref[tokens:], job_slots_ref, 1),
    ]
    held = tokens // LEN
    for out, inn, ids, k in parts:
        contrib = out * inn
        for i in range(held):
            kept = jnp.where(
                position < ids[1, k * held + i], contrib[i * LEN:(i + 1) * LEN], 0.0
            )
            sums.append(jnp.sum(kept, axis=0, keepdims=True))
            slots.append(ids[0, k * held + i])
    scores = jnp.dot(
        jnp.concatenate(sums), fold, precision=lax.Precision.HIGHEST, preferred_element_type=F32
    ) * (1.0 / math.sqrt(RANK * LEN))
    table = jnp.zeros(table_ref.shape, F32)
    for i, slot in enumerate(slots):
        table += jnp.where(row == slot, scores[i:i + 1], 0.0)
    table_ref[...] = table


def grid_shards(acts, grads, out_factors, in_factors, seq_slot, lengths):
    devices = lax.axis_size("dp")
    grid = Grid()
    tokens = grads.shape[0]
    rows, columns = out_factors.shape
    rows_in = in_factors.shape[0]
    order = lax.dynamic_index_in_dim(jnp.asarray(grid.table), lax.axis_index("dp"), keepdims=False)
    send = lambda x, pairs: lax.ppermute(x, "dp", pairs)
    swap = lambda x: send(x, [(d, d ^ 1) for d in range(devices)])
    around = ring_pairs(devices // 2)

    in_hops = [in_factors]
    hop = jnp.concatenate([send(in_factors, around), send(swap(in_factors), around)])
    for k in range(2):
        in_hops.append(hop)
        hop = send(hop, around)
    in_hops += [hop, send(hop[:rows_in], around)]

    pair = (grads, swap(grads))
    pair_in = (acts, swap(acts))
    slots = jnp.stack([seq_slot, lengths])
    slots = jnp.concatenate([slots, swap(slots)], axis=1)
    job_slots = send(slots, grid.inward)

    totals = [None]

    def sums(*arrays):
        totals.append(stage(order, pair, arrays, totals[-1], len(totals) - 1))

    def tie(x):
        x, totals[-1] = lax.optimization_barrier((x, totals[-1]))
        return x

    last, early = grid.flow(out_factors, send, sums, tie)

    job = call(
        window_kernel, order, [(x, rows, lambda i, o: (0, o[SKIPPED])) for x in pair], [], [],
        [jax.ShapeDtypeStruct((2 * tokens, rows), grads.dtype)], 0, "window",
    )[0]
    job = send(job, grid.inward)

    inn = inside(order, pair_in, rows_in, in_hops[:2], None, OWN_IN)
    inn = inside(order, pair_in, rows_in, in_hops[2:], inn, OWN_IN + 3)
    got = swap(inn)
    inn = inn + jnp.concatenate([got[tokens:], got[:tokens]])
    job_inn = send(inn, grid.inward)

    queries = columns // RANK
    held = lengths.shape[0]
    table = call(
        functools.partial(finish_kernel, len(last)), order,
        [(x, rows, lambda i, o: (0, o[7])) for x in pair],
        list(last) + [early, totals[-1], inn, job, job_inn], [slots, job_slots],
        [jax.ShapeDtypeStruct((held * devices, queries), F32)],
        8 * tokens * rows * columns, "finish",
    )[0]
    got = lax.all_to_all(table.reshape(devices, held, queries), "dp", 0, 0, tiled=True)
    return jnp.sum(got, axis=0)


def shards(acts, grads, out_factors, in_factors, seq_slot, lengths):
    small = lax.axis_size("dp") == 16 and in_factors.shape[0] % 128 == 0
    run = grid_shards if small else ring_shards
    return run(acts, grads, out_factors, in_factors, seq_slot, lengths)


def solution(mesh):
    return jax.shard_map(
        shards,
        mesh=mesh,
        in_specs=(
            P(("groups", "dp"), None),
            P(("groups", "dp"), None),
            P(("groups", "dp"), None),
            P(("groups", "dp"), None),
            P(("groups", "dp")),
            P(("groups", "dp")),
        ),
        out_specs=P(("groups", "dp"), None),
        check_vma=False,
    )
```

```python
import functools
import math

import jax
import jax.numpy as jnp
import numpy as np
from jax import lax
from jax.experimental import pallas as pl
from jax.experimental.pallas import tpu as pltpu
from jax.sharding import PartitionSpec as P

RANK = 32
LEN = 80
F32 = jnp.float32
VMEM = 56 << 20


def ring_of(chips):
    cols = max([d for d in range(1, math.isqrt(chips) + 1) if chips % d == 0 and d % 2 == 0] or [1])
    rows = chips // cols
    if cols == 1 or rows % 2:
        return list(range(chips))
    walk = []
    for r in range(rows):
        line = range(1, cols) if r % 2 == 0 else range(cols - 1, 0, -1)
        walk += [r * cols + c for c in line]
    return walk + [r * cols for r in reversed(range(rows))]


def block_orders(chips):
    ring = ring_of(chips)
    order = np.zeros((2 * chips, chips), np.int32)
    for p, chip in enumerate(ring):
        for s in range(chips):
            order[2 * chip, s] = 2 * ring[(p - s) % chips]
            order[2 * chip + 1, s] = 2 * ring[(p + s) % chips] + 1
    return order


def ring_pairs(chips):
    ring = ring_of(chips)
    pairs = []
    for p, chip in enumerate(ring):
        pairs.append((2 * chip, 2 * ring[(p + 1) % chips]))
        pairs.append((2 * chip + 1, 2 * ring[(p - 1) % chips] + 1))
    return pairs


def dot(a, b):
    return jnp.dot(a, b, preferred_element_type=F32)


def call(kernel, order, windows, whole, scalars, out_shape, flops, name):
    in_specs = [pl.BlockSpec((x.shape[0], w), at) for x, w, at in windows]
    in_specs += [pl.BlockSpec(x.shape, lambda i, o: (0, 0)) for x in whole]
    in_specs += [pl.BlockSpec(memory_space=pltpu.SMEM) for _ in scalars]
    size = sum(2 * x.shape[0] * w for x, w, _ in windows)
    size += sum(x.size * x.dtype.itemsize for x in list(whole) + list(out_shape))
    return pl.pallas_call(
        kernel,
        grid_spec=pltpu.PrefetchScalarGridSpec(
            num_scalar_prefetch=1,
            grid=(1,),
            in_specs=in_specs,
            out_specs=[pl.BlockSpec(x.shape, lambda i, o: (0, 0)) for x in out_shape],
        ),
        out_shape=out_shape,
        cost_estimate=pl.CostEstimate(flops=flops, bytes_accessed=size, transcendentals=0),
        compiler_params=pltpu.CompilerParams(vmem_limit_bytes=VMEM),
        name=name,
    )(order, *[x for x, _, _ in windows], *whole, *scalars)


def step_kernel(lead, rows_in, with_b, summed, order_ref, *refs):
    refs = list(refs)
    own_g, sib_g = refs.pop(0), refs.pop(0)
    own_a, sib_a = (refs.pop(0), refs.pop(0)) if rows_in else (None, None)
    a_ref = refs.pop(0)
    b_ref = refs.pop(0) if with_b else None
    tokens = own_g.shape[0]
    for k, (g, a) in enumerate(((own_g, own_a), (sib_g, sib_a))):
        at = pl.ds(k * tokens, tokens)
        out = dot(g[:, :lead], a_ref[rows_in:])
        if with_b:
            out += dot(g[:, lead:], b_ref[...])
        if summed:
            out += refs[0][at]
        if rows_in:
            inn = dot(a[...], a_ref[:rows_in])
            if summed:
                inn += refs[1][at]
            refs[-1][at] = inn
            refs[-2][at] = out
        else:
            refs[-1][at] = out


def step(order, own, sib, blocks, totals, s, lead, rows, rows_in):
    here = lambda i, o: (0, o[s])
    windows = [(own[0], rows, here), (sib[0], rows, here)]
    if rows_in:
        windows += [(own[1], rows_in, here), (sib[1], rows_in, here)]
    tokens, columns = own[0].shape[0], blocks[0].shape[1]
    depth = sum(b.shape[0] for b in blocks)
    shape = jax.ShapeDtypeStruct((2 * tokens, columns), F32)
    return call(
        functools.partial(step_kernel, lead, rows_in, len(blocks) > 1, bool(totals)),
        order, windows, list(blocks) + list(totals), [],
        [shape] * (2 if rows_in else 1), 4 * tokens * depth * columns, "step",
    )


def score_kernel(lead, order_ref, own_g, sib_g, b_ref, out_ref, inn_ref, got_ref,
                 seq_ref, len_ref, seq_sib, len_sib, table_ref):
    tokens = own_g.shape[0]
    columns = b_ref.shape[1]
    queries = columns // RANK
    column = lax.broadcasted_iota(jnp.int32, (columns, queries), 0) // RANK
    query = lax.broadcasted_iota(jnp.int32, (columns, queries), 1)
    fold = (column == query).astype(F32)
    position = lax.broadcasted_iota(jnp.int32, (LEN, columns), 0)
    row = lax.broadcasted_iota(jnp.int32, table_ref.shape, 0)
    table = jnp.zeros(table_ref.shape, F32)
    for k, (g, seq, lens) in enumerate(((own_g, seq_ref, len_ref), (sib_g, seq_sib, len_sib))):
        mine, other = pl.ds(k * tokens, tokens), pl.ds((1 - k) * tokens, tokens)
        out = out_ref[mine] + dot(g[:, lead:], b_ref[...])
        contrib = out * (inn_ref[mine] + got_ref[other])
        for i in range(tokens // LEN):
            kept = jnp.where(position < lens[i], contrib[i * LEN:(i + 1) * LEN], 0.0)
            summed = jnp.sum(kept, axis=0, keepdims=True)
            score = jnp.dot(
                summed, fold, precision=lax.Precision.HIGHEST, preferred_element_type=F32
            ) * (1.0 / math.sqrt(RANK * LEN))
            table = jnp.where(row == seq[i], score, table)
    table_ref[...] = table


def ring_shards(acts, grads, out_factors, in_factors, seq_slot, lengths):
    devices = lax.axis_size("dp")
    chips = devices // 2
    me = lax.axis_index("dp")
    tokens = grads.shape[0]
    rows, columns = out_factors.shape
    rows_in = in_factors.shape[0]
    orders = jnp.asarray(block_orders(chips))
    mine = lax.dynamic_index_in_dim(orders, me, keepdims=False)
    pairs = ring_pairs(chips)
    swap = [(d, d ^ 1) for d in range(devices)]

    own = [grads, acts]
    every = None
    if rows_in % 128:
        every = lax.all_gather(in_factors, "dp", axis=0, tiled=True)
        own, rows_in = own[:1], 0
    lead = (rows - rows_in) // 2
    first = out_factors[:lead]
    if rows_in:
        first = jnp.concatenate([in_factors, first])
    held = [(first, out_factors[lead:])]

    seq_sib, len_sib = lax.ppermute(jnp.stack([seq_slot, lengths]), "dp", swap)
    sib = [lax.ppermute(x, "dp", swap) for x in own]

    totals, summed = [], 0

    def sum_to(k, totals, summed):
        for j in range(summed, k):
            totals = step(mine, own, sib, held[j], totals, j, lead, rows, rows_in)
        return totals, max(k, summed)

    for s in range(chips - 1):
        a, b = held[s]
        if s >= 3:
            totals, summed = sum_to(min(2 * s - 5, s), totals, summed)
            a, *totals = lax.optimization_barrier((a, *totals))
            b, *totals = lax.optimization_barrier((b, *totals))
        held.append((lax.ppermute(a, "dp", pairs), lax.ppermute(b, "dp", pairs)))
    totals, summed = sum_to(chips - 1, totals, summed)
    s = chips - 1
    a, b = held[s]
    totals = step(mine, own, sib, [a], totals, s, lead, rows, rows_in)
    if every is not None:
        inn = dot(acts, every)
        totals = [totals[0], jnp.concatenate([inn, jnp.zeros_like(inn)])]
    got = lax.ppermute(totals[1], "dp", swap)

    slots = lengths.shape[0]
    queries = columns // RANK
    windows = [(x, rows, lambda i, o: (0, o[s])) for x in (grads, sib[0])]
    table = call(
        functools.partial(score_kernel, lead), mine, windows, [b, *totals, got],
        [seq_slot, lengths, seq_sib, len_sib],
        [jax.ShapeDtypeStruct((slots * devices, queries), F32)],
        4 * tokens * rows * columns, "score",
    )[0]
    got = lax.all_to_all(table.reshape(devices, slots, queries), "dp", 0, 0, tiled=True)
    return jnp.sum(got, axis=0)


FORWARD = {1: 2, 2: 5, 5: 6, 6: 1}
MIDDLE = {0: 1, 7: 6, 3: 2, 4: 5}
ACROSS = {0: 7, 7: 0, 3: 4, 4: 3}
LANE = {0: 0, 7: 1, 3: 1, 4: 0}


class Grid:
    def __init__(self):
        ring = ring_of(8)
        at = lambda place, core: 2 * ring[place] + core
        self.inner = [(at(m, 0), at(n, 0)) for m, n in FORWARD.items()]
        self.inner += [(at(n, 1), at(m, 1)) for m, n in FORWARD.items()]
        feed = [(at(m, LANE[q]), at(q, LANE[q])) for q, m in MIDDLE.items()]
        self.feed = feed
        self.other = [(at(m, 1 - LANE[q]), at(q, 1 - LANE[q])) for q, m in MIDDLE.items()]
        self.relay = [(at(q, LANE[q]), at(n, LANE[q])) for q, n in ACROSS.items()]
        self.cross = [(at(q, 1 - LANE[q]), at(n, 1 - LANE[q])) for q, n in ACROSS.items()]
        self.inward = [(at(q, c), at(m, c)) for q, m in MIDDLE.items() for c in (0, 1)]
        self.first = self.inner + self.relay

        def sent(ids, pairs):
            got = np.full(16, -1)
            for i, j in pairs:
                got[j] = ids[i]
            return got

        stages = []
        last, early = self.flow(np.arange(16), sent, lambda *arrays: stages.append(arrays))
        stages.append(last)
        table = np.stack([np.max(np.stack(x), axis=0) for x in stages], axis=1)
        late = [src for src, _ in feed]
        skipped = np.zeros(16, int)
        for q, m in self.inward:
            skipped[q] = (last[0] if m in late else early)[m]
        own_in = [[(e - 4 * k) % 16 for e in (d, d ^ 2) for k in range(4)] for d in range(16)]
        flag = np.array([d in late for d in range(16)], int)
        for d in range(16):
            blocks = sorted(x for x in table[d] if x >= 0)
            extra = [skipped[d]] if len(blocks) == 7 else []
            lane = sorted(set(range(16)) - set(blocks) - set(extra))
            assert len(blocks) + len(extra) == 8
            assert [x % 2 for x in lane] == [1 - d % 2] * 8
        table = np.maximum(table, 0)
        self.table = np.concatenate(
            [table, skipped[:, None], flag[:, None], np.array(own_in)], axis=1
        ).astype(np.int32)

    def flow(self, own, send, sums=lambda *arrays: None, tie=lambda level, *x: x):
        m0 = send(own, self.first)
        z0 = send(own, self.feed)
        c = send(own, self.inward)
        (m0,) = tie(1, m0)
        r1 = send(m0, self.inner)
        z1 = send(m0, self.feed)
        y1 = send(z0, self.relay)
        r2 = send(c, self.inner)
        z2 = send(r1, self.feed)
        y2 = send(z1, self.relay)
        sums(own)
        sums(m0, z0)
        r1, r2, z2 = tie(3, r1, r2, z2)
        r3 = send(r1, self.inner)
        w = send(r2, self.other)
        y3 = send(z2, self.relay)
        sums(c, y1, z1)
        sums(r1, y2, z2)
        r2, r3, own = tie(4, r2, r3, own)
        r4 = send(r2, self.inner)
        z4 = send(r3, self.feed)
        u = send(own, self.cross)
        sums(r2, w)
        r4, z4 = tie(5, r4, z4)
        r5 = send(r4, self.inner)
        z5 = send(r4, self.feed)
        y5 = send(z4, self.relay)
        sums(r3, y3, z4)
        sums(r4, u)
        return (r5, z5, y5), r4


SKIPPED, LATE, OWN_IN = 8, 9, 10


def joined(refs):
    block = refs[0][...]
    for ref in refs[1:]:
        block = block + ref[...]
    return block


def stage_kernel(count, summed, order_ref, own_ref, sib_ref, *refs):
    block = joined(refs[:count])
    tokens = own_ref.shape[0]
    for k, ref in enumerate((own_ref, sib_ref)):
        at = pl.ds(k * tokens, tokens)
        new = dot(ref[...], block)
        refs[-1][at] = refs[count][at] + new if summed else new


def stage(order, pair, arrays, total, j):
    rows, columns = arrays[0].shape
    tokens = pair[0].shape[0]
    windows = [(x, rows, lambda i, o: (0, o[j])) for x in pair]
    return call(
        functools.partial(stage_kernel, len(arrays), total is not None),
        order, windows, list(arrays) + ([] if total is None else [total]), [],
        [jax.ShapeDtypeStruct((2 * tokens, columns), F32)],
        4 * tokens * rows * columns, "stage",
    )[0]


EXTRA = 8


def inside_kernel(sizes, summed, order_ref, *refs):
    windows, refs = refs[:2 * sum(sizes)], refs[2 * sum(sizes):]
    blocks, refs = refs[:len(sizes)], refs[len(sizes):]
    tokens, rows = windows[0].shape
    for k in range(2):
        at = pl.ds(k * tokens, tokens)
        new = refs[0][at] if summed else 0.0
        w = 0
        for block, size in zip(blocks, sizes):
            for i in range(size):
                new += dot(windows[2 * w + k][...], block[i * rows:(i + 1) * rows])
                w += 1
        refs[-1][at] = new
    if summed:
        seq_ref, len_ref = refs[1:3]
        held = seq_ref.shape[0]
        lane = lax.broadcasted_iota(jnp.int32, (EXTRA, refs[-1].shape[1]), 1)
        numbers = jnp.zeros(lane.shape, F32)
        for i in range(held):
            numbers = jnp.where(lane == i, seq_ref[i].astype(F32), numbers)
            numbers = jnp.where(lane == held + i, len_ref[i].astype(F32), numbers)
        refs[-1][2 * tokens:] = numbers


def inside(order, pair, rows, arrays, total, first, slots):
    tokens, columns = pair[0].shape[0], arrays[0].shape[1]
    sizes = [x.shape[0] // rows for x in arrays]
    windows = []
    for w in range(sum(sizes)):
        pick = functools.partial(lambda i, o, col: (0, o[col]), col=first + w)
        windows += [(x, rows, pick) for x in pair]
    height = 2 * tokens + (0 if total is None else EXTRA)
    return call(
        functools.partial(inside_kernel, sizes, total is not None),
        order, windows, list(arrays) + ([] if total is None else [total]), slots,
        [jax.ShapeDtypeStruct((height, columns), F32)],
        4 * tokens * rows * sum(sizes) * columns, "inside",
    )[0]


def masked_kernel(order_ref, own_ref, got_ref, out_ref):
    tokens = (own_ref.shape[0] - EXTRA) // 2
    columns = own_ref.shape[1]
    held = tokens // LEN
    position = lax.broadcasted_iota(jnp.int32, (LEN, columns), 0).astype(F32)
    for k, (mine, other) in enumerate(((own_ref, got_ref), (got_ref, own_ref))):
        for i in range(held):
            at, across = pl.ds(i * LEN, LEN), pl.ds(tokens + i * LEN, LEN)
            length = mine[2 * tokens:2 * tokens + 1, held + i:held + i + 1]
            out_ref[pl.ds(k * tokens + i * LEN, LEN)] = jnp.where(
                position < length, mine[at] + other[across], 0.0
            )
    lane = lax.broadcasted_iota(jnp.int32, (EXTRA, columns), 1)
    numbers = jnp.zeros(lane.shape, F32)
    for k, ref in enumerate((own_ref, got_ref)):
        for i in range(held):
            slot = ref[2 * tokens:2 * tokens + 1, i:i + 1]
            numbers = jnp.where(lane == k * held + i, slot, numbers)
    out_ref[2 * tokens:] = numbers


def window_kernel(order_ref, own_ref, sib_ref, out_ref):
    tokens = own_ref.shape[0]
    out_ref[:tokens] = own_ref[...]
    out_ref[tokens:] = sib_ref[...]


def finish_kernel(count, order_ref, own_ref, sib_ref, *refs):
    arrays, refs = refs[:count], refs[count:]
    early_ref, total_ref, inn_ref, job_ref, job_inn_ref, table_ref = refs
    tokens, columns = own_ref.shape[0], total_ref.shape[1]
    queries = columns // RANK
    held = tokens // LEN
    column = lax.broadcasted_iota(jnp.int32, (columns, queries), 0) // RANK
    query = lax.broadcasted_iota(jnp.int32, (columns, queries), 1)
    fold = (column == query).astype(F32)
    row = lax.broadcasted_iota(jnp.int32, table_ref.shape, 0).astype(F32)
    late = jnp.full(early_ref.shape, order_ref[LATE], jnp.int32) == 1
    block = joined(arrays)
    skipped = jnp.where(late, arrays[0][...], early_ref[...])
    sums, slots = [], []
    parts = [
        (total_ref[:tokens] + dot(own_ref[...], block), inn_ref, 0),
        (total_ref[tokens:] + dot(sib_ref[...], block), inn_ref, 1),
        (dot(job_ref[:tokens], skipped), job_inn_ref, 0),
        (dot(job_ref[tokens:], skipped), job_inn_ref, 1),
    ]
    for out, inn, k in parts:
        contrib = out * inn[k * tokens:(k + 1) * tokens]
        for i in range(held):
            sums.append(jnp.sum(contrib[i * LEN:(i + 1) * LEN], axis=0, keepdims=True))
            at = k * held + i
            slots.append(inn[2 * tokens:2 * tokens + 1, at:at + 1])
    scores = jnp.dot(
        jnp.concatenate(sums), fold, precision=lax.Precision.HIGHEST, preferred_element_type=F32
    ) * (1.0 / math.sqrt(RANK * LEN))
    table = jnp.zeros(table_ref.shape, F32)
    for i, slot in enumerate(slots):
        table += jnp.where(row == slot, scores[i:i + 1], 0.0)
    table_ref[...] = table


def grid_shards(acts, grads, out_factors, in_factors, seq_slot, lengths):
    devices = lax.axis_size("dp")
    grid = Grid()
    tokens = grads.shape[0]
    rows, columns = out_factors.shape
    rows_in = in_factors.shape[0]
    order = lax.dynamic_index_in_dim(jnp.asarray(grid.table), lax.axis_index("dp"), keepdims=False)
    send = lambda x, pairs: lax.ppermute(x, "dp", pairs)
    swap = lambda x: send(x, [(d, d ^ 1) for d in range(devices)])

    across = [(d, d ^ 2) for d in range(devices)]
    column, beside = [in_factors], [send(in_factors, across)]
    for k in range(1, 4):
        column.append(send(in_factors, [(d, (d + 4 * k) % devices) for d in range(devices)]))
        beside.append(send(column[k], across))
    pair_in = (acts, swap(acts))
    pair = (grads, swap(grads))
    job = call(
        window_kernel, order, [(x, rows, lambda i, o: (0, o[SKIPPED])) for x in pair], [], [],
        [jax.ShapeDtypeStruct((2 * tokens, rows), grads.dtype)], 0, "window",
    )[0]
    inn = inside(order, pair_in, rows_in, column, None, OWN_IN, [])
    half_inn = inn
    inn = inside(order, pair_in, rows_in, beside, inn, OWN_IN + 4, [seq_slot, lengths])
    inn = call(
        masked_kernel, order, [], [inn, swap(inn)], [],
        [jax.ShapeDtypeStruct(inn.shape, F32)], 0, "masked",
    )[0]

    totals = [None]
    aside = {1: column[1:], 3: beside + [job], 4: [half_inn], 5: [inn]}

    def sums(*arrays):
        totals.append(stage(order, pair, arrays, totals[-1], len(totals) - 1))

    def tie(level, *x):
        keep = [t for t in totals[-1:] if t is not None]
        out = lax.optimization_barrier((*x, *keep, *aside.get(level, [])))
        if keep:
            totals[-1] = out[len(x)]
        return out[:len(x)]

    last, early = grid.flow(out_factors, send, sums, tie)
    job = send(job, grid.inward)
    job_inn = send(inn, grid.inward)

    queries = columns // RANK
    held = lengths.shape[0]
    table = call(
        functools.partial(finish_kernel, len(last)), order,
        [(x, rows, lambda i, o: (0, o[7])) for x in pair],
        list(last) + [early, totals[-1], inn, job, job_inn], [],
        [jax.ShapeDtypeStruct((held * devices, queries), F32)],
        8 * tokens * rows * columns, "finish",
    )[0]
    got = lax.all_to_all(table.reshape(devices, held, queries), "dp", 0, 0, tiled=True)
    return jnp.sum(got, axis=0)


def shards(acts, grads, out_factors, in_factors, seq_slot, lengths):
    small = lax.axis_size("dp") == 16 and in_factors.shape[0] % 128 == 0
    run = grid_shards if small else ring_shards
    return run(acts, grads, out_factors, in_factors, seq_slot, lengths)


def solution(mesh):
    return jax.shard_map(
        shards,
        mesh=mesh,
        in_specs=(
            P(("groups", "dp"), None),
            P(("groups", "dp"), None),
            P(("groups", "dp"), None),
            P(("groups", "dp"), None),
            P(("groups", "dp")),
            P(("groups", "dp")),
        ),
        out_specs=P(("groups", "dp"), None),
        check_vma=False,
    )
```

```python
import functools
import math

import jax
import jax.numpy as jnp
import numpy as np
from jax import lax
from jax.experimental import pallas as pl
from jax.experimental.pallas import tpu as pltpu
from jax.sharding import PartitionSpec as P

RANK = 32
LEN = 80
F32 = jnp.float32
VMEM = 20 << 20


def ring_of(chips):
    cols = max([d for d in range(1, math.isqrt(chips) + 1) if chips % d == 0 and d % 2 == 0] or [1])
    rows = chips // cols
    if cols == 1 or rows % 2:
        return list(range(chips))
    walk = []
    for r in range(rows):
        line = range(1, cols) if r % 2 == 0 else range(cols - 1, 0, -1)
        walk += [r * cols + c for c in line]
    return walk + [r * cols for r in reversed(range(rows))]


def block_orders(chips):
    ring = ring_of(chips)
    order = np.zeros((2 * chips, chips), np.int32)
    for p, chip in enumerate(ring):
        for s in range(chips):
            order[2 * chip, s] = 2 * ring[(p - s) % chips]
            order[2 * chip + 1, s] = 2 * ring[(p + s) % chips] + 1
    return order


def ring_pairs(chips):
    ring = ring_of(chips)
    pairs = []
    for p, chip in enumerate(ring):
        pairs.append((2 * chip, 2 * ring[(p + 1) % chips]))
        pairs.append((2 * chip + 1, 2 * ring[(p - 1) % chips] + 1))
    return pairs


def dot(a, b):
    return jnp.dot(a, b, preferred_element_type=F32)


def call(kernel, order, windows, whole, scalars, out_shape, flops, name):
    in_specs = [pl.BlockSpec((x.shape[0], w), at) for x, w, at in windows]
    in_specs += [pl.BlockSpec(x.shape, lambda i, o: (0, 0)) for x in whole]
    in_specs += [pl.BlockSpec(memory_space=pltpu.SMEM) for _ in scalars]
    size = sum(2 * x.shape[0] * w for x, w, _ in windows)
    size += sum(x.size * x.dtype.itemsize for x in list(whole) + list(out_shape))
    return pl.pallas_call(
        kernel,
        grid_spec=pltpu.PrefetchScalarGridSpec(
            num_scalar_prefetch=1,
            grid=(1,),
            in_specs=in_specs,
            out_specs=[pl.BlockSpec(x.shape, lambda i, o: (0, 0)) for x in out_shape],
        ),
        out_shape=out_shape,
        cost_estimate=pl.CostEstimate(flops=flops, bytes_accessed=size, transcendentals=0),
        compiler_params=pltpu.CompilerParams(vmem_limit_bytes=VMEM),
        name=name,
    )(order, *[x for x, _, _ in windows], *whole, *scalars)


def step_kernel(lead, rows_in, with_b, summed, order_ref, *refs):
    refs = list(refs)
    own_g, sib_g = refs.pop(0), refs.pop(0)
    own_a, sib_a = (refs.pop(0), refs.pop(0)) if rows_in else (None, None)
    a_ref = refs.pop(0)
    b_ref = refs.pop(0) if with_b else None
    tokens = own_g.shape[0]
    for k, (g, a) in enumerate(((own_g, own_a), (sib_g, sib_a))):
        at = pl.ds(k * tokens, tokens)
        out = dot(g[:, :lead], a_ref[rows_in:])
        if with_b:
            out += dot(g[:, lead:], b_ref[...])
        if summed:
            out += refs[0][at]
        if rows_in:
            inn = dot(a[...], a_ref[:rows_in])
            if summed:
                inn += refs[1][at]
            refs[-1][at] = inn
            refs[-2][at] = out
        else:
            refs[-1][at] = out


def step(order, own, sib, blocks, totals, s, lead, rows, rows_in):
    here = lambda i, o: (0, o[s])
    windows = [(own[0], rows, here), (sib[0], rows, here)]
    if rows_in:
        windows += [(own[1], rows_in, here), (sib[1], rows_in, here)]
    tokens, columns = own[0].shape[0], blocks[0].shape[1]
    depth = sum(b.shape[0] for b in blocks)
    shape = jax.ShapeDtypeStruct((2 * tokens, columns), F32)
    return call(
        functools.partial(step_kernel, lead, rows_in, len(blocks) > 1, bool(totals)),
        order, windows, list(blocks) + list(totals), [],
        [shape] * (2 if rows_in else 1), 4 * tokens * depth * columns, "step",
    )


def join_kernel(lead, in_ref, out_ref, joined_ref, sems):
    rows_in = in_ref.shape[0]
    copies = [
        pltpu.make_async_copy(in_ref, joined_ref.at[pl.ds(0, rows_in)], sems.at[0]),
        pltpu.make_async_copy(
            out_ref.at[pl.ds(0, lead)], joined_ref.at[pl.ds(rows_in, lead)], sems.at[1]
        ),
    ]
    for copy in copies:
        copy.start()
    for copy in copies:
        copy.wait()


def join(in_factors, out_factors, lead):
    rows_in, columns = in_factors.shape
    anywhere = pl.BlockSpec(memory_space=pl.ANY)
    return pl.pallas_call(
        functools.partial(join_kernel, lead),
        in_specs=[anywhere] * 2,
        out_specs=anywhere,
        out_shape=jax.ShapeDtypeStruct((rows_in + lead, columns), in_factors.dtype),
        scratch_shapes=[pltpu.SemaphoreType.DMA((2,))],
        cost_estimate=pl.CostEstimate(
            flops=0, bytes_accessed=4 * (rows_in + lead) * columns, transcendentals=0
        ),
        name="join",
    )(in_factors, out_factors)


def window_kernel(lead, order_ref, own_ref, sib_ref, out_ref):
    tokens = own_ref.shape[0]
    out_ref[:tokens] = own_ref[:, lead:]
    out_ref[tokens:] = sib_ref[:, lead:]


def score_kernel(seq_ref, len_ref, seq_sib, len_sib, window_ref, b_ref, out_ref, inn_ref, got_ref,
                 table_ref):
    columns = b_ref.shape[1]
    tokens = window_ref.shape[0] // 2
    queries = columns // RANK
    column = lax.broadcasted_iota(jnp.int32, (columns, queries), 0) // RANK
    query = lax.broadcasted_iota(jnp.int32, (columns, queries), 1)
    fold = (column == query).astype(F32)
    position = lax.broadcasted_iota(jnp.int32, (LEN, columns), 0)
    row = lax.broadcasted_iota(jnp.int32, table_ref.shape, 0)
    out = out_ref[...] + dot(window_ref[...], b_ref[...])
    sums, slots = [], []
    for k, (seq, lens) in enumerate(((seq_ref, len_ref), (seq_sib, len_sib))):
        mine, other = pl.ds(k * tokens, tokens), pl.ds((1 - k) * tokens, tokens)
        contrib = out[k * tokens:(k + 1) * tokens] * (inn_ref[mine] + got_ref[other])
        for i in range(tokens // LEN):
            kept = jnp.where(position < lens[i], contrib[i * LEN:(i + 1) * LEN], 0.0)
            sums.append(jnp.sum(kept, axis=0, keepdims=True))
            slots.append(seq[i])
    scores = jnp.dot(
        jnp.concatenate(sums), fold, precision=lax.Precision.HIGHEST, preferred_element_type=F32
    ) * (1.0 / math.sqrt(RANK * LEN))
    table = jnp.zeros(table_ref.shape, F32)
    for i, slot in enumerate(slots):
        table = jnp.where(row == slot, scores[i:i + 1], table)
    table_ref[...] = table


def score_table(numbers, arrays, rows, queries):
    smem, vmem = (pl.BlockSpec(memory_space=m) for m in (pltpu.SMEM, pltpu.VMEM))
    window, block = arrays[:2]
    size = sum(x.size * x.dtype.itemsize for x in arrays)
    return pl.pallas_call(
        score_kernel,
        in_specs=[smem] * len(numbers) + [vmem] * len(arrays),
        out_specs=vmem,
        out_shape=jax.ShapeDtypeStruct((rows, queries), F32),
        cost_estimate=pl.CostEstimate(
            flops=2 * window.size * block.shape[1], bytes_accessed=size, transcendentals=0
        ),
        compiler_params=pltpu.CompilerParams(vmem_limit_bytes=VMEM),
        name="score",
    )(*numbers, *arrays)


def shards(acts, grads, out_factors, in_factors, seq_slot, lengths):
    devices = lax.axis_size("dp")
    chips = devices // 2
    me = lax.axis_index("dp")
    tokens = grads.shape[0]
    rows, columns = out_factors.shape
    rows_in = in_factors.shape[0]
    orders = jnp.asarray(block_orders(chips))
    mine = lax.dynamic_index_in_dim(orders, me, keepdims=False)
    pairs = ring_pairs(chips)
    swap = [(d, d ^ 1) for d in range(devices)]

    own = [grads, acts]
    every = None
    if rows_in % 128:
        every = lax.all_gather(in_factors, "dp", axis=0, tiled=True)
        own, rows_in = own[:1], 0
    lead = (rows - rows_in) // 2
    first = join(in_factors, out_factors, lead) if rows_in else out_factors[:lead]
    held = [(first, out_factors[lead:])]

    seq_sib, len_sib = lax.ppermute(jnp.stack([seq_slot, lengths]), "dp", swap)
    sib = [lax.ppermute(x, "dp", swap) for x in own]
    totals, summed = [], 0

    def sum_to(k, totals, summed):
        for j in range(summed, k):
            totals = step(mine, own, sib, held[j], totals, j, lead, rows, rows_in)
        return totals, max(k, summed)

    for s in range(chips - 1):
        a, b = held[s]
        if s >= 3:
            totals, summed = sum_to(min(2 * s - 5, s), totals, summed)
            a, *totals = lax.optimization_barrier((a, *totals))
            b, *totals = lax.optimization_barrier((b, *totals))
        held.append((lax.ppermute(a, "dp", pairs), lax.ppermute(b, "dp", pairs)))
    s = chips - 1
    window = call(
        functools.partial(window_kernel, lead), mine,
        [(x, rows, lambda i, o: (0, o[s])) for x in (own[0], sib[0])], [], [],
        [jax.ShapeDtypeStruct((2 * tokens, rows - lead), grads.dtype)], 0, "window",
    )[0]
    totals[0], window = lax.optimization_barrier((totals[0], window))
    totals, summed = sum_to(s, totals, summed)
    a, b = held[s]
    totals = step(mine, own, sib, [a], totals, s, lead, rows, rows_in)
    if every is not None:
        inn = dot(acts, every)
        totals = [totals[0], jnp.concatenate([inn, jnp.zeros_like(inn)])]
    got = lax.ppermute(totals[1], "dp", swap)

    slots = lengths.shape[0]
    queries = columns // RANK
    table = score_table(
        [seq_slot, lengths, seq_sib, len_sib], [window, b, *totals, got], slots * devices, queries
    )
    got = lax.all_to_all(table.reshape(devices, slots, queries), "dp", 0, 0, tiled=True)
    return jnp.sum(got, axis=0)


def solution(mesh):
    return jax.shard_map(
        shards,
        mesh=mesh,
        in_specs=(
            P(("groups", "dp"), None),
            P(("groups", "dp"), None),
            P(("groups", "dp"), None),
            P(("groups", "dp"), None),
            P(("groups", "dp")),
            P(("groups", "dp")),
        ),
        out_specs=P(("groups", "dp"), None),
        check_vma=False,
    )
```

```python
import functools
import math

import jax
import jax.numpy as jnp
import numpy as np
from jax import lax
from jax.experimental import pallas as pl
from jax.experimental.pallas import tpu as pltpu
from jax.sharding import PartitionSpec as P

RANK = 32
LEN = 80
F32 = jnp.float32
VMEM = 20 << 20


def ring_of(chips):
    cols = max([d for d in range(1, math.isqrt(chips) + 1) if chips % d == 0 and d % 2 == 0] or [1])
    rows = chips // cols
    if cols == 1 or rows % 2:
        return list(range(chips))
    walk = []
    for r in range(rows):
        line = range(1, cols) if r % 2 == 0 else range(cols - 1, 0, -1)
        walk += [r * cols + c for c in line]
    return walk + [r * cols for r in reversed(range(rows))]


def block_orders(chips):
    ring = ring_of(chips)
    order = np.zeros((2 * chips, chips), np.int32)
    for p, chip in enumerate(ring):
        for s in range(chips):
            order[2 * chip, s] = 2 * ring[(p - s) % chips]
            order[2 * chip + 1, s] = 2 * ring[(p + s) % chips] + 1
    return order


def ring_pairs(chips):
    ring = ring_of(chips)
    pairs = []
    for p, chip in enumerate(ring):
        pairs.append((2 * chip, 2 * ring[(p + 1) % chips]))
        pairs.append((2 * chip + 1, 2 * ring[(p - 1) % chips] + 1))
    return pairs


def dot(a, b):
    return jnp.dot(a, b, preferred_element_type=F32)


def call(kernel, order, windows, whole, scalars, out_shape, flops, name):
    in_specs = [pl.BlockSpec((x.shape[0], w), at) for x, w, at in windows]
    in_specs += [pl.BlockSpec(x.shape, lambda i, o: (0, 0)) for x in whole]
    in_specs += [pl.BlockSpec(memory_space=pltpu.SMEM) for _ in scalars]
    size = sum(2 * x.shape[0] * w for x, w, _ in windows)
    size += sum(x.size * x.dtype.itemsize for x in list(whole) + list(out_shape))
    return pl.pallas_call(
        kernel,
        grid_spec=pltpu.PrefetchScalarGridSpec(
            num_scalar_prefetch=1,
            grid=(1,),
            in_specs=in_specs,
            out_specs=[pl.BlockSpec(x.shape, lambda i, o: (0, 0)) for x in out_shape],
        ),
        out_shape=out_shape,
        cost_estimate=pl.CostEstimate(flops=flops, bytes_accessed=size, transcendentals=0),
        compiler_params=pltpu.CompilerParams(vmem_limit_bytes=VMEM),
        name=name,
    )(order, *[x for x, _, _ in windows], *whole, *scalars)


def step_kernel(lead, rows_in, with_b, summed, order_ref, *refs):
    refs = list(refs)
    own_g, sib_g = refs.pop(0), refs.pop(0)
    own_a, sib_a = (refs.pop(0), refs.pop(0)) if rows_in else (None, None)
    a_ref = refs.pop(0)
    b_ref = refs.pop(0) if with_b else None
    tokens = own_g.shape[0]
    for k, (g, a) in enumerate(((own_g, own_a), (sib_g, sib_a))):
        at = pl.ds(k * tokens, tokens)
        out = dot(g[:, :lead], a_ref[rows_in:])
        if with_b:
            out += dot(g[:, lead:], b_ref[...])
        if summed:
            out += refs[0][at]
        if rows_in:
            inn = dot(a[...], a_ref[:rows_in])
            if summed:
                inn += refs[1][at]
            refs[-1][at] = inn
            refs[-2][at] = out
        else:
            refs[-1][at] = out


def step(order, own, sib, blocks, totals, s, lead, rows, rows_in):
    here = lambda i, o: (0, o[s])
    windows = [(own[0], rows, here), (sib[0], rows, here)]
    if rows_in:
        windows += [(own[1], rows_in, here), (sib[1], rows_in, here)]
    tokens, columns = own[0].shape[0], blocks[0].shape[1]
    depth = sum(b.shape[0] for b in blocks)
    shape = jax.ShapeDtypeStruct((2 * tokens, columns), F32)
    return call(
        functools.partial(step_kernel, lead, rows_in, len(blocks) > 1, bool(totals)),
        order, windows, list(blocks) + list(totals), [],
        [shape] * (2 if rows_in else 1), 4 * tokens * depth * columns, "step",
    )


def join_kernel(in_ref, out_ref, a_ref, b_ref, sems):
    rows_in = in_ref.shape[0]
    lead, rest = a_ref.shape[0] - rows_in, b_ref.shape[0]
    copies = [
        pltpu.make_async_copy(in_ref, a_ref.at[pl.ds(0, rows_in)], sems.at[0]),
        pltpu.make_async_copy(out_ref.at[pl.ds(0, lead)], a_ref.at[pl.ds(rows_in, lead)], sems.at[1]),
        pltpu.make_async_copy(out_ref.at[pl.ds(lead, rest)], b_ref, sems.at[2]),
    ]
    for copy in copies:
        copy.start()
    for copy in copies:
        copy.wait()


def join(in_factors, out_factors, lead):
    rows_in, columns = in_factors.shape
    heights = [rows_in + lead, out_factors.shape[0] - lead]
    return pl.pallas_call(
        join_kernel,
        in_specs=[pl.BlockSpec(memory_space=pltpu.HBM)] * 2,
        out_specs=[pl.BlockSpec(memory_space=pltpu.VMEM)] * 2,
        out_shape=[jax.ShapeDtypeStruct((h, columns), in_factors.dtype) for h in heights],
        scratch_shapes=[pltpu.SemaphoreType.DMA((3,))],
        cost_estimate=pl.CostEstimate(
            flops=0, bytes_accessed=4 * sum(heights) * columns, transcendentals=0
        ),
        compiler_params=pltpu.CompilerParams(vmem_limit_bytes=4 << 20),
        name="join",
    )(in_factors, out_factors)


def window_kernel(lead, order_ref, own_ref, sib_ref, out_ref):
    tokens = own_ref.shape[0]
    out_ref[:tokens] = own_ref[:, lead:]
    out_ref[tokens:] = sib_ref[:, lead:]


def score_kernel(seq_ref, len_ref, seq_sib, len_sib, window_ref, b_ref, out_ref, inn_ref, got_ref,
                 table_ref):
    columns = b_ref.shape[1]
    tokens = window_ref.shape[0] // 2
    queries = columns // RANK
    column = lax.broadcasted_iota(jnp.int32, (columns, queries), 0) // RANK
    query = lax.broadcasted_iota(jnp.int32, (columns, queries), 1)
    fold = (column == query).astype(F32)
    position = lax.broadcasted_iota(jnp.int32, (LEN, columns), 0)
    row = lax.broadcasted_iota(jnp.int32, table_ref.shape, 0)
    out = out_ref[...] + dot(window_ref[...], b_ref[...])
    sums, slots = [], []
    for k, (seq, lens) in enumerate(((seq_ref, len_ref), (seq_sib, len_sib))):
        mine, other = pl.ds(k * tokens, tokens), pl.ds((1 - k) * tokens, tokens)
        contrib = out[k * tokens:(k + 1) * tokens] * (inn_ref[mine] + got_ref[other])
        for i in range(tokens // LEN):
            kept = jnp.where(position < lens[i], contrib[i * LEN:(i + 1) * LEN], 0.0)
            sums.append(jnp.sum(kept, axis=0, keepdims=True))
            slots.append(seq[i])
    scores = jnp.dot(
        jnp.concatenate(sums), fold, precision=lax.Precision.HIGHEST, preferred_element_type=F32
    ) * (1.0 / math.sqrt(RANK * LEN))
    table = jnp.zeros(table_ref.shape, F32)
    for i, slot in enumerate(slots):
        table = jnp.where(row == slot, scores[i:i + 1], table)
    table_ref[...] = table


def score_table(numbers, arrays, rows, queries):
    smem, vmem = (pl.BlockSpec(memory_space=m) for m in (pltpu.SMEM, pltpu.VMEM))
    window, block = arrays[:2]
    size = sum(x.size * x.dtype.itemsize for x in arrays)
    return pl.pallas_call(
        score_kernel,
        in_specs=[smem] * len(numbers) + [vmem] * len(arrays),
        out_specs=vmem,
        out_shape=jax.ShapeDtypeStruct((rows, queries), F32),
        cost_estimate=pl.CostEstimate(
            flops=2 * window.size * block.shape[1], bytes_accessed=size, transcendentals=0
        ),
        compiler_params=pltpu.CompilerParams(vmem_limit_bytes=VMEM),
        name="score",
    )(*numbers, *arrays)


def shards(acts, grads, out_factors, in_factors, seq_slot, lengths):
    devices = lax.axis_size("dp")
    chips = devices // 2
    me = lax.axis_index("dp")
    tokens = grads.shape[0]
    rows, columns = out_factors.shape
    rows_in = in_factors.shape[0]
    orders = jnp.asarray(block_orders(chips))
    mine = lax.dynamic_index_in_dim(orders, me, keepdims=False)
    pairs = ring_pairs(chips)
    swap = [(d, d ^ 1) for d in range(devices)]

    own = [grads, acts]
    every = None
    if rows_in % 128:
        every = lax.all_gather(in_factors, "dp", axis=0, tiled=True)
        own, rows_in = own[:1], 0
    lead = (rows - rows_in) // 2
    if rows_in:
        held = [join(in_factors, out_factors, lead)]
    else:
        held = [(out_factors[:lead], out_factors[lead:])]

    seq_sib, len_sib = lax.ppermute(jnp.stack([seq_slot, lengths]), "dp", swap)
    sib = [lax.ppermute(x, "dp", swap) for x in own]
    totals, summed = [], 0

    def sum_to(k, totals, summed):
        for j in range(summed, k):
            totals = step(mine, own, sib, held[j], totals, j, lead, rows, rows_in)
        return totals, max(k, summed)

    for s in range(chips - 1):
        a, b = held[s]
        if s >= 3:
            totals, summed = sum_to(min(2 * s - 5, s), totals, summed)
            a, *totals = lax.optimization_barrier((a, *totals))
            b, *totals = lax.optimization_barrier((b, *totals))
        held.append((lax.ppermute(a, "dp", pairs), lax.ppermute(b, "dp", pairs)))
    s = chips - 1
    window = call(
        functools.partial(window_kernel, lead), mine,
        [(x, rows, lambda i, o: (0, o[s])) for x in (own[0], sib[0])], [], [],
        [jax.ShapeDtypeStruct((2 * tokens, rows - lead), grads.dtype)], 0, "window",
    )[0]
    totals[0], window = lax.optimization_barrier((totals[0], window))
    totals, summed = sum_to(s, totals, summed)
    a, b = held[s]
    totals = step(mine, own, sib, [a], totals, s, lead, rows, rows_in)
    if every is not None:
        inn = dot(acts, every)
        totals = [totals[0], jnp.concatenate([inn, jnp.zeros_like(inn)])]
    got = lax.ppermute(totals[1], "dp", swap)

    slots = lengths.shape[0]
    queries = columns // RANK
    table = score_table(
        [seq_slot, lengths, seq_sib, len_sib], [window, b, *totals, got], slots * devices, queries
    )
    got = lax.all_to_all(table.reshape(devices, slots, queries), "dp", 0, 0, tiled=True)
    return jnp.sum(got, axis=0)


def solution(mesh):
    return jax.shard_map(
        shards,
        mesh=mesh,
        in_specs=(
            P(("groups", "dp"), None),
            P(("groups", "dp"), None),
            P(("groups", "dp"), None),
            P(("groups", "dp"), None),
            P(("groups", "dp")),
            P(("groups", "dp")),
        ),
        out_specs=P(("groups", "dp"), None),
        check_vma=False,
    )
```

```python
import functools
import math

import jax
import jax.numpy as jnp
import numpy as np
from jax import lax
from jax.experimental import pallas as pl
from jax.experimental.pallas import tpu as pltpu
from jax.sharding import PartitionSpec as P

RANK = 32
LEN = 80
F32 = jnp.float32
VMEM = 52 << 20


def ring_of(chips):
    cols = max([d for d in range(1, math.isqrt(chips) + 1) if chips % d == 0 and d % 2 == 0] or [1])
    rows = chips // cols
    if cols == 1 or rows % 2:
        return list(range(chips))
    walk = []
    for r in range(rows):
        line = range(1, cols) if r % 2 == 0 else range(cols - 1, 0, -1)
        walk += [r * cols + c for c in line]
    return walk + [r * cols for r in reversed(range(rows))]


def block_orders(chips):
    ring = ring_of(chips)
    order = np.zeros((2 * chips, chips), np.int32)
    for p, chip in enumerate(ring):
        for s in range(chips):
            order[2 * chip, s] = 2 * ring[(p - s) % chips]
            order[2 * chip + 1, s] = 2 * ring[(p + s) % chips] + 1
    return order


def ring_pairs(chips):
    ring = ring_of(chips)
    pairs = []
    for p, chip in enumerate(ring):
        pairs.append((2 * chip, 2 * ring[(p + 1) % chips]))
        pairs.append((2 * chip + 1, 2 * ring[(p - 1) % chips] + 1))
    return pairs


def dot(a, b):
    return jnp.dot(a, b, preferred_element_type=F32)


def call(kernel, order, windows, whole, scalars, out_shape, flops, name):
    in_specs = [pl.BlockSpec((x.shape[0], w), at) for x, w, at in windows]
    in_specs += [pl.BlockSpec(x.shape, lambda i, o: (0, 0)) for x in whole]
    in_specs += [pl.BlockSpec(memory_space=pltpu.SMEM) for _ in scalars]
    size = sum(2 * x.shape[0] * w for x, w, _ in windows)
    size += sum(x.size * x.dtype.itemsize for x in list(whole) + list(out_shape))
    return pl.pallas_call(
        kernel,
        grid_spec=pltpu.PrefetchScalarGridSpec(
            num_scalar_prefetch=1,
            grid=(1,),
            in_specs=in_specs,
            out_specs=[pl.BlockSpec(x.shape, lambda i, o: (0, 0)) for x in out_shape],
        ),
        out_shape=out_shape,
        cost_estimate=pl.CostEstimate(flops=flops, bytes_accessed=size, transcendentals=0),
        compiler_params=pltpu.CompilerParams(vmem_limit_bytes=VMEM),
        name=name,
    )(order, *[x for x, _, _ in windows], *whole, *scalars)


def step_kernel(lead, rows_in, with_b, summed, order_ref, *refs):
    refs = list(refs)
    own_g, sib_g = refs.pop(0), refs.pop(0)
    own_a, sib_a = (refs.pop(0), refs.pop(0)) if rows_in else (None, None)
    a_ref = refs.pop(0)
    b_ref = refs.pop(0) if with_b else None
    tokens = own_g.shape[0]
    for k, (g, a) in enumerate(((own_g, own_a), (sib_g, sib_a))):
        at = pl.ds(k * tokens, tokens)
        out = dot(g[:, :lead], a_ref[rows_in:])
        if with_b:
            out += dot(g[:, lead:], b_ref[...])
        if summed:
            out += refs[0][at]
        if rows_in:
            inn = dot(a[...], a_ref[:rows_in])
            if summed:
                inn += refs[1][at]
            refs[-1][at] = inn
            refs[-2][at] = out
        else:
            refs[-1][at] = out


def step(order, own, sib, blocks, totals, s, lead, rows, rows_in):
    here = lambda i, o: (0, o[s])
    windows = [(own[0], rows, here), (sib[0], rows, here)]
    if rows_in:
        windows += [(own[1], rows_in, here), (sib[1], rows_in, here)]
    tokens, columns = own[0].shape[0], blocks[0].shape[1]
    depth = sum(b.shape[0] for b in blocks)
    shape = jax.ShapeDtypeStruct((2 * tokens, columns), F32)
    return call(
        functools.partial(step_kernel, lead, rows_in, len(blocks) > 1, bool(totals)),
        order, windows, list(blocks) + list(totals), [],
        [shape] * (2 if rows_in else 1), 4 * tokens * depth * columns, "step",
    )


def join_kernel(in_ref, out_ref, a_ref, b_ref, sems):
    rows_in = in_ref.shape[0]
    lead, rest = a_ref.shape[0] - rows_in, b_ref.shape[0]
    copies = [
        pltpu.make_async_copy(in_ref, a_ref.at[pl.ds(0, rows_in)], sems.at[0]),
        pltpu.make_async_copy(out_ref.at[pl.ds(0, lead)], a_ref.at[pl.ds(rows_in, lead)], sems.at[1]),
        pltpu.make_async_copy(out_ref.at[pl.ds(lead, rest)], b_ref, sems.at[2]),
    ]
    for copy in copies:
        copy.start()
    for copy in copies:
        copy.wait()


def join(in_factors, out_factors, lead):
    rows_in, columns = in_factors.shape
    heights = [rows_in + lead, out_factors.shape[0] - lead]
    return pl.pallas_call(
        join_kernel,
        in_specs=[pl.BlockSpec(memory_space=pltpu.HBM)] * 2,
        out_specs=[pl.BlockSpec(memory_space=pltpu.VMEM)] * 2,
        out_shape=[jax.ShapeDtypeStruct((h, columns), in_factors.dtype) for h in heights],
        scratch_shapes=[pltpu.SemaphoreType.DMA((3,))],
        cost_estimate=pl.CostEstimate(
            flops=0, bytes_accessed=4 * sum(heights) * columns, transcendentals=0
        ),
        name="join",
    )(in_factors, out_factors)


def window_kernel(lead, order_ref, own_ref, sib_ref, out_ref):
    tokens = own_ref.shape[0]
    out_ref[:tokens] = own_ref[:, lead:]
    out_ref[tokens:] = sib_ref[:, lead:]


def score_kernel(seq_ref, len_ref, seq_sib, len_sib, window_ref, b_ref, out_ref, inn_ref, got_ref,
                 table_ref):
    columns = b_ref.shape[1]
    tokens = window_ref.shape[0] // 2
    queries = columns // RANK
    column = lax.broadcasted_iota(jnp.int32, (columns, queries), 0) // RANK
    query = lax.broadcasted_iota(jnp.int32, (columns, queries), 1)
    fold = (column == query).astype(F32)
    position = lax.broadcasted_iota(jnp.int32, (LEN, columns), 0)
    row = lax.broadcasted_iota(jnp.int32, table_ref.shape, 0)
    out = out_ref[...] + dot(window_ref[...], b_ref[...])
    sums, slots = [], []
    for k, (seq, lens) in enumerate(((seq_ref, len_ref), (seq_sib, len_sib))):
        mine, other = pl.ds(k * tokens, tokens), pl.ds((1 - k) * tokens, tokens)
        contrib = out[k * tokens:(k + 1) * tokens] * (inn_ref[mine] + got_ref[other])
        for i in range(tokens // LEN):
            kept = jnp.where(position < lens[i], contrib[i * LEN:(i + 1) * LEN], 0.0)
            sums.append(jnp.sum(kept, axis=0, keepdims=True))
            slots.append(seq[i])
    scores = jnp.dot(
        jnp.concatenate(sums), fold, precision=lax.Precision.HIGHEST, preferred_element_type=F32
    ) * (1.0 / math.sqrt(RANK * LEN))
    table = jnp.zeros(table_ref.shape, F32)
    for i, slot in enumerate(slots):
        table = jnp.where(row == slot, scores[i:i + 1], table)
    table_ref[...] = table


def score_table(numbers, arrays, rows, queries):
    smem, vmem = (pl.BlockSpec(memory_space=m) for m in (pltpu.SMEM, pltpu.VMEM))
    window, block = arrays[:2]
    size = sum(x.size * x.dtype.itemsize for x in arrays)
    return pl.pallas_call(
        score_kernel,
        in_specs=[smem] * len(numbers) + [vmem] * len(arrays),
        out_specs=vmem,
        out_shape=jax.ShapeDtypeStruct((rows, queries), F32),
        cost_estimate=pl.CostEstimate(
            flops=2 * window.size * block.shape[1], bytes_accessed=size, transcendentals=0
        ),
        compiler_params=pltpu.CompilerParams(vmem_limit_bytes=16 << 20),
        name="score",
    )(*numbers, *arrays)


def shards(acts, grads, out_factors, in_factors, seq_slot, lengths):
    devices = lax.axis_size("dp")
    chips = devices // 2
    me = lax.axis_index("dp")
    tokens = grads.shape[0]
    rows, columns = out_factors.shape
    rows_in = in_factors.shape[0]
    orders = jnp.asarray(block_orders(chips))
    mine = lax.dynamic_index_in_dim(orders, me, keepdims=False)
    pairs = ring_pairs(chips)
    swap = [(d, d ^ 1) for d in range(devices)]

    own = [grads, acts]
    every = None
    if rows_in % 128:
        every = lax.all_gather(in_factors, "dp", axis=0, tiled=True)
        own, rows_in = own[:1], 0
    lead = (rows - rows_in) // 2
    if rows_in:
        held = [join(in_factors, out_factors, lead)]
    else:
        held = [(out_factors[:lead], out_factors[lead:])]

    seq_sib, len_sib = lax.ppermute(jnp.stack([seq_slot, lengths]), "dp", swap)
    sib = [lax.ppermute(x, "dp", swap) for x in own]
    totals, summed = [], 0

    def sum_to(k, totals, summed):
        for j in range(summed, k):
            totals = step(mine, own, sib, held[j], totals, j, lead, rows, rows_in)
        return totals, max(k, summed)

    for s in range(chips - 1):
        a, b = held[s]
        if s >= 3:
            totals, summed = sum_to(min(2 * s - 5, s), totals, summed)
            a, *totals = lax.optimization_barrier((a, *totals))
            b, *totals = lax.optimization_barrier((b, *totals))
        held.append((lax.ppermute(a, "dp", pairs), lax.ppermute(b, "dp", pairs)))
    s = chips - 1
    window = call(
        functools.partial(window_kernel, lead), mine,
        [(x, rows, lambda i, o: (0, o[s])) for x in (own[0], sib[0])], [], [],
        [jax.ShapeDtypeStruct((2 * tokens, rows - lead), grads.dtype)], 0, "window",
    )[0]
    totals[0], window = lax.optimization_barrier((totals[0], window))
    totals, summed = sum_to(s, totals, summed)
    a, b = held[s]
    totals = step(mine, own, sib, [a], totals, s, lead, rows, rows_in)
    if every is not None:
        inn = dot(acts, every)
        totals = [totals[0], jnp.concatenate([inn, jnp.zeros_like(inn)])]
    got = lax.ppermute(totals[1], "dp", swap)

    slots = lengths.shape[0]
    queries = columns // RANK
    table = score_table(
        [seq_slot, lengths, seq_sib, len_sib], [window, b, *totals, got], slots * devices, queries
    )
    got = lax.all_to_all(table.reshape(devices, slots, queries), "dp", 0, 0, tiled=True)
    return jnp.sum(got, axis=0)


def solution(mesh):
    return jax.shard_map(
        shards,
        mesh=mesh,
        in_specs=(
            P(("groups", "dp"), None),
            P(("groups", "dp"), None),
            P(("groups", "dp"), None),
            P(("groups", "dp"), None),
            P(("groups", "dp")),
            P(("groups", "dp")),
        ),
        out_specs=P(("groups", "dp"), None),
        check_vma=False,
    )
```

```python
import functools
import math

import jax
import jax.numpy as jnp
import numpy as np
from jax import lax
from jax.experimental import pallas as pl
from jax.experimental.pallas import tpu as pltpu
from jax.sharding import PartitionSpec as P

RANK = 32
LEN = 80
F32 = jnp.float32
VMEM = 52 << 20


def ring_of(chips):
    cols = max([d for d in range(1, math.isqrt(chips) + 1) if chips % d == 0 and d % 2 == 0] or [1])
    rows = chips // cols
    if cols == 1 or rows % 2:
        return list(range(chips))
    walk = []
    for r in range(rows):
        line = range(1, cols) if r % 2 == 0 else range(cols - 1, 0, -1)
        walk += [r * cols + c for c in line]
    return walk + [r * cols for r in reversed(range(rows))]


def block_orders(chips):
    ring = ring_of(chips)
    order = np.zeros((2 * chips, chips), np.int32)
    for p, chip in enumerate(ring):
        for s in range(chips):
            order[2 * chip, s] = 2 * ring[(p - s) % chips]
            order[2 * chip + 1, s] = 2 * ring[(p + s) % chips] + 1
    return order


def ring_pairs(chips):
    ring = ring_of(chips)
    pairs = []
    for p, chip in enumerate(ring):
        pairs.append((2 * chip, 2 * ring[(p + 1) % chips]))
        pairs.append((2 * chip + 1, 2 * ring[(p - 1) % chips] + 1))
    return pairs


def dot(a, b):
    return jnp.dot(a, b, preferred_element_type=F32)


def call(kernel, order, windows, whole, scalars, out_shape, flops, name):
    in_specs = [pl.BlockSpec((x.shape[0], w), at) for x, w, at in windows]
    in_specs += [pl.BlockSpec(x.shape, lambda i, o: (0, 0)) for x in whole]
    in_specs += [pl.BlockSpec(memory_space=pltpu.SMEM) for _ in scalars]
    size = sum(2 * x.shape[0] * w for x, w, _ in windows)
    size += sum(x.size * x.dtype.itemsize for x in list(whole) + list(out_shape))
    return pl.pallas_call(
        kernel,
        grid_spec=pltpu.PrefetchScalarGridSpec(
            num_scalar_prefetch=1,
            grid=(1,),
            in_specs=in_specs,
            out_specs=[pl.BlockSpec(x.shape, lambda i, o: (0, 0)) for x in out_shape],
        ),
        out_shape=out_shape,
        cost_estimate=pl.CostEstimate(flops=flops, bytes_accessed=size, transcendentals=0),
        compiler_params=pltpu.CompilerParams(vmem_limit_bytes=VMEM),
        name=name,
    )(order, *[x for x, _, _ in windows], *whole, *scalars)


def step_kernel(lead, rows_in, with_b, summed, order_ref, *refs):
    refs = list(refs)
    own_g, sib_g = refs.pop(0), refs.pop(0)
    own_a, sib_a = (refs.pop(0), refs.pop(0)) if rows_in else (None, None)
    a_ref = refs.pop(0)
    b_ref = refs.pop(0) if with_b else None
    tokens = own_g.shape[0]
    for k, (g, a) in enumerate(((own_g, own_a), (sib_g, sib_a))):
        at = pl.ds(k * tokens, tokens)
        out = dot(g[:, :lead], a_ref[rows_in:])
        if with_b:
            out += dot(g[:, lead:], b_ref[...])
        if summed:
            out += refs[0][at]
        if rows_in:
            inn = dot(a[...], a_ref[:rows_in])
            if summed:
                inn += refs[1][at]
            refs[-1][at] = inn
            refs[-2][at] = out
        else:
            refs[-1][at] = out


def step(order, own, sib, blocks, totals, s, lead, rows, rows_in):
    here = lambda i, o: (0, o[s])
    windows = [(own[0], rows, here), (sib[0], rows, here)]
    if rows_in:
        windows += [(own[1], rows_in, here), (sib[1], rows_in, here)]
    tokens, columns = own[0].shape[0], blocks[0].shape[1]
    depth = sum(b.shape[0] for b in blocks)
    shape = jax.ShapeDtypeStruct((2 * tokens, columns), F32)
    return call(
        functools.partial(step_kernel, lead, rows_in, len(blocks) > 1, bool(totals)),
        order, windows, list(blocks) + list(totals), [],
        [shape] * (2 if rows_in else 1), 4 * tokens * depth * columns, "step",
    )


def join_kernel(in_ref, out_ref, a_ref, b_ref, sems):
    rows_in = in_ref.shape[0]
    lead, rest = a_ref.shape[0] - rows_in, b_ref.shape[0]
    copies = [
        pltpu.make_async_copy(in_ref, a_ref.at[pl.ds(0, rows_in)], sems.at[0]),
        pltpu.make_async_copy(out_ref.at[pl.ds(0, lead)], a_ref.at[pl.ds(rows_in, lead)], sems.at[1]),
        pltpu.make_async_copy(out_ref.at[pl.ds(lead, rest)], b_ref, sems.at[2]),
    ]
    for copy in copies:
        copy.start()
    for copy in copies:
        copy.wait()


def join(in_factors, out_factors, lead):
    rows_in, columns = in_factors.shape
    heights = [rows_in + lead, out_factors.shape[0] - lead]
    return pl.pallas_call(
        join_kernel,
        in_specs=[pl.BlockSpec(memory_space=pltpu.HBM)] * 2,
        out_specs=[pl.BlockSpec(memory_space=pltpu.VMEM)] * 2,
        out_shape=[jax.ShapeDtypeStruct((h, columns), in_factors.dtype) for h in heights],
        scratch_shapes=[pltpu.SemaphoreType.DMA((3,))],
        cost_estimate=pl.CostEstimate(
            flops=0, bytes_accessed=4 * sum(heights) * columns, transcendentals=0
        ),
        name="join",
    )(in_factors, out_factors)


def window_kernel(lead, order_ref, own_ref, sib_ref, out_ref):
    tokens = own_ref.shape[0]
    out_ref[:tokens] = own_ref[:, lead:]
    out_ref[tokens:] = sib_ref[:, lead:]


def score_kernel(seq_ref, len_ref, seq_sib, len_sib, window_ref, b_ref, out_ref, inn_ref, got_ref,
                 table_ref):
    columns = b_ref.shape[1]
    tokens = window_ref.shape[0] // 2
    queries = columns // RANK
    column = lax.broadcasted_iota(jnp.int32, (columns, queries), 0) // RANK
    query = lax.broadcasted_iota(jnp.int32, (columns, queries), 1)
    fold = (column == query).astype(F32)
    position = lax.broadcasted_iota(jnp.int32, (LEN, columns), 0)
    row = lax.broadcasted_iota(jnp.int32, table_ref.shape, 0)
    out = out_ref[...] + dot(window_ref[...], b_ref[...])
    sums, slots = [], []
    for k, (seq, lens) in enumerate(((seq_ref, len_ref), (seq_sib, len_sib))):
        mine, other = pl.ds(k * tokens, tokens), pl.ds((1 - k) * tokens, tokens)
        contrib = out[k * tokens:(k + 1) * tokens] * (inn_ref[mine] + got_ref[other])
        for i in range(tokens // LEN):
            kept = jnp.where(position < lens[i], contrib[i * LEN:(i + 1) * LEN], 0.0)
            sums.append(jnp.sum(kept, axis=0, keepdims=True))
            slots.append(seq[i])
    scores = jnp.dot(
        jnp.concatenate(sums), fold, precision=lax.Precision.HIGHEST, preferred_element_type=F32
    ) * (1.0 / math.sqrt(RANK * LEN))
    table = jnp.zeros(table_ref.shape, F32)
    for i, slot in enumerate(slots):
        table = jnp.where(row == slot, scores[i:i + 1], table)
    table_ref[...] = table


def score_table(numbers, arrays, rows, queries):
    smem, vmem = (pl.BlockSpec(memory_space=m) for m in (pltpu.SMEM, pltpu.VMEM))
    window, block = arrays[:2]
    size = sum(x.size * x.dtype.itemsize for x in arrays)
    return pl.pallas_call(
        score_kernel,
        in_specs=[smem] * len(numbers) + [vmem] * len(arrays),
        out_specs=vmem,
        out_shape=jax.ShapeDtypeStruct((rows, queries), F32),
        cost_estimate=pl.CostEstimate(
            flops=2 * window.size * block.shape[1], bytes_accessed=size, transcendentals=0
        ),
        compiler_params=pltpu.CompilerParams(vmem_limit_bytes=16 << 20),
        name="score",
    )(*numbers, *arrays)


def shards(acts, grads, out_factors, in_factors, seq_slot, lengths):
    devices = lax.axis_size("dp")
    chips = devices // 2
    me = lax.axis_index("dp")
    tokens = grads.shape[0]
    rows, columns = out_factors.shape
    rows_in = in_factors.shape[0]
    orders = jnp.asarray(block_orders(chips))
    mine = lax.dynamic_index_in_dim(orders, me, keepdims=False)
    pairs = ring_pairs(chips)
    swap = [(d, d ^ 1) for d in range(devices)]

    own = [grads, acts]
    every = None
    if rows_in % 128:
        every = lax.all_gather(in_factors, "dp", axis=0, tiled=True)
        own, rows_in = own[:1], 0
    lead = (rows - rows_in) // 2
    if rows_in:
        held = [list(join(in_factors, out_factors, lead))]
        *held[0], grads, acts = lax.optimization_barrier((*held[0], grads, acts))
        own = [grads, acts]
    else:
        held = [(out_factors[:lead], out_factors[lead:])]

    seq_sib, len_sib = lax.ppermute(jnp.stack([seq_slot, lengths]), "dp", swap)
    sib = [lax.ppermute(x, "dp", swap) for x in own]
    totals, summed = [], 0

    def sum_to(k, totals, summed):
        for j in range(summed, k):
            totals = step(mine, own, sib, held[j], totals, j, lead, rows, rows_in)
        return totals, max(k, summed)

    for s in range(chips - 1):
        a, b = held[s]
        if s >= 3:
            totals, summed = sum_to(min(2 * s - 5, s), totals, summed)
            a, *totals = lax.optimization_barrier((a, *totals))
            b, *totals = lax.optimization_barrier((b, *totals))
        held.append((lax.ppermute(a, "dp", pairs), lax.ppermute(b, "dp", pairs)))
    s = chips - 1
    window = call(
        functools.partial(window_kernel, lead), mine,
        [(x, rows, lambda i, o: (0, o[s])) for x in (own[0], sib[0])], [], [],
        [jax.ShapeDtypeStruct((2 * tokens, rows - lead), grads.dtype)], 0, "window",
    )[0]
    totals[0], window = lax.optimization_barrier((totals[0], window))
    totals, summed = sum_to(s, totals, summed)
    a, b = held[s]
    totals = step(mine, own, sib, [a], totals, s, lead, rows, rows_in)
    if every is not None:
        inn = dot(acts, every)
        totals = [totals[0], jnp.concatenate([inn, jnp.zeros_like(inn)])]
    got = lax.ppermute(totals[1], "dp", swap)

    slots = lengths.shape[0]
    queries = columns // RANK
    table = score_table(
        [seq_slot, lengths, seq_sib, len_sib], [window, b, *totals, got], slots * devices, queries
    )
    got = lax.all_to_all(table.reshape(devices, slots, queries), "dp", 0, 0, tiled=True)
    return jnp.sum(got, axis=0)


def solution(mesh):
    return jax.shard_map(
        shards,
        mesh=mesh,
        in_specs=(
            P(("groups", "dp"), None),
            P(("groups", "dp"), None),
            P(("groups", "dp"), None),
            P(("groups", "dp"), None),
            P(("groups", "dp")),
            P(("groups", "dp")),
        ),
        out_specs=P(("groups", "dp"), None),
        check_vma=False,
    )
```

```python
import functools
import math

import jax
import jax.numpy as jnp
import numpy as np
from jax import lax
from jax.experimental import pallas as pl
from jax.experimental.pallas import tpu as pltpu
from jax.sharding import PartitionSpec as P

RANK = 32
LEN = 80
F32 = jnp.float32
VMEM = 52 << 20


def ring_of(chips):
    cols = max([d for d in range(1, math.isqrt(chips) + 1) if chips % d == 0 and d % 2 == 0] or [1])
    rows = chips // cols
    if cols == 1 or rows % 2:
        return list(range(chips))
    walk = []
    for r in range(rows):
        line = range(1, cols) if r % 2 == 0 else range(cols - 1, 0, -1)
        walk += [r * cols + c for c in line]
    return walk + [r * cols for r in reversed(range(rows))]


def block_orders(chips):
    ring = ring_of(chips)
    order = np.zeros((2 * chips, chips), np.int32)
    for p, chip in enumerate(ring):
        for s in range(chips):
            order[2 * chip, s] = 2 * ring[(p - s) % chips]
            order[2 * chip + 1, s] = 2 * ring[(p + s) % chips] + 1
    return order


def ring_pairs(chips):
    ring = ring_of(chips)
    pairs = []
    for p, chip in enumerate(ring):
        pairs.append((2 * chip, 2 * ring[(p + 1) % chips]))
        pairs.append((2 * chip + 1, 2 * ring[(p - 1) % chips] + 1))
    return pairs


def dot(a, b):
    return jnp.dot(a, b, preferred_element_type=F32)


def call(kernel, order, windows, whole, scalars, out_shape, flops, name):
    in_specs = [pl.BlockSpec((x.shape[0], w), at) for x, w, at in windows]
    in_specs += [pl.BlockSpec(x.shape, lambda i, o: (0, 0)) for x in whole]
    in_specs += [pl.BlockSpec(memory_space=pltpu.SMEM) for _ in scalars]
    size = sum(2 * x.shape[0] * w for x, w, _ in windows)
    size += sum(x.size * x.dtype.itemsize for x in list(whole) + list(out_shape))
    return pl.pallas_call(
        kernel,
        grid_spec=pltpu.PrefetchScalarGridSpec(
            num_scalar_prefetch=1,
            grid=(1,),
            in_specs=in_specs,
            out_specs=[pl.BlockSpec(x.shape, lambda i, o: (0, 0)) for x in out_shape],
        ),
        out_shape=out_shape,
        cost_estimate=pl.CostEstimate(flops=flops, bytes_accessed=size, transcendentals=0),
        compiler_params=pltpu.CompilerParams(vmem_limit_bytes=VMEM),
        name=name,
    )(order, *[x for x, _, _ in windows], *whole, *scalars)


def step_kernel(pieces, kinds, count, summed, order_ref, *refs):
    windows = {kind: refs[2 * i:2 * i + 2] for i, kind in enumerate(kinds)}
    blocks, refs = refs[2 * len(kinds):2 * len(kinds) + count], refs[2 * len(kinds) + count:]
    tokens = windows[kinds[0]][0].shape[0]
    for i, kind in enumerate(kinds):
        for k in range(2):
            at = pl.ds(k * tokens, tokens)
            total = refs[i][at] if summed else 0.0
            for which, row, height, of, column in pieces:
                if of == kind:
                    window = windows[kind][k][:, column:column + height]
                    total += dot(window, blocks[which][row:row + height])
            refs[i - len(kinds)][at] = total


def step(order, tokens_of, blocks, pieces, totals, s):
    kinds = sorted({piece[3] for piece in pieces})
    windows = []
    for kind in kinds:
        own, sib, width = tokens_of[kind]
        windows += [(x, width, lambda i, o: (0, o[s])) for x in (own, sib)]
    tokens, columns = windows[0][0].shape[0], blocks[0].shape[1]
    summed = all(kind in totals for kind in kinds)
    shape = jax.ShapeDtypeStruct((2 * tokens, columns), F32)
    out = call(
        functools.partial(step_kernel, pieces, kinds, len(blocks), summed),
        order, windows, list(blocks) + ([totals[k] for k in kinds] if summed else []), [],
        [shape] * len(kinds), 4 * tokens * sum(p[2] for p in pieces) * columns, "step",
    )
    return {**totals, **dict(zip(kinds, out))}


def window_kernel(lead, order_ref, own_ref, sib_ref, out_ref):
    tokens = own_ref.shape[0]
    out_ref[:tokens] = own_ref[:, :lead]
    out_ref[tokens:] = sib_ref[:, :lead]


def score_kernel(seq_ref, len_ref, seq_sib, len_sib, window_ref, b_ref, out_ref, inn_ref, got_ref,
                 table_ref):
    columns = b_ref.shape[1]
    tokens = window_ref.shape[0] // 2
    queries = columns // RANK
    column = lax.broadcasted_iota(jnp.int32, (columns, queries), 0) // RANK
    query = lax.broadcasted_iota(jnp.int32, (columns, queries), 1)
    fold = (column == query).astype(F32)
    position = lax.broadcasted_iota(jnp.int32, (LEN, columns), 0)
    row = lax.broadcasted_iota(jnp.int32, table_ref.shape, 0)
    out = out_ref[...] + dot(window_ref[...], b_ref[...])
    sums, slots = [], []
    for k, (seq, lens) in enumerate(((seq_ref, len_ref), (seq_sib, len_sib))):
        mine, other = pl.ds(k * tokens, tokens), pl.ds((1 - k) * tokens, tokens)
        contrib = out[k * tokens:(k + 1) * tokens] * (inn_ref[mine] + got_ref[other])
        for i in range(tokens // LEN):
            kept = jnp.where(position < lens[i], contrib[i * LEN:(i + 1) * LEN], 0.0)
            sums.append(jnp.sum(kept, axis=0, keepdims=True))
            slots.append(seq[i])
    scores = jnp.dot(
        jnp.concatenate(sums), fold, precision=lax.Precision.HIGHEST, preferred_element_type=F32
    ) * (1.0 / math.sqrt(RANK * LEN))
    table = jnp.zeros(table_ref.shape, F32)
    for i, slot in enumerate(slots):
        table = jnp.where(row == slot, scores[i:i + 1], table)
    table_ref[...] = table


def score_table(numbers, arrays, rows, queries):
    smem, vmem = (pl.BlockSpec(memory_space=m) for m in (pltpu.SMEM, pltpu.VMEM))
    window, block = arrays[:2]
    size = sum(x.size * x.dtype.itemsize for x in arrays)
    return pl.pallas_call(
        score_kernel,
        in_specs=[smem] * len(numbers) + [vmem] * len(arrays),
        out_specs=vmem,
        out_shape=jax.ShapeDtypeStruct((rows, queries), F32),
        cost_estimate=pl.CostEstimate(
            flops=2 * window.size * block.shape[1], bytes_accessed=size, transcendentals=0
        ),
        compiler_params=pltpu.CompilerParams(vmem_limit_bytes=16 << 20),
        name="score",
    )(*numbers, *arrays)


def shards(acts, grads, out_factors, in_factors, seq_slot, lengths):
    devices = lax.axis_size("dp")
    chips = devices // 2
    me = lax.axis_index("dp")
    tokens = grads.shape[0]
    rows, columns = out_factors.shape
    rows_in = in_factors.shape[0]
    orders = jnp.asarray(block_orders(chips))
    mine = lax.dynamic_index_in_dim(orders, me, keepdims=False)
    pairs = ring_pairs(chips)
    swap = [(d, d ^ 1) for d in range(devices)]

    send = lambda x: lax.ppermute(x, "dp", pairs)
    across = lambda x: lax.ppermute(x, "dp", swap)

    every = None
    if rows_in % 128:
        every = lax.all_gather(in_factors, "dp", axis=0, tiled=True)
        rows_in = 0
    lead = (rows - rows_in) // 2
    tokens_of = {"out": (grads, across(grads), rows)}
    if rows_in:
        tokens_of["in"] = (acts, across(acts), rows_in)
    slots_sib = across(jnp.stack([seq_slot, lengths]))

    inside = [(1, 0, rows_in, "in", 0)] if rows_in else []
    held = [[out_factors] + [in_factors] * (rows_in > 0)]
    pieces = [[(0, 0, rows, "out", 0)] + inside]
    came = send(out_factors)
    late, early = came[lead:], came[:lead]
    if rows_in:
        early = jnp.concatenate([send(in_factors), early])
    totals, summed = {}, 0

    def sum_to(k, totals, summed):
        for j in range(summed, k):
            totals = step(mine, tokens_of, held[j], pieces[j], totals, j)
        return totals, max(k, summed)

    last = chips - 1
    for s in range(1, chips):
        held.append([late, early])
        pieces.append([(0, 0, rows - lead, "out", lead), (1, rows_in, lead, "out", 0)] + inside)
        if s == last:
            break
        if s >= 3:
            totals, summed = sum_to(min(2 * s - 5, s), totals, summed)
            late, totals = lax.optimization_barrier((late, totals))
            early, totals = lax.optimization_barrier((early, totals))
        late = send(late)
        if s < last - 1:
            early = send(early)
        else:
            inner, early = early[:rows_in], early[rows_in:]
            if rows_in:
                inner = send(inner)
            early = send(early)

    window = call(
        functools.partial(window_kernel, lead), mine,
        [(x, rows, lambda i, o: (0, o[last])) for x in tokens_of["out"][:2]], [], [],
        [jax.ShapeDtypeStruct((2 * tokens, lead), grads.dtype)], 0, "window",
    )[0]
    totals, window, slots_sib = lax.optimization_barrier((totals, window, slots_sib))
    seq_sib, len_sib = slots_sib
    totals, summed = sum_to(last, totals, summed)
    totals = step(mine, tokens_of, [late], pieces[last][:1], totals, last)
    if rows_in:
        totals, inner = lax.optimization_barrier((totals, inner))
        totals = step(mine, tokens_of, [inner], [(0, 0, rows_in, "in", 0)], totals, last)
        inn = totals["in"]
    else:
        inn = dot(acts, every)
        inn = jnp.concatenate([inn, jnp.zeros_like(inn)])
    got = across(inn)

    slots = lengths.shape[0]
    queries = columns // RANK
    table = score_table(
        [seq_slot, lengths, seq_sib, len_sib], [window, early, totals["out"], inn, got],
        slots * devices, queries,
    )
    got = lax.all_to_all(table.reshape(devices, slots, queries), "dp", 0, 0, tiled=True)
    return jnp.sum(got, axis=0)


def solution(mesh):
    return jax.shard_map(
        shards,
        mesh=mesh,
        in_specs=(
            P(("groups", "dp"), None),
            P(("groups", "dp"), None),
            P(("groups", "dp"), None),
            P(("groups", "dp"), None),
            P(("groups", "dp")),
            P(("groups", "dp")),
        ),
        out_specs=P(("groups", "dp"), None),
        check_vma=False,
    )
```

```python
import functools
import math

import jax
import jax.numpy as jnp
import numpy as np
from jax import lax
from jax.experimental import pallas as pl
from jax.experimental.pallas import tpu as pltpu
from jax.sharding import PartitionSpec as P

RANK = 32
LEN = 80
F32 = jnp.float32
PAD = 8
VMEM = 52 << 20


def ring_of(chips):
    cols = max([d for d in range(1, math.isqrt(chips) + 1) if chips % d == 0 and d % 2 == 0] or [1])
    rows = chips // cols
    if cols == 1 or rows % 2:
        return list(range(chips))
    walk = []
    for r in range(rows):
        line = range(1, cols) if r % 2 == 0 else range(cols - 1, 0, -1)
        walk += [r * cols + c for c in line]
    return walk + [r * cols for r in reversed(range(rows))]


def block_orders(chips):
    ring = ring_of(chips)
    order = np.zeros((2 * chips, chips), np.int32)
    for p, chip in enumerate(ring):
        for s in range(chips):
            order[2 * chip, s] = 2 * ring[(p - s) % chips]
            order[2 * chip + 1, s] = 2 * ring[(p + s) % chips] + 1
    return order


def ring_pairs(chips):
    ring = ring_of(chips)
    pairs = []
    for p, chip in enumerate(ring):
        pairs.append((2 * chip, 2 * ring[(p + 1) % chips]))
        pairs.append((2 * chip + 1, 2 * ring[(p - 1) % chips] + 1))
    return pairs


def dot(a, b):
    return jnp.dot(a, b, preferred_element_type=F32)


def call(kernel, order, windows, whole, scalars, out_shape, flops, name):
    in_specs = [pl.BlockSpec((x.shape[0], w), at) for x, w, at in windows]
    in_specs += [pl.BlockSpec(x.shape, lambda i, o: (0, 0)) for x in whole]
    in_specs += [pl.BlockSpec(memory_space=pltpu.SMEM) for _ in scalars]
    size = sum(2 * x.shape[0] * w for x, w, _ in windows)
    size += sum(x.size * x.dtype.itemsize for x in list(whole) + list(out_shape))
    return pl.pallas_call(
        kernel,
        grid_spec=pltpu.PrefetchScalarGridSpec(
            num_scalar_prefetch=1,
            grid=(1,),
            in_specs=in_specs,
            out_specs=[pl.BlockSpec(x.shape, lambda i, o: (0, 0)) for x in out_shape],
        ),
        out_shape=out_shape,
        cost_estimate=pl.CostEstimate(flops=flops, bytes_accessed=size, transcendentals=0),
        compiler_params=pltpu.CompilerParams(vmem_limit_bytes=VMEM),
        name=name,
    )(order, *[x for x, _, _ in windows], *whole, *scalars)


def step_kernel(pieces, kinds, count, summed, order_ref, *refs):
    windows = {kind: refs[2 * i:2 * i + 2] for i, kind in enumerate(kinds)}
    blocks, refs = refs[2 * len(kinds):2 * len(kinds) + count], refs[2 * len(kinds) + count:]
    tokens = windows[kinds[0]][0].shape[0]
    for i, kind in enumerate(kinds):
        for k in range(2):
            at = pl.ds(k * tokens, tokens)
            total = refs[i][at] if summed else 0.0
            for which, row, height, of, column in pieces:
                if of == kind:
                    window = windows[kind][k][:, column:column + height]
                    total += dot(window, blocks[which][row:row + height])
            refs[i - len(kinds)][at] = total


def step(order, tokens_of, blocks, pieces, totals, s):
    kinds = sorted({piece[3] for piece in pieces})
    windows = []
    for kind in kinds:
        own, sib, width = tokens_of[kind]
        windows += [(x, width, lambda i, o: (0, o[s])) for x in (own, sib)]
    tokens, columns = windows[0][0].shape[0], blocks[0].shape[1]
    summed = all(kind in totals for kind in kinds)
    shape = jax.ShapeDtypeStruct((2 * tokens, columns), F32)
    out = call(
        functools.partial(step_kernel, pieces, kinds, len(blocks), summed),
        order, windows, list(blocks) + ([totals[k] for k in kinds] if summed else []), [],
        [shape] * len(kinds), 4 * tokens * sum(p[2] for p in pieces) * columns, "step",
    )
    return {**totals, **dict(zip(kinds, out))}


def window_kernel(lead, order_ref, own_ref, sib_ref, out_ref):
    tokens = own_ref.shape[0]
    out_ref[:tokens] = own_ref[:, :lead]
    out_ref[tokens:] = sib_ref[:, :lead]


def score_kernel(per_device, me_ref, seq_ref, len_ref, seq_sib, len_sib, window_ref, b_ref, out_ref,
                 inn_ref, got_ref, *tables):
    columns = b_ref.shape[1]
    tokens = window_ref.shape[0] // 2
    queries = columns // RANK
    shape = tables[0].shape
    column = lax.broadcasted_iota(jnp.int32, (columns, shape[1]), 0) // RANK
    query = lax.broadcasted_iota(jnp.int32, (columns, shape[1]), 1)
    fold = (column == query).astype(F32)
    position = lax.broadcasted_iota(jnp.int32, (LEN, columns), 0)
    row = lax.broadcasted_iota(jnp.int32, shape, 0)
    out = out_ref[...] + dot(window_ref[...], b_ref[...])
    sums, seqs = [], []
    for k, (seq, lens) in enumerate(((seq_ref, len_ref), (seq_sib, len_sib))):
        mine, other = pl.ds(k * tokens, tokens), pl.ds((1 - k) * tokens, tokens)
        contrib = out[k * tokens:(k + 1) * tokens] * (inn_ref[mine] + got_ref[other])
        for i in range(tokens // LEN):
            kept = jnp.where(position < lens[i], contrib[i * LEN:(i + 1) * LEN], 0.0)
            sums.append(jnp.sum(kept, axis=0, keepdims=True))
            seqs.append(seq[i])
    scores = jnp.dot(
        jnp.concatenate(sums), fold, precision=lax.Precision.HIGHEST, preferred_element_type=F32
    ) * (1.0 / math.sqrt(RANK * LEN))
    me = me_ref[0]
    for t, table_ref in enumerate(tables):
        table = jnp.zeros(shape, F32)
        for i, seq in enumerate(seqs):
            at = seq
            if len(tables) == 2:
                chips = shape[0] // PAD
                owner = lax.div(seq, per_device)
                ahead = lax.rem(lax.div(owner, 2) - lax.div(me, 2) + chips, chips)
                at = ahead * PAD + lax.rem(seq, per_device)
                same = lax.rem(owner + me, 2) == t
                at = jnp.where(same, at, -1)
            table = jnp.where(row == at, scores[i:i + 1], table)
        table_ref[...] = table


def score_tables(numbers, arrays, per_device, shape, count):
    smem, vmem = (pl.BlockSpec(memory_space=m) for m in (pltpu.SMEM, pltpu.VMEM))
    window, block = arrays[:2]
    size = sum(x.size * x.dtype.itemsize for x in arrays)
    return pl.pallas_call(
        functools.partial(score_kernel, per_device),
        in_specs=[smem] * len(numbers) + [vmem] * len(arrays),
        out_specs=[vmem] * count,
        out_shape=[jax.ShapeDtypeStruct(shape, F32)] * count,
        cost_estimate=pl.CostEstimate(
            flops=2 * window.size * block.shape[1], bytes_accessed=size, transcendentals=0
        ),
        compiler_params=pltpu.CompilerParams(vmem_limit_bytes=16 << 20),
        name="score",
    )(*numbers, *arrays)


def deal_kernel(mine_ref, got_ref, *outs):
    for k, out_ref in enumerate(outs):
        at = pl.ds(k * PAD, PAD)
        out_ref[...] = mine_ref[at] + got_ref[at]


def gather_kernel(*refs):
    total = refs[0][...]
    for ref in refs[1:-1]:
        total += ref[...]
    rows, queries = refs[-1].shape
    refs[-1][...] = total[:rows, :queries]


def exchange(tables, rows, queries):
    chips = lax.axis_size("dp") // 2
    vmem = pl.BlockSpec(memory_space=pltpu.VMEM)
    got = lax.ppermute(tables[1], "dp", [(d, d ^ 1) for d in range(2 * chips)])
    parts = pl.pallas_call(
        deal_kernel,
        in_specs=[vmem] * 2,
        out_specs=[vmem] * chips,
        out_shape=[jax.ShapeDtypeStruct((PAD, tables[0].shape[1]), F32)] * chips,
        name="deal",
    )(tables[0], got)
    parts = list(parts)
    for k in range(1, chips):
        ahead = [(d, (d + 2 * k) % (2 * chips)) for d in range(2 * chips)]
        parts[k] = lax.ppermute(parts[k], "dp", ahead)
    return pl.pallas_call(
        gather_kernel,
        in_specs=[vmem] * chips,
        out_specs=vmem,
        out_shape=jax.ShapeDtypeStruct((rows, queries), F32),
        name="gather",
    )(*parts)


def shards(acts, grads, out_factors, in_factors, seq_slot, lengths):
    devices = lax.axis_size("dp")
    chips = devices // 2
    me = lax.axis_index("dp")
    tokens = grads.shape[0]
    rows, columns = out_factors.shape
    rows_in = in_factors.shape[0]
    orders = jnp.asarray(block_orders(chips))
    mine = lax.dynamic_index_in_dim(orders, me, keepdims=False)
    pairs = ring_pairs(chips)
    swap = [(d, d ^ 1) for d in range(devices)]

    send = lambda x: lax.ppermute(x, "dp", pairs)
    across = lambda x: lax.ppermute(x, "dp", swap)

    every = None
    if rows_in % 128:
        every = lax.all_gather(in_factors, "dp", axis=0, tiled=True)
        rows_in = 0
    lead = (rows - rows_in) // 2
    tokens_of = {"out": (grads, across(grads), rows)}
    if rows_in:
        tokens_of["in"] = (acts, across(acts), rows_in)
    slots_sib = across(jnp.stack([seq_slot, lengths]))

    inside = [(1, 0, rows_in, "in", 0)] if rows_in else []
    held = [[out_factors] + [in_factors] * (rows_in > 0)]
    pieces = [[(0, 0, rows, "out", 0)] + inside]
    came = send(out_factors)
    late, early = came[lead:], came[:lead]
    if rows_in:
        early = jnp.concatenate([send(in_factors), early])
    totals, summed = {}, 0

    def sum_to(k, totals, summed):
        for j in range(summed, k):
            totals = step(mine, tokens_of, held[j], pieces[j], totals, j)
        return totals, max(k, summed)

    last = chips - 1
    for s in range(1, chips):
        held.append([late, early])
        pieces.append([(0, 0, rows - lead, "out", lead), (1, rows_in, lead, "out", 0)] + inside)
        if s == last:
            break
        if s >= 3:
            totals, summed = sum_to(min(2 * s - 5, s), totals, summed)
            late, totals = lax.optimization_barrier((late, totals))
            early, totals = lax.optimization_barrier((early, totals))
        late = send(late)
        if s < last - 1:
            early = send(early)
        else:
            inner, early = early[:rows_in], early[rows_in:]
            if rows_in:
                inner = send(inner)
            early = send(early)

    window = call(
        functools.partial(window_kernel, lead), mine,
        [(x, rows, lambda i, o: (0, o[last])) for x in tokens_of["out"][:2]], [], [],
        [jax.ShapeDtypeStruct((2 * tokens, lead), grads.dtype)], 0, "window",
    )[0]
    totals, window, slots_sib = lax.optimization_barrier((totals, window, slots_sib))
    seq_sib, len_sib = slots_sib
    totals, summed = sum_to(last, totals, summed)
    totals = step(mine, tokens_of, [late], pieces[last][:1], totals, last)
    if rows_in:
        totals, inner = lax.optimization_barrier((totals, inner))
        totals = step(mine, tokens_of, [inner], [(0, 0, rows_in, "in", 0)], totals, last)
        inn = totals["in"]
    else:
        inn = dot(acts, every)
        inn = jnp.concatenate([inn, jnp.zeros_like(inn)])
    got = across(inn)

    slots = lengths.shape[0]
    queries = columns // RANK
    numbers = [jnp.reshape(me, (1,)), seq_slot, lengths, seq_sib, len_sib]
    arrays = [window, early, totals["out"], inn, got]
    if chips <= 8 and slots <= PAD:
        tables = score_tables(numbers, arrays, slots, (chips * PAD, 128), 2)
        return exchange(tables, slots, queries)
    table = score_tables(numbers, arrays, slots, (slots * devices, queries), 1)[0]
    got = lax.all_to_all(table.reshape(devices, slots, queries), "dp", 0, 0, tiled=True)
    return jnp.sum(got, axis=0)


def solution(mesh):
    return jax.shard_map(
        shards,
        mesh=mesh,
        in_specs=(
            P(("groups", "dp"), None),
            P(("groups", "dp"), None),
            P(("groups", "dp"), None),
            P(("groups", "dp"), None),
            P(("groups", "dp")),
            P(("groups", "dp")),
        ),
        out_specs=P(("groups", "dp"), None),
        check_vma=False,
    )
```

```python
import functools
import math

import jax
import jax.numpy as jnp
import numpy as np
from jax import lax
from jax.experimental import pallas as pl
from jax.experimental.pallas import tpu as pltpu
from jax.sharding import PartitionSpec as P

RANK = 32
LEN = 80
F32 = jnp.float32
VMEM = 52 << 20


def ring_of(chips):
    cols = max([d for d in range(1, math.isqrt(chips) + 1) if chips % d == 0 and d % 2 == 0] or [1])
    rows = chips // cols
    if cols == 1 or rows % 2:
        return list(range(chips))
    walk = []
    for r in range(rows):
        line = range(1, cols) if r % 2 == 0 else range(cols - 1, 0, -1)
        walk += [r * cols + c for c in line]
    return walk + [r * cols for r in reversed(range(rows))]


def block_orders(chips):
    ring = ring_of(chips)
    order = np.zeros((2 * chips, chips), np.int32)
    for p, chip in enumerate(ring):
        for s in range(chips):
            order[2 * chip, s] = 2 * ring[(p - s) % chips]
            order[2 * chip + 1, s] = 2 * ring[(p + s) % chips] + 1
    return order


def ring_pairs(chips):
    ring = ring_of(chips)
    pairs = []
    for p, chip in enumerate(ring):
        pairs.append((2 * chip, 2 * ring[(p + 1) % chips]))
        pairs.append((2 * chip + 1, 2 * ring[(p - 1) % chips] + 1))
    return pairs


def dot(a, b):
    return jnp.dot(a, b, preferred_element_type=F32)


def call(kernel, order, windows, whole, scalars, out_shape, flops, name):
    in_specs = [pl.BlockSpec((x.shape[0], w), at) for x, w, at in windows]
    in_specs += [pl.BlockSpec(x.shape, lambda i, o: (0, 0)) for x in whole]
    in_specs += [pl.BlockSpec(memory_space=pltpu.SMEM) for _ in scalars]
    size = sum(2 * x.shape[0] * w for x, w, _ in windows)
    size += sum(x.size * x.dtype.itemsize for x in list(whole) + list(out_shape))
    return pl.pallas_call(
        kernel,
        grid_spec=pltpu.PrefetchScalarGridSpec(
            num_scalar_prefetch=1,
            grid=(1,),
            in_specs=in_specs,
            out_specs=[pl.BlockSpec(x.shape, lambda i, o: (0, 0)) for x in out_shape],
        ),
        out_shape=out_shape,
        cost_estimate=pl.CostEstimate(flops=flops, bytes_accessed=size, transcendentals=0),
        compiler_params=pltpu.CompilerParams(vmem_limit_bytes=VMEM),
        name=name,
    )(order, *[x for x, _, _ in windows], *whole, *scalars)


def step_kernel(pieces, kinds, count, summed, order_ref, *refs):
    windows = {kind: refs[2 * i:2 * i + 2] for i, kind in enumerate(kinds)}
    blocks, refs = refs[2 * len(kinds):2 * len(kinds) + count], refs[2 * len(kinds) + count:]
    tokens = windows[kinds[0]][0].shape[0]
    for i, kind in enumerate(kinds):
        for k in range(2):
            at = pl.ds(k * tokens, tokens)
            total = refs[i][at] if summed else 0.0
            for which, row, height, of, column in pieces:
                if of == kind:
                    window = windows[kind][k][:, column:column + height]
                    total += dot(window, blocks[which][row:row + height])
            refs[i - len(kinds)][at] = total


def step(order, tokens_of, blocks, pieces, totals, s):
    kinds = sorted({piece[3] for piece in pieces})
    windows = []
    for kind in kinds:
        own, sib, width = tokens_of[kind]
        windows += [(x, width, lambda i, o: (0, o[s])) for x in (own, sib)]
    tokens, columns = windows[0][0].shape[0], blocks[0].shape[1]
    summed = all(kind in totals for kind in kinds)
    shape = jax.ShapeDtypeStruct((2 * tokens, columns), F32)
    out = call(
        functools.partial(step_kernel, pieces, kinds, len(blocks), summed),
        order, windows, list(blocks) + ([totals[k] for k in kinds] if summed else []), [],
        [shape] * len(kinds), 4 * tokens * sum(p[2] for p in pieces) * columns, "step",
    )
    return {**totals, **dict(zip(kinds, out))}


def window_kernel(lead, order_ref, own_ref, sib_ref, out_ref):
    tokens = own_ref.shape[0]
    out_ref[:tokens] = own_ref[:, :lead]
    out_ref[tokens:] = sib_ref[:, :lead]


def score_kernel(seq_ref, len_ref, seq_sib, len_sib, window_ref, b_ref, out_ref, inn_ref, got_ref,
                 table_ref):
    columns = b_ref.shape[1]
    tokens = window_ref.shape[0] // 2
    queries = columns // RANK
    column = lax.broadcasted_iota(jnp.int32, (columns, queries), 0) // RANK
    query = lax.broadcasted_iota(jnp.int32, (columns, queries), 1)
    fold = (column == query).astype(F32)
    position = lax.broadcasted_iota(jnp.int32, (LEN, columns), 0)
    row = lax.broadcasted_iota(jnp.int32, table_ref.shape, 0)
    out = out_ref[...] + dot(window_ref[...], b_ref[...])
    sums, slots = [], []
    for k, (seq, lens) in enumerate(((seq_ref, len_ref), (seq_sib, len_sib))):
        mine, other = pl.ds(k * tokens, tokens), pl.ds((1 - k) * tokens, tokens)
        contrib = out[k * tokens:(k + 1) * tokens] * (inn_ref[mine] + got_ref[other])
        for i in range(tokens // LEN):
            kept = jnp.where(position < lens[i], contrib[i * LEN:(i + 1) * LEN], 0.0)
            sums.append(jnp.sum(kept, axis=0, keepdims=True))
            slots.append(seq[i])
    scores = jnp.dot(
        jnp.concatenate(sums), fold, precision=lax.Precision.HIGHEST, preferred_element_type=F32
    ) * (1.0 / math.sqrt(RANK * LEN))
    table = jnp.zeros(table_ref.shape, F32)
    for i, slot in enumerate(slots):
        table = jnp.where(row == slot, scores[i:i + 1], table)
    table_ref[...] = table


def score_table(numbers, arrays, rows, queries):
    smem, vmem = (pl.BlockSpec(memory_space=m) for m in (pltpu.SMEM, pltpu.VMEM))
    window, block = arrays[:2]
    size = sum(x.size * x.dtype.itemsize for x in arrays)
    return pl.pallas_call(
        score_kernel,
        in_specs=[smem] * len(numbers) + [vmem] * len(arrays),
        out_specs=vmem,
        out_shape=jax.ShapeDtypeStruct((rows, queries), F32),
        cost_estimate=pl.CostEstimate(
            flops=2 * window.size * block.shape[1], bytes_accessed=size, transcendentals=0
        ),
        compiler_params=pltpu.CompilerParams(vmem_limit_bytes=16 << 20),
        name="score",
    )(*numbers, *arrays)


def shards(acts, grads, out_factors, in_factors, seq_slot, lengths):
    devices = lax.axis_size("dp")
    chips = devices // 2
    me = lax.axis_index("dp")
    tokens = grads.shape[0]
    rows, columns = out_factors.shape
    rows_in = in_factors.shape[0]
    orders = jnp.asarray(block_orders(chips))
    mine = lax.dynamic_index_in_dim(orders, me, keepdims=False)
    pairs = ring_pairs(chips)
    swap = [(d, d ^ 1) for d in range(devices)]

    send = lambda x: lax.ppermute(x, "dp", pairs)
    across = lambda x: lax.ppermute(x, "dp", swap)

    every = None
    if rows_in % 128:
        every = lax.all_gather(in_factors, "dp", axis=0, tiled=True)
        rows_in = 0
    lead = (rows - rows_in) // 2
    tokens_of = {"out": (grads, across(grads), rows)}
    if rows_in:
        tokens_of["in"] = (acts, across(acts), rows_in)
    slots_sib = across(jnp.stack([seq_slot, lengths]))

    inside = [(1, 0, rows_in, "in", 0)] if rows_in else []
    held = [[out_factors] + [in_factors] * (rows_in > 0)]
    pieces = [[(0, 0, rows, "out", 0)] + inside]
    came = send(out_factors)
    late, early = came[lead:], came[:lead]
    if rows_in:
        turned = lax.ppermute(in_factors, "dp", [(j, i) for i, j in pairs])
        early = jnp.concatenate([send(in_factors), early])
        early, turned = lax.optimization_barrier((early, turned))
    totals, summed, last = {}, 0, chips - 1

    def sum_to(k, totals, summed):
        for j in range(summed, k):
            totals = step(mine, tokens_of, held[j], pieces[j], totals, j)
        return totals, max(k, summed)

    for s in range(1, chips):
        held.append([late, early])
        pieces.append([(0, 0, rows - lead, "out", lead), (1, rows_in, lead, "out", 0)] + inside)
        if s == last:
            break
        if s >= 4:
            totals, summed = sum_to(min(2 * s - 6, s), totals, summed)
            late, totals = lax.optimization_barrier((late, totals))
            early, totals = lax.optimization_barrier((early, totals))
        late = send(late)
        early = send(early if s < last - 1 else early[rows_in:])

    window = call(
        functools.partial(window_kernel, lead), mine,
        [(x, rows, lambda i, o: (0, o[last])) for x in tokens_of["out"][:2]], [], [],
        [jax.ShapeDtypeStruct((2 * tokens, lead), grads.dtype)], 0, "window",
    )[0]
    totals, window, slots_sib = lax.optimization_barrier((totals, window, slots_sib))
    seq_sib, len_sib = slots_sib
    totals, summed = sum_to(last, totals, summed)
    if rows_in:
        totals = step(mine, tokens_of, [turned], [(0, 0, rows_in, "in", 0)], totals, last)
        inn = totals["in"]
    else:
        inn = dot(acts, every)
        inn = jnp.concatenate([inn, jnp.zeros_like(inn)])
    got = across(inn)
    totals = step(mine, tokens_of, [late], pieces[last][:1], totals, last)

    slots = lengths.shape[0]
    queries = columns // RANK
    table = score_table(
        [seq_slot, lengths, seq_sib, len_sib], [window, early, totals["out"], inn, got],
        slots * devices, queries,
    )
    got = lax.all_to_all(table.reshape(devices, slots, queries), "dp", 0, 0, tiled=True)
    return jnp.sum(got, axis=0)


def solution(mesh):
    return jax.shard_map(
        shards,
        mesh=mesh,
        in_specs=(
            P(("groups", "dp"), None),
            P(("groups", "dp"), None),
            P(("groups", "dp"), None),
            P(("groups", "dp"), None),
            P(("groups", "dp")),
            P(("groups", "dp")),
        ),
        out_specs=P(("groups", "dp"), None),
        check_vma=False,
    )
```

```python
import functools
import math

import jax
import jax.numpy as jnp
import numpy as np
from jax import lax
from jax.experimental import pallas as pl
from jax.experimental.pallas import tpu as pltpu
from jax.sharding import PartitionSpec as P

RANK = 32
LEN = 80
F32 = jnp.float32
VMEM = 52 << 20


def ring_of(chips):
    cols = max([d for d in range(1, math.isqrt(chips) + 1) if chips % d == 0 and d % 2 == 0] or [1])
    rows = chips // cols
    if cols == 1 or rows % 2:
        return list(range(chips))
    walk = []
    for r in range(rows):
        line = range(1, cols) if r % 2 == 0 else range(cols - 1, 0, -1)
        walk += [r * cols + c for c in line]
    return walk + [r * cols for r in reversed(range(rows))]


def block_orders(chips):
    ring = ring_of(chips)
    order = np.zeros((2 * chips, chips), np.int32)
    for p, chip in enumerate(ring):
        for s in range(chips):
            order[2 * chip, s] = 2 * ring[(p - s) % chips]
            order[2 * chip + 1, s] = 2 * ring[(p + s) % chips] + 1
    return order


def ring_pairs(chips):
    ring = ring_of(chips)
    pairs = []
    for p, chip in enumerate(ring):
        pairs.append((2 * chip, 2 * ring[(p + 1) % chips]))
        pairs.append((2 * chip + 1, 2 * ring[(p - 1) % chips] + 1))
    return pairs


def dot(a, b):
    return jnp.dot(a, b, preferred_element_type=F32)


def call(kernel, order, windows, whole, scalars, out_shape, flops, name):
    in_specs = [pl.BlockSpec((x.shape[0], w), at) for x, w, at in windows]
    in_specs += [pl.BlockSpec(x.shape, lambda i, o: (0, 0)) for x in whole]
    in_specs += [pl.BlockSpec(memory_space=pltpu.SMEM) for _ in scalars]
    size = sum(2 * x.shape[0] * w for x, w, _ in windows)
    size += sum(x.size * x.dtype.itemsize for x in list(whole) + list(out_shape))
    return pl.pallas_call(
        kernel,
        grid_spec=pltpu.PrefetchScalarGridSpec(
            num_scalar_prefetch=1,
            grid=(1,),
            in_specs=in_specs,
            out_specs=[pl.BlockSpec(x.shape, lambda i, o: (0, 0)) for x in out_shape],
        ),
        out_shape=out_shape,
        cost_estimate=pl.CostEstimate(flops=flops, bytes_accessed=size, transcendentals=0),
        compiler_params=pltpu.CompilerParams(vmem_limit_bytes=VMEM),
        name=name,
    )(order, *[x for x, _, _ in windows], *whole, *scalars)


def step_kernel(pieces, kinds, count, summed, order_ref, *refs):
    windows = {kind: refs[2 * i:2 * i + 2] for i, kind in enumerate(kinds)}
    blocks, refs = refs[2 * len(kinds):2 * len(kinds) + count], refs[2 * len(kinds) + count:]
    tokens = windows[kinds[0]][0].shape[0]
    for i, kind in enumerate(kinds):
        for k in range(2):
            at = pl.ds(k * tokens, tokens)
            total = refs[i][at] if summed else 0.0
            for which, row, height, of, column in pieces:
                if of == kind:
                    window = windows[kind][k][:, column:column + height]
                    total += dot(window, blocks[which][row:row + height])
            refs[i - len(kinds)][at] = total


def step(order, tokens_of, blocks, pieces, totals, s):
    kinds = sorted({piece[3] for piece in pieces})
    windows = []
    for kind in kinds:
        own, sib, width = tokens_of[kind]
        windows += [(x, width, lambda i, o: (0, o[s])) for x in (own, sib)]
    tokens, columns = windows[0][0].shape[0], blocks[0].shape[1]
    summed = all(kind in totals for kind in kinds)
    shape = jax.ShapeDtypeStruct((2 * tokens, columns), F32)
    out = call(
        functools.partial(step_kernel, pieces, kinds, len(blocks), summed),
        order, windows, list(blocks) + ([totals[k] for k in kinds] if summed else []), [],
        [shape] * len(kinds), 4 * tokens * sum(p[2] for p in pieces) * columns, "step",
    )
    return {**totals, **dict(zip(kinds, out))}


def window_kernel(lead, order_ref, own_ref, sib_ref, out_ref):
    tokens = own_ref.shape[0]
    out_ref[:tokens] = own_ref[:, :lead]
    out_ref[tokens:] = sib_ref[:, :lead]


def score_kernel(seq_ref, len_ref, seq_sib, len_sib, window_ref, b_ref, out_ref, inn_ref, got_ref,
                 table_ref):
    columns = b_ref.shape[1]
    tokens = window_ref.shape[0] // 2
    queries = columns // RANK
    column = lax.broadcasted_iota(jnp.int32, (columns, queries), 0) // RANK
    query = lax.broadcasted_iota(jnp.int32, (columns, queries), 1)
    fold = (column == query).astype(F32)
    position = lax.broadcasted_iota(jnp.int32, (LEN, columns), 0)
    row = lax.broadcasted_iota(jnp.int32, table_ref.shape, 0)
    out = out_ref[...] + dot(window_ref[...], b_ref[...])
    sums, slots = [], []
    for k, (seq, lens) in enumerate(((seq_ref, len_ref), (seq_sib, len_sib))):
        mine, other = pl.ds(k * tokens, tokens), pl.ds((1 - k) * tokens, tokens)
        contrib = out[k * tokens:(k + 1) * tokens] * (inn_ref[mine] + got_ref[other])
        for i in range(tokens // LEN):
            kept = jnp.where(position < lens[i], contrib[i * LEN:(i + 1) * LEN], 0.0)
            sums.append(jnp.sum(kept, axis=0, keepdims=True))
            slots.append(seq[i])
    scores = jnp.dot(
        jnp.concatenate(sums), fold, precision=lax.Precision.HIGHEST, preferred_element_type=F32
    ) * (1.0 / math.sqrt(RANK * LEN))
    table = jnp.zeros(table_ref.shape, F32)
    for i, slot in enumerate(slots):
        table = jnp.where(row == slot, scores[i:i + 1], table)
    table_ref[...] = table


def score_table(numbers, arrays, rows, queries):
    smem, vmem = (pl.BlockSpec(memory_space=m) for m in (pltpu.SMEM, pltpu.VMEM))
    window, block = arrays[:2]
    size = sum(x.size * x.dtype.itemsize for x in arrays)
    return pl.pallas_call(
        score_kernel,
        in_specs=[smem] * len(numbers) + [vmem] * len(arrays),
        out_specs=vmem,
        out_shape=jax.ShapeDtypeStruct((rows, queries), F32),
        cost_estimate=pl.CostEstimate(
            flops=2 * window.size * block.shape[1], bytes_accessed=size, transcendentals=0
        ),
        compiler_params=pltpu.CompilerParams(vmem_limit_bytes=16 << 20),
        name="score",
    )(*numbers, *arrays)


def shards(acts, grads, out_factors, in_factors, seq_slot, lengths):
    devices = lax.axis_size("dp")
    chips = devices // 2
    me = lax.axis_index("dp")
    tokens = grads.shape[0]
    rows, columns = out_factors.shape
    rows_in = in_factors.shape[0]
    orders = jnp.asarray(block_orders(chips))
    mine = lax.dynamic_index_in_dim(orders, me, keepdims=False)
    pairs = ring_pairs(chips)
    swap = [(d, d ^ 1) for d in range(devices)]

    send = lambda x: lax.ppermute(x, "dp", pairs)
    across = lambda x: lax.ppermute(x, "dp", swap)

    every = None
    if rows_in % 128:
        every = lax.all_gather(in_factors, "dp", axis=0, tiled=True)
        rows_in = 0
    lead = (rows - rows_in) // 2
    tokens_of = {"out": (grads, across(grads), rows)}
    if rows_in:
        tokens_of["in"] = (acts, across(acts), rows_in)
    slots_sib = across(jnp.stack([seq_slot, lengths]))

    inside = [(1, 0, rows_in, "in", 0)] if rows_in else []
    held = [[out_factors] + [in_factors] * (rows_in > 0)]
    pieces = [[(0, 0, rows, "out", 0)] + inside]
    came = send(out_factors)
    late, early = came[lead:], came[:lead]
    if rows_in:
        came, turned = lax.optimization_barrier((came, in_factors))
        turned = lax.ppermute(turned, "dp", [(j, i) for i, j in pairs])
        late, early = came[lead:], came[:lead]
        early = jnp.concatenate([send(in_factors), early])
        early, turned = lax.optimization_barrier((early, turned))
    totals, summed, last = {}, 0, chips - 1

    def sum_to(k, totals, summed):
        for j in range(summed, k):
            totals = step(mine, tokens_of, held[j], pieces[j], totals, j)
        return totals, max(k, summed)

    for s in range(1, chips):
        held.append([late, early])
        pieces.append([(0, 0, rows - lead, "out", lead), (1, rows_in, lead, "out", 0)] + inside)
        if s == last:
            break
        if s >= 4:
            totals, summed = sum_to(min(2 * s - 6, s), totals, summed)
            late, totals = lax.optimization_barrier((late, totals))
            early, totals = lax.optimization_barrier((early, totals))
        late = send(late)
        early = send(early if s < last - 1 else early[rows_in:])

    window = call(
        functools.partial(window_kernel, lead), mine,
        [(x, rows, lambda i, o: (0, o[last])) for x in tokens_of["out"][:2]], [], [],
        [jax.ShapeDtypeStruct((2 * tokens, lead), grads.dtype)], 0, "window",
    )[0]
    totals, window, slots_sib = lax.optimization_barrier((totals, window, slots_sib))
    seq_sib, len_sib = slots_sib
    totals, summed = sum_to(last, totals, summed)
    if rows_in:
        totals = step(mine, tokens_of, [turned], [(0, 0, rows_in, "in", 0)], totals, last)
        inn = totals["in"]
    else:
        inn = dot(acts, every)
        inn = jnp.concatenate([inn, jnp.zeros_like(inn)])
    got = across(inn)
    totals = step(mine, tokens_of, [late], pieces[last][:1], totals, last)

    slots = lengths.shape[0]
    queries = columns // RANK
    table = score_table(
        [seq_slot, lengths, seq_sib, len_sib], [window, early, totals["out"], inn, got],
        slots * devices, queries,
    )
    got = lax.all_to_all(table.reshape(devices, slots, queries), "dp", 0, 0, tiled=True)
    return jnp.sum(got, axis=0)


def solution(mesh):
    return jax.shard_map(
        shards,
        mesh=mesh,
        in_specs=(
            P(("groups", "dp"), None),
            P(("groups", "dp"), None),
            P(("groups", "dp"), None),
            P(("groups", "dp"), None),
            P(("groups", "dp")),
            P(("groups", "dp")),
        ),
        out_specs=P(("groups", "dp"), None),
        check_vma=False,
    )
```

```python
import functools
import math

import jax
import jax.numpy as jnp
import numpy as np
from jax import lax
from jax.experimental import pallas as pl
from jax.experimental.pallas import tpu as pltpu
from jax.sharding import PartitionSpec as P

RANK = 32
LEN = 80
F32 = jnp.float32
VMEM = 52 << 20


def ring_of(chips):
    cols = max([d for d in range(1, math.isqrt(chips) + 1) if chips % d == 0 and d % 2 == 0] or [1])
    rows = chips // cols
    if cols == 1 or rows % 2:
        return list(range(chips))
    walk = []
    for r in range(rows):
        line = range(1, cols) if r % 2 == 0 else range(cols - 1, 0, -1)
        walk += [r * cols + c for c in line]
    return walk + [r * cols for r in reversed(range(rows))]


def block_orders(chips):
    ring = ring_of(chips)
    order = np.zeros((2 * chips, chips), np.int32)
    for p, chip in enumerate(ring):
        for s in range(chips):
            order[2 * chip, s] = 2 * ring[(p - s) % chips]
            order[2 * chip + 1, s] = 2 * ring[(p + s) % chips] + 1
    return order


def ring_pairs(chips):
    ring = ring_of(chips)
    pairs = []
    for p, chip in enumerate(ring):
        pairs.append((2 * chip, 2 * ring[(p + 1) % chips]))
        pairs.append((2 * chip + 1, 2 * ring[(p - 1) % chips] + 1))
    return pairs


def dot(a, b):
    return jnp.dot(a, b, preferred_element_type=F32)


def call(kernel, order, windows, whole, scalars, out_shape, flops, name):
    in_specs = [pl.BlockSpec((x.shape[0], w), at) for x, w, at in windows]
    in_specs += [pl.BlockSpec(x.shape, lambda i, o: (0, 0)) for x in whole]
    in_specs += [pl.BlockSpec(memory_space=pltpu.SMEM) for _ in scalars]
    size = sum(2 * x.shape[0] * w for x, w, _ in windows)
    size += sum(x.size * x.dtype.itemsize for x in list(whole) + list(out_shape))
    return pl.pallas_call(
        kernel,
        grid_spec=pltpu.PrefetchScalarGridSpec(
            num_scalar_prefetch=1,
            grid=(1,),
            in_specs=in_specs,
            out_specs=[pl.BlockSpec(x.shape, lambda i, o: (0, 0)) for x in out_shape],
        ),
        out_shape=out_shape,
        cost_estimate=pl.CostEstimate(flops=flops, bytes_accessed=size, transcendentals=0),
        compiler_params=pltpu.CompilerParams(vmem_limit_bytes=VMEM),
        name=name,
    )(order, *[x for x, _, _ in windows], *whole, *scalars)


def step_kernel(pieces, kinds, count, summed, order_ref, *refs):
    windows = {kind: refs[2 * i:2 * i + 2] for i, kind in enumerate(kinds)}
    blocks, refs = refs[2 * len(kinds):2 * len(kinds) + count], refs[2 * len(kinds) + count:]
    tokens = windows[kinds[0]][0].shape[0]
    for i, kind in enumerate(kinds):
        for k in range(2):
            at = pl.ds(k * tokens, tokens)
            total = refs[i][at] if summed else 0.0
            for which, row, height, of, column in pieces:
                if of == kind:
                    window = windows[kind][k][:, column:column + height]
                    total += dot(window, blocks[which][row:row + height])
            refs[i - len(kinds)][at] = total


def step(order, tokens_of, blocks, pieces, totals, s):
    kinds = sorted({piece[3] for piece in pieces})
    windows = []
    for kind in kinds:
        own, sib, width = tokens_of[kind]
        windows += [(x, width, lambda i, o: (0, o[s])) for x in (own, sib)]
    tokens, columns = windows[0][0].shape[0], blocks[0].shape[1]
    summed = all(kind in totals for kind in kinds)
    shape = jax.ShapeDtypeStruct((2 * tokens, columns), F32)
    out = call(
        functools.partial(step_kernel, pieces, kinds, len(blocks), summed),
        order, windows, list(blocks) + ([totals[k] for k in kinds] if summed else []), [],
        [shape] * len(kinds), 4 * tokens * sum(p[2] for p in pieces) * columns, "step",
    )
    return {**totals, **dict(zip(kinds, out))}


def window_kernel(lead, order_ref, own_ref, sib_ref, out_ref):
    tokens = own_ref.shape[0]
    out_ref[:tokens] = own_ref[:, :lead]
    out_ref[tokens:] = sib_ref[:, :lead]


def score_kernel(seq_ref, len_ref, seq_sib, len_sib, window_ref, b_ref, out_ref, inn_ref, got_ref,
                 table_ref):
    columns = b_ref.shape[1]
    tokens = window_ref.shape[0] // 2
    queries = columns // RANK
    column = lax.broadcasted_iota(jnp.int32, (columns, queries), 0) // RANK
    query = lax.broadcasted_iota(jnp.int32, (columns, queries), 1)
    fold = (column == query).astype(F32)
    position = lax.broadcasted_iota(jnp.int32, (LEN, columns), 0)
    row = lax.broadcasted_iota(jnp.int32, table_ref.shape, 0)
    out = out_ref[...] + dot(window_ref[...], b_ref[...])
    sums, slots = [], []
    for k, (seq, lens) in enumerate(((seq_ref, len_ref), (seq_sib, len_sib))):
        mine, other = pl.ds(k * tokens, tokens), pl.ds((1 - k) * tokens, tokens)
        contrib = out[k * tokens:(k + 1) * tokens] * (inn_ref[mine] + got_ref[other])
        for i in range(tokens // LEN):
            kept = jnp.where(position < lens[i], contrib[i * LEN:(i + 1) * LEN], 0.0)
            sums.append(jnp.sum(kept, axis=0, keepdims=True))
            slots.append(seq[i])
    scores = jnp.dot(
        jnp.concatenate(sums), fold, precision=lax.Precision.HIGHEST, preferred_element_type=F32
    ) * (1.0 / math.sqrt(RANK * LEN))
    table = jnp.zeros(table_ref.shape, F32)
    for i, slot in enumerate(slots):
        table = jnp.where(row == slot, scores[i:i + 1], table)
    table_ref[...] = table


def score_table(numbers, arrays, rows, queries):
    smem, vmem = (pl.BlockSpec(memory_space=m) for m in (pltpu.SMEM, pltpu.VMEM))
    window, block = arrays[:2]
    size = sum(x.size * x.dtype.itemsize for x in arrays)
    return pl.pallas_call(
        score_kernel,
        in_specs=[smem] * len(numbers) + [vmem] * len(arrays),
        out_specs=vmem,
        out_shape=jax.ShapeDtypeStruct((rows, queries), F32),
        cost_estimate=pl.CostEstimate(
            flops=2 * window.size * block.shape[1], bytes_accessed=size, transcendentals=0
        ),
        compiler_params=pltpu.CompilerParams(vmem_limit_bytes=16 << 20),
        name="score",
    )(*numbers, *arrays)


def ring_shards(acts, grads, out_factors, in_factors, seq_slot, lengths):
    devices = lax.axis_size("dp")
    chips = devices // 2
    me = lax.axis_index("dp")
    tokens = grads.shape[0]
    rows, columns = out_factors.shape
    rows_in = in_factors.shape[0]
    orders = jnp.asarray(block_orders(chips))
    mine = lax.dynamic_index_in_dim(orders, me, keepdims=False)
    pairs = ring_pairs(chips)
    swap = [(d, d ^ 1) for d in range(devices)]

    send = lambda x: lax.ppermute(x, "dp", pairs)
    across = lambda x: lax.ppermute(x, "dp", swap)

    every = None
    if rows_in % 128:
        every = lax.all_gather(in_factors, "dp", axis=0, tiled=True)
        rows_in = 0
    lead = (rows - rows_in) // 2
    tokens_of = {"out": (grads, across(grads), rows)}
    if rows_in:
        tokens_of["in"] = (acts, across(acts), rows_in)
    slots_sib = across(jnp.stack([seq_slot, lengths]))

    inside = [(1, 0, rows_in, "in", 0)] if rows_in else []
    held = [[out_factors] + [in_factors] * (rows_in > 0)]
    pieces = [[(0, 0, rows, "out", 0)] + inside]
    came = send(out_factors)
    late, early = came[lead:], came[:lead]
    if rows_in:
        came, turned = lax.optimization_barrier((came, in_factors))
        turned = lax.ppermute(turned, "dp", [(j, i) for i, j in pairs])
        late, early = came[lead:], came[:lead]
        early = jnp.concatenate([send(in_factors), early])
        early, turned = lax.optimization_barrier((early, turned))
    totals, summed, last = {}, 0, chips - 1

    def sum_to(k, totals, summed):
        for j in range(summed, k):
            totals = step(mine, tokens_of, held[j], pieces[j], totals, j)
        return totals, max(k, summed)

    for s in range(1, chips):
        held.append([late, early])
        pieces.append([(0, 0, rows - lead, "out", lead), (1, rows_in, lead, "out", 0)] + inside)
        if s == last:
            break
        if s >= 4:
            totals, summed = sum_to(min(2 * s - 6, s), totals, summed)
            late, totals = lax.optimization_barrier((late, totals))
            early, totals = lax.optimization_barrier((early, totals))
        late = send(late)
        early = send(early if s < last - 1 else early[rows_in:])

    window = call(
        functools.partial(window_kernel, lead), mine,
        [(x, rows, lambda i, o: (0, o[last])) for x in tokens_of["out"][:2]], [], [],
        [jax.ShapeDtypeStruct((2 * tokens, lead), grads.dtype)], 0, "window",
    )[0]
    totals, window, slots_sib = lax.optimization_barrier((totals, window, slots_sib))
    seq_sib, len_sib = slots_sib
    totals, summed = sum_to(last, totals, summed)
    if rows_in:
        totals = step(mine, tokens_of, [turned], [(0, 0, rows_in, "in", 0)], totals, last)
        inn = totals["in"]
    else:
        inn = dot(acts, every)
        inn = jnp.concatenate([inn, jnp.zeros_like(inn)])
    got = across(inn)
    totals = step(mine, tokens_of, [late], pieces[last][:1], totals, last)

    slots = lengths.shape[0]
    queries = columns // RANK
    table = score_table(
        [seq_slot, lengths, seq_sib, len_sib], [window, early, totals["out"], inn, got],
        slots * devices, queries,
    )
    got = lax.all_to_all(table.reshape(devices, slots, queries), "dp", 0, 0, tiled=True)
    return jnp.sum(got, axis=0)


EXTRA = 8
MIDDLE = {0: 1, 7: 6, 3: 2, 4: 5}
INTERIOR = {1: 6, 6: 1, 2: 5, 5: 2}
LANE = {0: 0, 7: 1, 3: 1, 4: 0}


class Links:
    def __init__(self):
        ring = ring_of(8)
        at = lambda place, core: 2 * ring[place] + core
        self.ring = ring_pairs(8)
        self.back = [(j, i) for i, j in self.ring]
        self.inward = [(at(q, c), at(m, c)) for q, m in MIDDLE.items() for c in (0, 1)]
        out = [(at(q, LANE[q]), at(m, LANE[q])) for q, m in MIDDLE.items()]
        self.relieved = [pair for pair in self.ring if pair not in out]
        self.near = [(at(INTERIOR[m], LANE[q]), at(m, LANE[q])) for q, m in MIDDLE.items()]
        self.far = [(at(INTERIOR[m], 1 - LANE[q]), at(m, 1 - LANE[q])) for q, m in MIDDLE.items()]
        flag = np.zeros((16, 1), np.int32)
        flag[[j for _, j in self.near]] = 1
        self.table = np.concatenate([block_orders(8), flag], axis=1)
        blocks = block_orders(8)
        for i, j in self.inward:
            at_hand = blocks[j, 0] if flag[j] else blocks[dict((y, x) for x, y in self.far)[j], 1]
            assert blocks[i, 7] == at_hand
        for i, j in self.near:
            assert all(blocks[i, s - 2] == blocks[j, s + 1] for s in (2, 3, 4, 5, 6))
        for i, j in self.far:
            assert blocks[i, 2] == blocks[j, 7]


FLAG = 8


def turned_kernel(count, order_ref, *refs):
    windows, blocks = refs[:2 * count], refs[2 * count:3 * count]
    total_ref, seq_ref, len_ref, out_ref = refs[3 * count:]
    tokens = windows[0].shape[0]
    for k in range(2):
        at = pl.ds(k * tokens, tokens)
        total = total_ref[at]
        for w in range(count):
            total += dot(windows[2 * w + k][...], blocks[w][...])
        out_ref[at] = total
    held = seq_ref.shape[0]
    lane = lax.broadcasted_iota(jnp.int32, (EXTRA, out_ref.shape[1]), 1)
    numbers = jnp.zeros(lane.shape, F32)
    for i in range(held):
        numbers = jnp.where(lane == i, seq_ref[i].astype(F32), numbers)
        numbers = jnp.where(lane == held + i, len_ref[i].astype(F32), numbers)
    out_ref[2 * tokens:] = numbers


def masked_kernel(order_ref, own_ref, got_ref, out_ref):
    tokens = (own_ref.shape[0] - EXTRA) // 2
    columns = own_ref.shape[1]
    held = tokens // LEN
    position = lax.broadcasted_iota(jnp.int32, (LEN, columns), 0).astype(F32)
    for k, (mine, other) in enumerate(((own_ref, got_ref), (got_ref, own_ref))):
        for i in range(held):
            at, across = pl.ds(i * LEN, LEN), pl.ds(tokens + i * LEN, LEN)
            length = mine[2 * tokens:2 * tokens + 1, held + i:held + i + 1]
            out_ref[pl.ds(k * tokens + i * LEN, LEN)] = jnp.where(
                position < length, mine[at] + other[across], 0.0
            )
    lane = lax.broadcasted_iota(jnp.int32, (EXTRA, columns), 1)
    numbers = jnp.zeros(lane.shape, F32)
    for k, ref in enumerate((own_ref, got_ref)):
        for i in range(held):
            slot = ref[2 * tokens:2 * tokens + 1, i:i + 1]
            numbers = jnp.where(lane == k * held + i, slot, numbers)
    out_ref[2 * tokens:] = numbers


def cut_kernel(order_ref, own_ref, sib_ref, *outs):
    tokens = own_ref.shape[0]
    start = 0
    for out_ref in outs:
        width = out_ref.shape[1]
        out_ref[:tokens] = own_ref[:, start:start + width]
        out_ref[tokens:] = sib_ref[:, start:start + width]
        start += width


def job_kernel(order_ref, first_ref, second_ref, own_ref, far_ref, out_ref):
    rows, half = far_ref.shape[0], first_ref.shape[1]
    own = jnp.full(far_ref.shape, order_ref[FLAG], jnp.int32) == 1
    block = jnp.where(own, own_ref[:rows], far_ref[...])
    out_ref[...] = dot(first_ref[...], block[:half]) + dot(second_ref[...], block[half:])


def finish_kernel(window_ref, block_ref, total_ref, inn_ref, job_ref, job_inn_ref, table_ref):
    height, columns = total_ref.shape
    queries = columns // RANK
    column = lax.broadcasted_iota(jnp.int32, (columns, queries), 0) // RANK
    query = lax.broadcasted_iota(jnp.int32, (columns, queries), 1)
    fold = (column == query).astype(F32)
    row = lax.broadcasted_iota(jnp.int32, table_ref.shape, 0).astype(F32)
    sums, slots = [], []
    out = total_ref[...] + dot(window_ref[...], block_ref[...])
    for got, inn in ((out, inn_ref), (job_ref[...], job_inn_ref)):
        contrib = got * inn[:height]
        for i in range(height // LEN):
            sums.append(jnp.sum(contrib[i * LEN:(i + 1) * LEN], axis=0, keepdims=True))
            slots.append(inn[height:height + 1, i:i + 1])
    scores = jnp.dot(
        jnp.concatenate(sums), fold, precision=lax.Precision.HIGHEST, preferred_element_type=F32
    ) * (1.0 / math.sqrt(RANK * LEN))
    table = jnp.zeros(table_ref.shape, F32)
    for i, slot in enumerate(slots):
        table += jnp.where(row == slot, scores[i:i + 1], 0.0)
    table_ref[...] = table


def ring8_shards(acts, grads, out_factors, in_factors, seq_slot, lengths):
    devices = lax.axis_size("dp")
    links = Links()
    order = lax.dynamic_index_in_dim(
        jnp.asarray(links.table), lax.axis_index("dp"), keepdims=False
    )
    tokens = grads.shape[0]
    rows, columns = out_factors.shape
    ins = in_factors.shape[0]
    lead = rows // 2
    send = lambda x, pairs=links.ring: lax.ppermute(x, "dp", pairs)
    swap = lambda x: send(x, [(d, d ^ 1) for d in range(devices)])
    tie = lax.optimization_barrier

    tokens_of = {"out": (grads, swap(grads), rows), "in": (acts, swap(acts), ins)}
    g1, g2, window = call(
        cut_kernel, order, [(x, rows, lambda i, o: (0, o[7])) for x in tokens_of["out"][:2]],
        [], [],
        [jax.ShapeDtypeStruct((2 * tokens, w), grads.dtype) for w in (lead // 2, lead // 2, rows - lead)],
        0, "cut",
    )

    came = send(out_factors)
    late, early = [None, came[lead:]], [out_factors[:lead], came[:lead]]
    ahead, back = [None, send(in_factors)], [None, send(in_factors, links.back)]

    pieces = [[(0, 0, rows, "out", 0), (1, 0, ins, "in", 0)]]
    pieces += [
        [(0, 0, rows - lead, "out", lead), (1, 0, lead, "out", 0), (2, 0, ins, "in", 0)]
    ] * 4
    pieces += [[(0, 0, rows - lead, "out", lead), (1, 0, lead, "out", 0)]] * 2
    totals = {}

    def add(*stages):
        nonlocal totals
        for k in stages:
            blocks = [late[k], early[k]] + ahead[k:k + 1] if k else [out_factors, in_factors]
            totals = step(order, tokens_of, blocks, pieces[k], totals, k)

    def hold(k, *others):
        nonlocal totals
        late[k], totals = tie((late[k], totals))
        early[k], totals, others = tie((early[k], totals, others))
        return others

    def hop(k):
        late.append(send(late[k]))
        if k == 1:
            early.append(send(early[k]))
        else:
            early.append(send(early[k], links.relieved) + send(early[k - 2], links.near))
        if k <= 3:
            ahead.append(send(ahead[k]))
        if k <= 2:
            back.append(send(back[k], links.back))

    hop(1)
    far = send(early[1], links.far)
    hop(2)
    missing = send(early[2], links.far)

    add(0)
    g1, g2, ahead[2], back[2] = hold(3, g1, g2, ahead[2], back[2])
    hop(3)
    g1 = send(g1, links.inward)

    add(1, 2)
    g1, far, ahead[3], back[3] = hold(4, g1, far, ahead[3], back[3])
    hop(4)
    g2 = send(g2, links.inward)

    add(3, 4)
    inn = call(
        functools.partial(turned_kernel, 3), order,
        [
            (x, ins, functools.partial(lambda i, o, k: (0, o[k]), k=8 - k))
            for k in (1, 2, 3) for x in tokens_of["in"][:2]
        ],
        back[1:] + [totals["in"]], [seq_slot, lengths],
        [jax.ShapeDtypeStruct((2 * tokens + EXTRA, columns), F32)],
        12 * tokens * ins * columns, "turned",
    )[0]
    g2, inn, missing = hold(5, g2, inn, missing)
    hop(5)
    near = send(early[4], links.near)
    inn = call(
        masked_kernel, order, [], [inn, swap(inn)], [],
        [jax.ShapeDtypeStruct(inn.shape, F32)], 0, "masked",
    )[0]

    job = call(
        job_kernel, order, [], [g1, g2, out_factors, far], [],
        [jax.ShapeDtypeStruct((2 * tokens, columns), F32)],
        4 * tokens * lead * columns, "job",
    )[0]
    add(5)
    late[6], totals, inn, job, window = tie((late[6], totals, inn, job, window))
    last = send(late[6])
    job_inn = send(inn, links.inward)
    totals = step(
        order, tokens_of, [missing + near], [(0, 0, lead, "out", 0)], totals, 7
    )
    add(6)

    slots = lengths.shape[0]
    queries = columns // RANK
    arrays = [window, last, totals["out"], inn, job, job_inn]
    table = pl.pallas_call(
        finish_kernel,
        in_specs=[pl.BlockSpec(memory_space=pltpu.VMEM)] * len(arrays),
        out_specs=pl.BlockSpec(memory_space=pltpu.VMEM),
        out_shape=jax.ShapeDtypeStruct((slots * devices, queries), F32),
        cost_estimate=pl.CostEstimate(
            flops=2 * window.size * columns, bytes_accessed=8 << 20, transcendentals=0
        ),
        compiler_params=pltpu.CompilerParams(vmem_limit_bytes=16 << 20),
        name="finish",
    )(*arrays)
    got = lax.all_to_all(table.reshape(devices, slots, queries), "dp", 0, 0, tiled=True)
    return jnp.sum(got, axis=0)


def shards(acts, grads, out_factors, in_factors, seq_slot, lengths):
    small = lax.axis_size("dp") == 16 and in_factors.shape[0] % 128 == 0
    run = ring8_shards if small else ring_shards
    return run(acts, grads, out_factors, in_factors, seq_slot, lengths)


def solution(mesh):
    return jax.shard_map(
        shards,
        mesh=mesh,
        in_specs=(
            P(("groups", "dp"), None),
            P(("groups", "dp"), None),
            P(("groups", "dp"), None),
            P(("groups", "dp"), None),
            P(("groups", "dp")),
            P(("groups", "dp")),
        ),
        out_specs=P(("groups", "dp"), None),
        check_vma=False,
    )
```

```python
import functools
import math

import jax
import jax.numpy as jnp
import numpy as np
from jax import lax
from jax.experimental import pallas as pl
from jax.experimental.pallas import tpu as pltpu
from jax.sharding import PartitionSpec as P

RANK = 32
LEN = 80
F32 = jnp.float32
VMEM = 52 << 20


def ring_of(chips):
    cols = max([d for d in range(1, math.isqrt(chips) + 1) if chips % d == 0 and d % 2 == 0] or [1])
    rows = chips // cols
    if cols == 1 or rows % 2:
        return list(range(chips))
    walk = []
    for r in range(rows):
        line = range(1, cols) if r % 2 == 0 else range(cols - 1, 0, -1)
        walk += [r * cols + c for c in line]
    return walk + [r * cols for r in reversed(range(rows))]


def block_orders(chips):
    ring = ring_of(chips)
    order = np.zeros((2 * chips, chips), np.int32)
    for p, chip in enumerate(ring):
        for s in range(chips):
            order[2 * chip, s] = 2 * ring[(p - s) % chips]
            order[2 * chip + 1, s] = 2 * ring[(p + s) % chips] + 1
    return order


def ring_pairs(chips):
    ring = ring_of(chips)
    pairs = []
    for p, chip in enumerate(ring):
        pairs.append((2 * chip, 2 * ring[(p + 1) % chips]))
        pairs.append((2 * chip + 1, 2 * ring[(p - 1) % chips] + 1))
    return pairs


def dot(a, b):
    return jnp.dot(a, b, preferred_element_type=F32)


def call(kernel, order, windows, whole, scalars, out_shape, flops, name):
    in_specs = [pl.BlockSpec((x.shape[0], w), at) for x, w, at in windows]
    in_specs += [pl.BlockSpec(x.shape, lambda i, o: (0, 0)) for x in whole]
    in_specs += [pl.BlockSpec(memory_space=pltpu.SMEM) for _ in scalars]
    size = sum(2 * x.shape[0] * w for x, w, _ in windows)
    size += sum(x.size * x.dtype.itemsize for x in list(whole) + list(out_shape))
    return pl.pallas_call(
        kernel,
        grid_spec=pltpu.PrefetchScalarGridSpec(
            num_scalar_prefetch=1,
            grid=(1,),
            in_specs=in_specs,
            out_specs=[pl.BlockSpec(x.shape, lambda i, o: (0, 0)) for x in out_shape],
        ),
        out_shape=out_shape,
        cost_estimate=pl.CostEstimate(flops=flops, bytes_accessed=size, transcendentals=0),
        compiler_params=pltpu.CompilerParams(vmem_limit_bytes=VMEM),
        name=name,
    )(order, *[x for x, _, _ in windows], *whole, *scalars)


def step_kernel(pieces, kinds, count, summed, order_ref, *refs):
    windows = {kind: refs[2 * i:2 * i + 2] for i, kind in enumerate(kinds)}
    blocks, refs = refs[2 * len(kinds):2 * len(kinds) + count], refs[2 * len(kinds) + count:]
    tokens = windows[kinds[0]][0].shape[0]
    for i, kind in enumerate(kinds):
        for k in range(2):
            at = pl.ds(k * tokens, tokens)
            total = refs[i][at] if summed else 0.0
            for which, row, height, of, column in pieces:
                if of == kind:
                    window = windows[kind][k][:, column:column + height]
                    total += dot(window, blocks[which][row:row + height])
            refs[i - len(kinds)][at] = total


def step(order, tokens_of, blocks, pieces, totals, s):
    kinds = sorted({piece[3] for piece in pieces})
    windows = []
    for kind in kinds:
        own, sib, width = tokens_of[kind]
        windows += [(x, width, lambda i, o: (0, o[s])) for x in (own, sib)]
    tokens, columns = windows[0][0].shape[0], blocks[0].shape[1]
    summed = all(kind in totals for kind in kinds)
    shape = jax.ShapeDtypeStruct((2 * tokens, columns), F32)
    out = call(
        functools.partial(step_kernel, pieces, kinds, len(blocks), summed),
        order, windows, list(blocks) + ([totals[k] for k in kinds] if summed else []), [],
        [shape] * len(kinds), 4 * tokens * sum(p[2] for p in pieces) * columns, "step",
    )
    return {**totals, **dict(zip(kinds, out))}


def window_kernel(lead, order_ref, own_ref, sib_ref, out_ref):
    tokens = own_ref.shape[0]
    out_ref[:tokens] = own_ref[:, :lead]
    out_ref[tokens:] = sib_ref[:, :lead]


EXTRA = 8


def turned_kernel(count, order_ref, *refs):
    windows, blocks = refs[:2 * count], refs[2 * count:3 * count]
    total_ref, seq_ref, len_ref, out_ref = refs[3 * count:]
    tokens = windows[0].shape[0]
    for k in range(2):
        at = pl.ds(k * tokens, tokens)
        total = total_ref[at]
        for w in range(count):
            total += dot(windows[2 * w + k][...], blocks[w][...])
        out_ref[at] = total
    held = seq_ref.shape[0]
    lane = lax.broadcasted_iota(jnp.int32, (EXTRA, out_ref.shape[1]), 1)
    numbers = jnp.zeros(lane.shape, F32)
    for i in range(held):
        numbers = jnp.where(lane == i, seq_ref[i].astype(F32), numbers)
        numbers = jnp.where(lane == held + i, len_ref[i].astype(F32), numbers)
    out_ref[2 * tokens:] = numbers


def masked_kernel(order_ref, own_ref, got_ref, out_ref):
    tokens = (own_ref.shape[0] - EXTRA) // 2
    columns = own_ref.shape[1]
    held = tokens // LEN
    position = lax.broadcasted_iota(jnp.int32, (LEN, columns), 0).astype(F32)
    for k, (mine, other) in enumerate(((own_ref, got_ref), (got_ref, own_ref))):
        for i in range(held):
            at, across = pl.ds(i * LEN, LEN), pl.ds(tokens + i * LEN, LEN)
            length = mine[2 * tokens:2 * tokens + 1, held + i:held + i + 1]
            out_ref[pl.ds(k * tokens + i * LEN, LEN)] = jnp.where(
                position < length, mine[at] + other[across], 0.0
            )
    lane = lax.broadcasted_iota(jnp.int32, (EXTRA, columns), 1)
    numbers = jnp.zeros(lane.shape, F32)
    for k, ref in enumerate((own_ref, got_ref)):
        for i in range(held):
            slot = ref[2 * tokens:2 * tokens + 1, i:i + 1]
            numbers = jnp.where(lane == k * held + i, slot, numbers)
    out_ref[2 * tokens:] = numbers


def score_kernel(window_ref, block_ref, total_ref, inn_ref, table_ref):
    height, columns = total_ref.shape
    queries = columns // RANK
    column = lax.broadcasted_iota(jnp.int32, (columns, queries), 0) // RANK
    query = lax.broadcasted_iota(jnp.int32, (columns, queries), 1)
    fold = (column == query).astype(F32)
    row = lax.broadcasted_iota(jnp.int32, table_ref.shape, 0).astype(F32)
    contrib = (total_ref[...] + dot(window_ref[...], block_ref[...])) * inn_ref[:height]
    count = height // LEN
    sums = [jnp.sum(contrib[i * LEN:(i + 1) * LEN], axis=0, keepdims=True) for i in range(count)]
    scores = jnp.dot(
        jnp.concatenate(sums), fold, precision=lax.Precision.HIGHEST, preferred_element_type=F32
    ) * (1.0 / math.sqrt(RANK * LEN))
    table = jnp.zeros(table_ref.shape, F32)
    for i in range(count):
        slot = inn_ref[height:height + 1, i:i + 1]
        table = jnp.where(row == slot, scores[i:i + 1], table)
    table_ref[...] = table


def score_table(arrays, rows, queries):
    vmem = pl.BlockSpec(memory_space=pltpu.VMEM)
    window, block = arrays[:2]
    size = sum(x.size * x.dtype.itemsize for x in arrays)
    return pl.pallas_call(
        score_kernel,
        in_specs=[vmem] * len(arrays),
        out_specs=vmem,
        out_shape=jax.ShapeDtypeStruct((rows, queries), F32),
        cost_estimate=pl.CostEstimate(
            flops=2 * window.size * block.shape[1], bytes_accessed=size, transcendentals=0
        ),
        compiler_params=pltpu.CompilerParams(vmem_limit_bytes=16 << 20),
        name="score",
    )(*arrays)


def shards(acts, grads, out_factors, in_factors, seq_slot, lengths):
    devices = lax.axis_size("dp")
    chips = devices // 2
    me = lax.axis_index("dp")
    tokens = grads.shape[0]
    rows, columns = out_factors.shape
    rows_in = in_factors.shape[0]
    orders = jnp.asarray(block_orders(chips))
    mine = lax.dynamic_index_in_dim(orders, me, keepdims=False)
    pairs = ring_pairs(chips)
    swap = [(d, d ^ 1) for d in range(devices)]

    send = lambda x: lax.ppermute(x, "dp", pairs)
    across = lambda x: lax.ppermute(x, "dp", swap)

    every = None
    if rows_in % 128:
        every = lax.all_gather(in_factors, "dp", axis=0, tiled=True)
        rows_in = 0
    lead = (rows - rows_in) // 2
    tokens_of = {"out": (grads, across(grads), rows)}
    if rows_in:
        tokens_of["in"] = (acts, across(acts), rows_in)

    inside = [(1, 0, rows_in, "in", 0)] if rows_in else []
    held = [[out_factors] + [in_factors] * (rows_in > 0)]
    pieces = [[(0, 0, rows, "out", 0)] + inside]
    came = send(out_factors)
    late, early = came[lead:], came[:lead]
    if rows_in:
        came, turned = lax.optimization_barrier((came, in_factors))
        turned = lax.ppermute(turned, "dp", [(j, i) for i, j in pairs])
        late, early = came[lead:], came[:lead]
        early = jnp.concatenate([send(in_factors), early])
        early, turned = lax.optimization_barrier((early, turned))
    totals, summed, last = {}, 0, chips - 1

    def sum_to(k, totals, summed):
        for j in range(summed, k):
            totals = step(mine, tokens_of, held[j], pieces[j], totals, j)
        return totals, max(k, summed)

    for s in range(1, chips):
        held.append([late, early])
        pieces.append([(0, 0, rows - lead, "out", lead), (1, rows_in, lead, "out", 0)] + inside)
        if s == last:
            break
        if s >= 4:
            totals, summed = sum_to(min(2 * s - 6, s), totals, summed)
            late, totals = lax.optimization_barrier((late, totals))
            early, totals = lax.optimization_barrier((early, totals))
        late = send(late)
        early = send(early if s < last - 1 else early[rows_in:])

    window = call(
        functools.partial(window_kernel, lead), mine,
        [(x, rows, lambda i, o: (0, o[last])) for x in tokens_of["out"][:2]], [], [],
        [jax.ShapeDtypeStruct((2 * tokens, lead), grads.dtype)], 0, "window",
    )[0]
    totals, window = lax.optimization_barrier((totals, window))
    totals, summed = sum_to(last, totals, summed)
    slots = lengths.shape[0]
    height = (2 * tokens + EXTRA, columns)
    if rows_in:
        inn = call(
            functools.partial(turned_kernel, 1), mine,
            [(x, rows_in, lambda i, o: (0, o[last])) for x in tokens_of["in"][:2]],
            [turned, totals["in"]], [seq_slot, lengths],
            [jax.ShapeDtypeStruct(height, F32)], 4 * tokens * rows_in * columns, "turned",
        )[0]
    else:
        numbers = jnp.concatenate([seq_slot, lengths]).astype(F32)
        inn = jnp.zeros(height, F32).at[:tokens].set(dot(acts, every))
        inn = inn.at[2 * tokens, :2 * slots].set(numbers)
    inn = call(
        masked_kernel, mine, [], [inn, across(inn)], [],
        [jax.ShapeDtypeStruct(height, F32)], 0, "masked",
    )[0]
    totals = step(mine, tokens_of, [late], pieces[last][:1], totals, last)

    queries = columns // RANK
    table = score_table([window, early, totals["out"], inn], slots * devices, queries)
    got = lax.all_to_all(table.reshape(devices, slots, queries), "dp", 0, 0, tiled=True)
    return jnp.sum(got, axis=0)


def solution(mesh):
    return jax.shard_map(
        shards,
        mesh=mesh,
        in_specs=(
            P(("groups", "dp"), None),
            P(("groups", "dp"), None),
            P(("groups", "dp"), None),
            P(("groups", "dp"), None),
            P(("groups", "dp")),
            P(("groups", "dp")),
        ),
        out_specs=P(("groups", "dp"), None),
        check_vma=False,
    )
```

```python
import functools
import math

import jax
import jax.numpy as jnp
import numpy as np
from jax import lax
from jax.experimental import pallas as pl
from jax.experimental.pallas import tpu as pltpu
from jax.sharding import PartitionSpec as P

RANK = 32
LEN = 80
F32 = jnp.float32
VMEM = 52 << 20


def ring_of(chips):
    cols = max([d for d in range(1, math.isqrt(chips) + 1) if chips % d == 0 and d % 2 == 0] or [1])
    rows = chips // cols
    if cols == 1 or rows % 2:
        return list(range(chips))
    walk = []
    for r in range(rows):
        line = range(1, cols) if r % 2 == 0 else range(cols - 1, 0, -1)
        walk += [r * cols + c for c in line]
    return walk + [r * cols for r in reversed(range(rows))]


def block_orders(chips):
    ring = ring_of(chips)
    order = np.zeros((2 * chips, chips), np.int32)
    for p, chip in enumerate(ring):
        for s in range(chips):
            order[2 * chip, s] = 2 * ring[(p - s) % chips]
            order[2 * chip + 1, s] = 2 * ring[(p + s) % chips] + 1
    return order


def ring_pairs(chips):
    ring = ring_of(chips)
    pairs = []
    for p, chip in enumerate(ring):
        pairs.append((2 * chip, 2 * ring[(p + 1) % chips]))
        pairs.append((2 * chip + 1, 2 * ring[(p - 1) % chips] + 1))
    return pairs


def dot(a, b):
    return jnp.dot(a, b, preferred_element_type=F32)


def call(kernel, order, windows, whole, scalars, out_shape, flops, name):
    in_specs = [pl.BlockSpec((x.shape[0], w), at) for x, w, at in windows]
    in_specs += [pl.BlockSpec(x.shape, lambda i, o: (0, 0)) for x in whole]
    in_specs += [pl.BlockSpec(memory_space=pltpu.SMEM) for _ in scalars]
    size = sum(2 * x.shape[0] * w for x, w, _ in windows)
    size += sum(x.size * x.dtype.itemsize for x in list(whole) + list(out_shape))
    return pl.pallas_call(
        kernel,
        grid_spec=pltpu.PrefetchScalarGridSpec(
            num_scalar_prefetch=1,
            grid=(1,),
            in_specs=in_specs,
            out_specs=[pl.BlockSpec(x.shape, lambda i, o: (0, 0)) for x in out_shape],
        ),
        out_shape=out_shape,
        cost_estimate=pl.CostEstimate(flops=flops, bytes_accessed=size, transcendentals=0),
        compiler_params=pltpu.CompilerParams(vmem_limit_bytes=VMEM),
        name=name,
    )(order, *[x for x, _, _ in windows], *whole, *scalars)


def step_kernel(pieces, kinds, count, summed, order_ref, *refs):
    windows = {kind: refs[2 * i:2 * i + 2] for i, kind in enumerate(kinds)}
    blocks, refs = refs[2 * len(kinds):2 * len(kinds) + count], refs[2 * len(kinds) + count:]
    tokens = windows[kinds[0]][0].shape[0]
    for i, kind in enumerate(kinds):
        for k in range(2):
            at = pl.ds(k * tokens, tokens)
            total = refs[i][at] if summed else 0.0
            for which, row, height, of, column in pieces:
                if of == kind:
                    window = windows[kind][k][:, column:column + height]
                    total += dot(window, blocks[which][row:row + height])
            refs[i - len(kinds)][at] = total


def step(order, tokens_of, blocks, pieces, totals, s):
    kinds = sorted({piece[3] for piece in pieces})
    windows = []
    for kind in kinds:
        own, sib, width = tokens_of[kind]
        windows += [(x, width, lambda i, o: (0, o[s])) for x in (own, sib)]
    tokens, columns = windows[0][0].shape[0], blocks[0].shape[1]
    summed = all(kind in totals for kind in kinds)
    shape = jax.ShapeDtypeStruct((2 * tokens, columns), F32)
    out = call(
        functools.partial(step_kernel, pieces, kinds, len(blocks), summed),
        order, windows, list(blocks) + ([totals[k] for k in kinds] if summed else []), [],
        [shape] * len(kinds), 4 * tokens * sum(p[2] for p in pieces) * columns, "step",
    )
    return {**totals, **dict(zip(kinds, out))}


def window_kernel(lead, order_ref, own_ref, sib_ref, out_ref):
    tokens = own_ref.shape[0]
    out_ref[:tokens] = own_ref[:, :lead]
    out_ref[tokens:] = sib_ref[:, :lead]


EXTRA = 8


def turned_kernel(count, order_ref, *refs):
    windows, blocks = refs[:2 * count], refs[2 * count:3 * count]
    total_ref, seq_ref, len_ref, out_ref = refs[3 * count:]
    tokens = windows[0].shape[0]
    for k in range(2):
        at = pl.ds(k * tokens, tokens)
        total = total_ref[at]
        for w in range(count):
            total += dot(windows[2 * w + k][...], blocks[w][...])
        out_ref[at] = total
    held = seq_ref.shape[0]
    lane = lax.broadcasted_iota(jnp.int32, (EXTRA, out_ref.shape[1]), 1)
    numbers = jnp.zeros(lane.shape, F32)
    for i in range(held):
        numbers = jnp.where(lane == i, seq_ref[i].astype(F32), numbers)
        numbers = jnp.where(lane == held + i, len_ref[i].astype(F32), numbers)
    out_ref[2 * tokens:] = numbers


def masked_kernel(order_ref, own_ref, got_ref, out_ref):
    tokens = (own_ref.shape[0] - EXTRA) // 2
    columns = own_ref.shape[1]
    held = tokens // LEN
    position = lax.broadcasted_iota(jnp.int32, (LEN, columns), 0).astype(F32)
    for k, (mine, other) in enumerate(((own_ref, got_ref), (got_ref, own_ref))):
        for i in range(held):
            at, across = pl.ds(i * LEN, LEN), pl.ds(tokens + i * LEN, LEN)
            length = mine[2 * tokens:2 * tokens + 1, held + i:held + i + 1]
            out_ref[pl.ds(k * tokens + i * LEN, LEN)] = jnp.where(
                position < length, mine[at] + other[across], 0.0
            )
    lane = lax.broadcasted_iota(jnp.int32, (EXTRA, columns), 1)
    numbers = jnp.zeros(lane.shape, F32)
    for k, ref in enumerate((own_ref, got_ref)):
        for i in range(held):
            slot = ref[2 * tokens:2 * tokens + 1, i:i + 1]
            numbers = jnp.where(lane == k * held + i, slot, numbers)
    out_ref[2 * tokens:] = numbers


def score_kernel(window_ref, block_ref, total_ref, inn_ref, table_ref):
    height, columns = total_ref.shape
    queries = columns // RANK
    column = lax.broadcasted_iota(jnp.int32, (columns, queries), 0) // RANK
    query = lax.broadcasted_iota(jnp.int32, (columns, queries), 1)
    fold = (column == query).astype(F32)
    row = lax.broadcasted_iota(jnp.int32, table_ref.shape, 0).astype(F32)
    contrib = (total_ref[...] + dot(window_ref[...], block_ref[...])) * inn_ref[:height]
    count = height // LEN
    sums = [jnp.sum(contrib[i * LEN:(i + 1) * LEN], axis=0, keepdims=True) for i in range(count)]
    scores = jnp.dot(
        jnp.concatenate(sums), fold, precision=lax.Precision.HIGHEST, preferred_element_type=F32
    ) * (1.0 / math.sqrt(RANK * LEN))
    table = jnp.zeros(table_ref.shape, F32)
    for i in range(count):
        slot = inn_ref[height:height + 1, i:i + 1]
        table = jnp.where(row == slot, scores[i:i + 1], table)
    table_ref[...] = table


def score_table(arrays, rows, queries):
    vmem = pl.BlockSpec(memory_space=pltpu.VMEM)
    window, block = arrays[:2]
    size = sum(x.size * x.dtype.itemsize for x in arrays)
    return pl.pallas_call(
        score_kernel,
        in_specs=[vmem] * len(arrays),
        out_specs=vmem,
        out_shape=jax.ShapeDtypeStruct((rows, queries), F32),
        cost_estimate=pl.CostEstimate(
            flops=2 * window.size * block.shape[1], bytes_accessed=size, transcendentals=0
        ),
        compiler_params=pltpu.CompilerParams(vmem_limit_bytes=16 << 20),
        name="score",
    )(*arrays)


def shards(acts, grads, out_factors, in_factors, seq_slot, lengths):
    devices = lax.axis_size("dp")
    chips = devices // 2
    me = lax.axis_index("dp")
    tokens = grads.shape[0]
    rows, columns = out_factors.shape
    rows_in = in_factors.shape[0]
    orders = jnp.asarray(block_orders(chips))
    mine = lax.dynamic_index_in_dim(orders, me, keepdims=False)
    pairs = ring_pairs(chips)
    swap = [(d, d ^ 1) for d in range(devices)]

    send = lambda x: lax.ppermute(x, "dp", pairs)
    across = lambda x: lax.ppermute(x, "dp", swap)

    every = None
    if rows_in % 128:
        every = lax.all_gather(in_factors, "dp", axis=0, tiled=True)
        rows_in = 0
    lead = (rows - rows_in) // 2
    tokens_of = {"out": (grads, across(grads), rows)}
    if rows_in:
        tokens_of["in"] = (acts, across(acts), rows_in)

    inside = [(1, 0, rows_in, "in", 0)] if rows_in else []
    held = [[out_factors] + [in_factors] * (rows_in > 0)]
    pieces = [[(0, 0, rows, "out", 0)] + inside]
    came = send(out_factors)
    late, early = came[lead:], came[:lead]
    if rows_in:
        came, turned = lax.optimization_barrier((came, in_factors))
        turned = lax.ppermute(turned, "dp", [(j, i) for i, j in pairs])
        late, early = came[lead:], came[:lead]
        inner, turned = lax.optimization_barrier((send(in_factors), turned))
        early = jnp.concatenate([inner, early])
    totals, summed, last = {}, 0, chips - 1

    def sum_to(k, totals, summed):
        for j in range(summed, k):
            totals = step(mine, tokens_of, held[j], pieces[j], totals, j)
        return totals, max(k, summed)

    for s in range(1, chips):
        held.append([late, early])
        pieces.append([(0, 0, rows - lead, "out", lead), (1, rows_in, lead, "out", 0)] + inside)
        if s == last:
            break
        if s >= 4:
            totals, summed = sum_to(min(2 * s - 6, s), totals, summed)
            late, totals = lax.optimization_barrier((late, totals))
            early, totals = lax.optimization_barrier((early, totals))
        late = send(late)
        early = send(early if s < last - 1 else early[rows_in:])

    window = call(
        functools.partial(window_kernel, lead), mine,
        [(x, rows, lambda i, o: (0, o[last])) for x in tokens_of["out"][:2]], [], [],
        [jax.ShapeDtypeStruct((2 * tokens, lead), grads.dtype)], 0, "window",
    )[0]
    totals, window = lax.optimization_barrier((totals, window))
    totals, summed = sum_to(last, totals, summed)
    slots = lengths.shape[0]
    height = (2 * tokens + EXTRA, columns)
    if rows_in:
        inn = call(
            functools.partial(turned_kernel, 1), mine,
            [(x, rows_in, lambda i, o: (0, o[last])) for x in tokens_of["in"][:2]],
            [turned, totals["in"]], [seq_slot, lengths],
            [jax.ShapeDtypeStruct(height, F32)], 4 * tokens * rows_in * columns, "turned",
        )[0]
    else:
        numbers = jnp.concatenate([seq_slot, lengths]).astype(F32)
        inn = jnp.zeros(height, F32).at[:tokens].set(dot(acts, every))
        inn = inn.at[2 * tokens, :2 * slots].set(numbers)
    inn = call(
        masked_kernel, mine, [], [inn, across(inn)], [],
        [jax.ShapeDtypeStruct(height, F32)], 0, "masked",
    )[0]
    totals = step(mine, tokens_of, [late], pieces[last][:1], totals, last)

    queries = columns // RANK
    table = score_table([window, early, totals["out"], inn], slots * devices, queries)
    got = lax.all_to_all(table.reshape(devices, slots, queries), "dp", 0, 0, tiled=True)
    return jnp.sum(got, axis=0)


def solution(mesh):
    return jax.shard_map(
        shards,
        mesh=mesh,
        in_specs=(
            P(("groups", "dp"), None),
            P(("groups", "dp"), None),
            P(("groups", "dp"), None),
            P(("groups", "dp"), None),
            P(("groups", "dp")),
            P(("groups", "dp")),
        ),
        out_specs=P(("groups", "dp"), None),
        check_vma=False,
    )
```

```python
import functools
import math

import jax
import jax.numpy as jnp
import numpy as np
from jax import lax
from jax.experimental import pallas as pl
from jax.experimental.pallas import tpu as pltpu
from jax.sharding import PartitionSpec as P

RANK = 32
LEN = 80
F32 = jnp.float32
VMEM = 52 << 20


def ring_of(chips):
    cols = max([d for d in range(1, math.isqrt(chips) + 1) if chips % d == 0 and d % 2 == 0] or [1])
    rows = chips // cols
    if cols == 1 or rows % 2:
        return list(range(chips))
    walk = []
    for r in range(rows):
        line = range(1, cols) if r % 2 == 0 else range(cols - 1, 0, -1)
        walk += [r * cols + c for c in line]
    return walk + [r * cols for r in reversed(range(rows))]


def block_orders(chips):
    ring = ring_of(chips)
    order = np.zeros((2 * chips, chips), np.int32)
    for p, chip in enumerate(ring):
        for s in range(chips):
            order[2 * chip, s] = 2 * ring[(p - s) % chips]
            order[2 * chip + 1, s] = 2 * ring[(p + s) % chips] + 1
    return order


def ring_pairs(chips):
    ring = ring_of(chips)
    pairs = []
    for p, chip in enumerate(ring):
        pairs.append((2 * chip, 2 * ring[(p + 1) % chips]))
        pairs.append((2 * chip + 1, 2 * ring[(p - 1) % chips] + 1))
    return pairs


def dot(a, b):
    return jnp.dot(a, b, preferred_element_type=F32)


def call(kernel, order, windows, whole, scalars, out_shape, flops, name):
    in_specs = [pl.BlockSpec((x.shape[0], w), at) for x, w, at in windows]
    in_specs += [pl.BlockSpec(x.shape, lambda i, o: (0, 0)) for x in whole]
    in_specs += [pl.BlockSpec(memory_space=pltpu.SMEM) for _ in scalars]
    size = sum(2 * x.shape[0] * w for x, w, _ in windows)
    size += sum(x.size * x.dtype.itemsize for x in list(whole) + list(out_shape))
    return pl.pallas_call(
        kernel,
        grid_spec=pltpu.PrefetchScalarGridSpec(
            num_scalar_prefetch=1,
            grid=(1,),
            in_specs=in_specs,
            out_specs=[pl.BlockSpec(x.shape, lambda i, o: (0, 0)) for x in out_shape],
        ),
        out_shape=out_shape,
        cost_estimate=pl.CostEstimate(flops=flops, bytes_accessed=size, transcendentals=0),
        compiler_params=pltpu.CompilerParams(vmem_limit_bytes=VMEM),
        name=name,
    )(order, *[x for x, _, _ in windows], *whole, *scalars)


def step_kernel(pieces, kinds, count, summed, order_ref, *refs):
    windows = {kind: refs[2 * i:2 * i + 2] for i, kind in enumerate(kinds)}
    blocks, refs = refs[2 * len(kinds):2 * len(kinds) + count], refs[2 * len(kinds) + count:]
    tokens = windows[kinds[0]][0].shape[0]
    for i, kind in enumerate(kinds):
        for k in range(2):
            at = pl.ds(k * tokens, tokens)
            total = refs[i][at] if summed else 0.0
            for which, row, height, of, column in pieces:
                if of == kind:
                    window = windows[kind][k][:, column:column + height]
                    total += dot(window, blocks[which][row:row + height])
            refs[i - len(kinds)][at] = total


def step(order, tokens_of, blocks, pieces, totals, s):
    kinds = sorted({piece[3] for piece in pieces})
    windows = []
    for kind in kinds:
        own, sib, width = tokens_of[kind]
        windows += [(x, width, lambda i, o: (0, o[s])) for x in (own, sib)]
    tokens, columns = windows[0][0].shape[0], blocks[0].shape[1]
    summed = all(kind in totals for kind in kinds)
    shape = jax.ShapeDtypeStruct((2 * tokens, columns), F32)
    out = call(
        functools.partial(step_kernel, pieces, kinds, len(blocks), summed),
        order, windows, list(blocks) + ([totals[k] for k in kinds] if summed else []), [],
        [shape] * len(kinds), 4 * tokens * sum(p[2] for p in pieces) * columns, "step",
    )
    return {**totals, **dict(zip(kinds, out))}


def window_kernel(lead, order_ref, own_ref, sib_ref, out_ref):
    tokens = own_ref.shape[0]
    out_ref[:tokens] = own_ref[:, :lead]
    out_ref[tokens:] = sib_ref[:, :lead]


EXTRA = 8


def turned_kernel(count, order_ref, *refs):
    windows, blocks = refs[:2 * count], refs[2 * count:3 * count]
    total_ref, seq_ref, len_ref, out_ref = refs[3 * count:]
    tokens = windows[0].shape[0]
    for k in range(2):
        at = pl.ds(k * tokens, tokens)
        total = total_ref[at]
        for w in range(count):
            total += dot(windows[2 * w + k][...], blocks[w][...])
        out_ref[at] = total
    held = seq_ref.shape[0]
    lane = lax.broadcasted_iota(jnp.int32, (EXTRA, out_ref.shape[1]), 1)
    numbers = jnp.zeros(lane.shape, F32)
    for i in range(held):
        numbers = jnp.where(lane == i, seq_ref[i].astype(F32), numbers)
        numbers = jnp.where(lane == held + i, len_ref[i].astype(F32), numbers)
    out_ref[2 * tokens:] = numbers


def masked_kernel(order_ref, own_ref, got_ref, out_ref):
    tokens = (own_ref.shape[0] - EXTRA) // 2
    columns = own_ref.shape[1]
    held = tokens // LEN
    position = lax.broadcasted_iota(jnp.int32, (LEN, columns), 0).astype(F32)
    for k, (mine, other) in enumerate(((own_ref, got_ref), (got_ref, own_ref))):
        for i in range(held):
            at, across = pl.ds(i * LEN, LEN), pl.ds(tokens + i * LEN, LEN)
            length = mine[2 * tokens:2 * tokens + 1, held + i:held + i + 1]
            out_ref[pl.ds(k * tokens + i * LEN, LEN)] = jnp.where(
                position < length, mine[at] + other[across], 0.0
            )
    lane = lax.broadcasted_iota(jnp.int32, (EXTRA, columns), 1)
    numbers = jnp.zeros(lane.shape, F32)
    for k, ref in enumerate((own_ref, got_ref)):
        for i in range(held):
            slot = ref[2 * tokens:2 * tokens + 1, i:i + 1]
            numbers = jnp.where(lane == k * held + i, slot, numbers)
    out_ref[2 * tokens:] = numbers


def score_kernel(window_ref, block_ref, total_ref, inn_ref, table_ref):
    height, columns = total_ref.shape
    queries = columns // RANK
    column = lax.broadcasted_iota(jnp.int32, (columns, queries), 0) // RANK
    query = lax.broadcasted_iota(jnp.int32, (columns, queries), 1)
    fold = (column == query).astype(F32)
    row = lax.broadcasted_iota(jnp.int32, table_ref.shape, 0).astype(F32)
    contrib = (total_ref[...] + dot(window_ref[...], block_ref[...])) * inn_ref[:height]
    count = height // LEN
    sums = [jnp.sum(contrib[i * LEN:(i + 1) * LEN], axis=0, keepdims=True) for i in range(count)]
    scores = jnp.dot(
        jnp.concatenate(sums), fold, precision=lax.Precision.HIGHEST, preferred_element_type=F32
    ) * (1.0 / math.sqrt(RANK * LEN))
    table = jnp.zeros(table_ref.shape, F32)
    for i in range(count):
        slot = inn_ref[height:height + 1, i:i + 1]
        table = jnp.where(row == slot, scores[i:i + 1], table)
    table_ref[...] = table


def score_table(arrays, rows, queries):
    vmem = pl.BlockSpec(memory_space=pltpu.VMEM)
    window, block = arrays[:2]
    size = sum(x.size * x.dtype.itemsize for x in arrays)
    return pl.pallas_call(
        score_kernel,
        in_specs=[vmem] * len(arrays),
        out_specs=vmem,
        out_shape=jax.ShapeDtypeStruct((rows, queries), F32),
        cost_estimate=pl.CostEstimate(
            flops=2 * window.size * block.shape[1], bytes_accessed=size, transcendentals=0
        ),
        compiler_params=pltpu.CompilerParams(vmem_limit_bytes=16 << 20),
        name="score",
    )(*arrays)


def shards(acts, grads, out_factors, in_factors, seq_slot, lengths):
    devices = lax.axis_size("dp")
    chips = devices // 2
    me = lax.axis_index("dp")
    tokens = grads.shape[0]
    rows, columns = out_factors.shape
    rows_in = in_factors.shape[0]
    orders = jnp.asarray(block_orders(chips))
    mine = lax.dynamic_index_in_dim(orders, me, keepdims=False)
    pairs = ring_pairs(chips)
    swap = [(d, d ^ 1) for d in range(devices)]

    send = lambda x: lax.ppermute(x, "dp", pairs)
    across = lambda x: lax.ppermute(x, "dp", swap)

    every = None
    if rows_in % 128:
        every = lax.all_gather(in_factors, "dp", axis=0, tiled=True)
        rows_in = 0
    lead = (rows - rows_in) // 2
    tokens_of = {"out": (grads, across(grads), rows)}
    if rows_in:
        tokens_of["in"] = (acts, across(acts), rows_in)

    inside = [(1, 0, rows_in, "in", 0)] if rows_in else []
    held = [[out_factors] + [in_factors] * (rows_in > 0)]
    pieces = [[(0, 0, rows, "out", 0)] + inside]
    came = send(out_factors)
    late, early = came[lead:], came[:lead]
    if rows_in:
        came, turned = lax.optimization_barrier((came, in_factors))
        turned = lax.ppermute(turned, "dp", [(j, i) for i, j in pairs])
        late, early = came[lead:], came[:lead]
        inner, turned = lax.optimization_barrier((send(in_factors), turned))
        early = jnp.concatenate([inner, early])
    totals, summed, last = {}, 0, chips - 1

    def sum_to(k, totals, summed):
        for j in range(summed, k):
            totals = step(mine, tokens_of, held[j], pieces[j], totals, j)
        return totals, max(k, summed)

    for s in range(1, chips):
        held.append([late, early])
        pieces.append([(0, 0, rows - lead, "out", lead), (1, rows_in, lead, "out", 0)] + inside)
        if s == last:
            break
        if s >= 4:
            totals, summed = sum_to(min(2 * s - 6, s), totals, summed)
            late, totals = lax.optimization_barrier((late, totals))
            early, totals = lax.optimization_barrier((early, totals))
        late = send(late)
        early = send(early if s < last - 1 else early[rows_in:])

    window = call(
        functools.partial(window_kernel, lead), mine,
        [(x, rows, lambda i, o: (0, o[last])) for x in tokens_of["out"][:2]], [], [],
        [jax.ShapeDtypeStruct((2 * tokens, lead), grads.dtype)], 0, "window",
    )[0]
    totals, window = lax.optimization_barrier((totals, window))
    totals, summed = sum_to(last, totals, summed)
    slots = lengths.shape[0]
    height = (2 * tokens + EXTRA, columns)
    if rows_in:
        inn = call(
            functools.partial(turned_kernel, 1), mine,
            [(x, rows_in, lambda i, o: (0, o[last])) for x in tokens_of["in"][:2]],
            [turned, totals["in"]], [seq_slot, lengths],
            [jax.ShapeDtypeStruct(height, F32)], 4 * tokens * rows_in * columns, "turned",
        )[0]
    else:
        numbers = jnp.concatenate([seq_slot, lengths]).astype(F32)
        inn = jnp.zeros(height, F32).at[:tokens].set(dot(acts, every))
        inn = inn.at[2 * tokens, :2 * slots].set(numbers)
    inn = call(
        masked_kernel, mine, [], [inn, across(inn)], [],
        [jax.ShapeDtypeStruct(height, F32)], 0, "masked",
    )[0]
    totals = step(mine, tokens_of, [late], pieces[last][:1], totals, last)

    queries = columns // RANK
    table = score_table([window, early, totals["out"], inn], slots * devices, queries)
    groups = [list(range(core, devices, 2)) for core in (0, 1)]
    got = lax.all_to_all(
        table.reshape(chips, 2 * slots, queries), "dp", 0, 0, axis_index_groups=groups, tiled=True
    )
    got = jnp.sum(got, axis=0)
    first = me % 2 == 0
    keep = jnp.where(first, got[:slots], got[slots:])
    give = jnp.where(first, got[slots:], got[:slots])
    return keep + across(give)


def solution(mesh):
    return jax.shard_map(
        shards,
        mesh=mesh,
        in_specs=(
            P(("groups", "dp"), None),
            P(("groups", "dp"), None),
            P(("groups", "dp"), None),
            P(("groups", "dp"), None),
            P(("groups", "dp")),
            P(("groups", "dp")),
        ),
        out_specs=P(("groups", "dp"), None),
        check_vma=False,
    )
```

```python
import functools
import math

import jax
import jax.numpy as jnp
import numpy as np
from jax import lax
from jax.experimental import pallas as pl
from jax.experimental.pallas import tpu as pltpu
from jax.sharding import PartitionSpec as P

RANK = 32
LEN = 80
F32 = jnp.float32
VMEM = 52 << 20


def ring_of(chips):
    cols = max([d for d in range(1, math.isqrt(chips) + 1) if chips % d == 0 and d % 2 == 0] or [1])
    rows = chips // cols
    if cols == 1 or rows % 2:
        return list(range(chips))
    walk = []
    for r in range(rows):
        line = range(1, cols) if r % 2 == 0 else range(cols - 1, 0, -1)
        walk += [r * cols + c for c in line]
    return walk + [r * cols for r in reversed(range(rows))]


def block_orders(chips):
    ring = ring_of(chips)
    order = np.zeros((2 * chips, chips), np.int32)
    for p, chip in enumerate(ring):
        for s in range(chips):
            order[2 * chip, s] = 2 * ring[(p - s) % chips]
            order[2 * chip + 1, s] = 2 * ring[(p + s) % chips] + 1
    return order


def ring_pairs(chips):
    ring = ring_of(chips)
    pairs = []
    for p, chip in enumerate(ring):
        pairs.append((2 * chip, 2 * ring[(p + 1) % chips]))
        pairs.append((2 * chip + 1, 2 * ring[(p - 1) % chips] + 1))
    return pairs


def dot(a, b):
    return jnp.dot(a, b, preferred_element_type=F32)


def call(kernel, order, windows, whole, scalars, out_shape, flops, name):
    in_specs = [pl.BlockSpec((x.shape[0], w), at) for x, w, at in windows]
    in_specs += [pl.BlockSpec(x.shape, lambda i, o: (0, 0)) for x in whole]
    in_specs += [pl.BlockSpec(memory_space=pltpu.SMEM) for _ in scalars]
    size = sum(2 * x.shape[0] * w for x, w, _ in windows)
    size += sum(x.size * x.dtype.itemsize for x in list(whole) + list(out_shape))
    return pl.pallas_call(
        kernel,
        grid_spec=pltpu.PrefetchScalarGridSpec(
            num_scalar_prefetch=1,
            grid=(1,),
            in_specs=in_specs,
            out_specs=[pl.BlockSpec(x.shape, lambda i, o: (0, 0)) for x in out_shape],
        ),
        out_shape=out_shape,
        cost_estimate=pl.CostEstimate(flops=flops, bytes_accessed=size, transcendentals=0),
        compiler_params=pltpu.CompilerParams(vmem_limit_bytes=VMEM),
        name=name,
    )(order, *[x for x, _, _ in windows], *whole, *scalars)


def step_kernel(pieces, kinds, count, summed, order_ref, *refs):
    windows = {kind: refs[2 * i:2 * i + 2] for i, kind in enumerate(kinds)}
    blocks, refs = refs[2 * len(kinds):2 * len(kinds) + count], refs[2 * len(kinds) + count:]
    tokens = windows[kinds[0]][0].shape[0]
    for i, kind in enumerate(kinds):
        for k in range(2):
            at = pl.ds(k * tokens, tokens)
            total = refs[i][at] if summed else 0.0
            for which, row, height, of, column in pieces:
                if of == kind:
                    window = windows[kind][k][:, column:column + height]
                    total += dot(window, blocks[which][row:row + height])
            refs[i - len(kinds)][at] = total


def step(order, tokens_of, blocks, pieces, totals, s):
    kinds = sorted({piece[3] for piece in pieces})
    windows = []
    for kind in kinds:
        own, sib, width = tokens_of[kind]
        windows += [(x, width, lambda i, o: (0, o[s])) for x in (own, sib)]
    tokens, columns = windows[0][0].shape[0], blocks[0].shape[1]
    summed = all(kind in totals for kind in kinds)
    shape = jax.ShapeDtypeStruct((2 * tokens, columns), F32)
    out = call(
        functools.partial(step_kernel, pieces, kinds, len(blocks), summed),
        order, windows, list(blocks) + ([totals[k] for k in kinds] if summed else []), [],
        [shape] * len(kinds), 4 * tokens * sum(p[2] for p in pieces) * columns, "step",
    )
    return {**totals, **dict(zip(kinds, out))}


def window_kernel(lead, order_ref, own_ref, sib_ref, out_ref):
    tokens = own_ref.shape[0]
    out_ref[:tokens] = own_ref[:, :lead]
    out_ref[tokens:] = sib_ref[:, :lead]


EXTRA = 8


def turned_kernel(count, order_ref, *refs):
    windows, blocks = refs[:2 * count], refs[2 * count:3 * count]
    total_ref, seq_ref, len_ref, out_ref = refs[3 * count:]
    tokens = windows[0].shape[0]
    for k in range(2):
        at = pl.ds(k * tokens, tokens)
        total = total_ref[at]
        for w in range(count):
            total += dot(windows[2 * w + k][...], blocks[w][...])
        out_ref[at] = total
    held = seq_ref.shape[0]
    lane = lax.broadcasted_iota(jnp.int32, (EXTRA, out_ref.shape[1]), 1)
    numbers = jnp.zeros(lane.shape, F32)
    for i in range(held):
        numbers = jnp.where(lane == i, seq_ref[i].astype(F32), numbers)
        numbers = jnp.where(lane == held + i, len_ref[i].astype(F32), numbers)
    out_ref[2 * tokens:] = numbers


def masked_kernel(order_ref, own_ref, got_ref, out_ref):
    tokens = (own_ref.shape[0] - EXTRA) // 2
    columns = own_ref.shape[1]
    held = tokens // LEN
    position = lax.broadcasted_iota(jnp.int32, (LEN, columns), 0).astype(F32)
    for k, (mine, other) in enumerate(((own_ref, got_ref), (got_ref, own_ref))):
        for i in range(held):
            at, across = pl.ds(i * LEN, LEN), pl.ds(tokens + i * LEN, LEN)
            length = mine[2 * tokens:2 * tokens + 1, held + i:held + i + 1]
            out_ref[pl.ds(k * tokens + i * LEN, LEN)] = jnp.where(
                position < length, mine[at] + other[across], 0.0
            )
    lane = lax.broadcasted_iota(jnp.int32, (EXTRA, columns), 1)
    numbers = jnp.zeros(lane.shape, F32)
    for k, ref in enumerate((own_ref, got_ref)):
        for i in range(held):
            slot = ref[2 * tokens:2 * tokens + 1, i:i + 1]
            numbers = jnp.where(lane == k * held + i, slot, numbers)
    out_ref[2 * tokens:] = numbers


def score_kernel(window_ref, block_ref, total_ref, inn_ref, table_ref):
    height, columns = total_ref.shape
    queries = columns // RANK
    column = lax.broadcasted_iota(jnp.int32, (columns, queries), 0) // RANK
    query = lax.broadcasted_iota(jnp.int32, (columns, queries), 1)
    fold = (column == query).astype(F32)
    row = lax.broadcasted_iota(jnp.int32, table_ref.shape, 0).astype(F32)
    contrib = (total_ref[...] + dot(window_ref[...], block_ref[...])) * inn_ref[:height]
    count = height // LEN
    sums = [jnp.sum(contrib[i * LEN:(i + 1) * LEN], axis=0, keepdims=True) for i in range(count)]
    scores = jnp.dot(
        jnp.concatenate(sums), fold, precision=lax.Precision.HIGHEST, preferred_element_type=F32
    ) * (1.0 / math.sqrt(RANK * LEN))
    table = jnp.zeros(table_ref.shape, F32)
    for i in range(count):
        slot = inn_ref[height:height + 1, i:i + 1]
        table = jnp.where(row == slot, scores[i:i + 1], table)
    table_ref[...] = table


def score_table(arrays, rows, queries):
    vmem = pl.BlockSpec(memory_space=pltpu.VMEM)
    window, block = arrays[:2]
    size = sum(x.size * x.dtype.itemsize for x in arrays)
    return pl.pallas_call(
        score_kernel,
        in_specs=[vmem] * len(arrays),
        out_specs=vmem,
        out_shape=jax.ShapeDtypeStruct((rows, queries), F32),
        cost_estimate=pl.CostEstimate(
            flops=2 * window.size * block.shape[1], bytes_accessed=size, transcendentals=0
        ),
        compiler_params=pltpu.CompilerParams(vmem_limit_bytes=16 << 20),
        name="score",
    )(*arrays)


def shards(acts, grads, out_factors, in_factors, seq_slot, lengths):
    devices = lax.axis_size("dp")
    chips = devices // 2
    me = lax.axis_index("dp")
    tokens = grads.shape[0]
    rows, columns = out_factors.shape
    rows_in = in_factors.shape[0]
    orders = jnp.asarray(block_orders(chips))
    mine = lax.dynamic_index_in_dim(orders, me, keepdims=False)
    pairs = ring_pairs(chips)
    swap = [(d, d ^ 1) for d in range(devices)]

    send = lambda x: lax.ppermute(x, "dp", pairs)
    across = lambda x: lax.ppermute(x, "dp", swap)

    every = None
    if rows_in % 128:
        every = lax.all_gather(in_factors, "dp", axis=0, tiled=True)
        rows_in = 0
    lead = (rows - rows_in) // 2
    tokens_of = {"out": (grads, across(grads), rows)}
    if rows_in:
        tokens_of["in"] = (acts, across(acts), rows_in)

    inside = [(1, 0, rows_in, "in", 0)] if rows_in else []
    held = [[out_factors] + [in_factors] * (rows_in > 0)]
    pieces = [[(0, 0, rows, "out", 0)] + inside]
    came = send(out_factors)
    late, early = came[lead:], came[:lead]
    if rows_in:
        came, turned = lax.optimization_barrier((came, in_factors))
        turned = lax.ppermute(turned, "dp", [(j, i) for i, j in pairs])
        late, early = came[lead:], came[:lead]
        inner, turned = lax.optimization_barrier((send(in_factors), turned))
        early = jnp.concatenate([inner, early])
    totals, summed, last = {}, 0, chips - 1

    def sum_to(k, totals, summed):
        for j in range(summed, k):
            totals = step(mine, tokens_of, held[j], pieces[j], totals, j)
        return totals, max(k, summed)

    for s in range(1, chips):
        held.append([late, early])
        pieces.append([(0, 0, rows - lead, "out", lead), (1, rows_in, lead, "out", 0)] + inside)
        if s == last:
            break
        if s >= 4:
            totals, summed = sum_to(min(2 * s - 6, s), totals, summed)
            late, totals = lax.optimization_barrier((late, totals))
            early, totals = lax.optimization_barrier((early, totals))
        late = send(late)
        early = send(early if s < last - 1 else early[rows_in:])

    window = call(
        functools.partial(window_kernel, lead), mine,
        [(x, rows, lambda i, o: (0, o[last])) for x in tokens_of["out"][:2]], [], [],
        [jax.ShapeDtypeStruct((2 * tokens, lead), grads.dtype)], 0, "window",
    )[0]
    totals, window = lax.optimization_barrier((totals, window))
    totals, summed = sum_to(last, totals, summed)
    slots = lengths.shape[0]
    height = (2 * tokens + EXTRA, columns)
    if rows_in:
        inn = call(
            functools.partial(turned_kernel, 1), mine,
            [(x, rows_in, lambda i, o: (0, o[last])) for x in tokens_of["in"][:2]],
            [turned, totals["in"]], [seq_slot, lengths],
            [jax.ShapeDtypeStruct(height, F32)], 4 * tokens * rows_in * columns, "turned",
        )[0]
    else:
        numbers = jnp.concatenate([seq_slot, lengths]).astype(F32)
        inn = jnp.zeros(height, F32).at[:tokens].set(dot(acts, every))
        inn = inn.at[2 * tokens, :2 * slots].set(numbers)
    inn = call(
        masked_kernel, mine, [], [inn, across(inn)], [],
        [jax.ShapeDtypeStruct(height, F32)], 0, "masked",
    )[0]
    totals = step(mine, tokens_of, [late], pieces[last][:1], totals, last)

    queries = columns // RANK
    table = score_table([window, early, totals["out"], inn], slots * devices, queries)
    if devices & (devices - 1):
        got = lax.all_to_all(table.reshape(devices, slots, queries), "dp", 0, 0, tiled=True)
        return jnp.sum(got, axis=0)
    bit = devices // 2
    while bit:
        upper = lax.rem(lax.div(me, bit), 2) == 1
        low, high = table[:bit * slots], table[bit * slots:]
        give = lax.ppermute(
            jnp.where(upper, low, high), "dp", [(d, d ^ bit) for d in range(devices)]
        )
        table = jnp.where(upper, high, low) + give
        bit //= 2
    return table


def solution(mesh):
    return jax.shard_map(
        shards,
        mesh=mesh,
        in_specs=(
            P(("groups", "dp"), None),
            P(("groups", "dp"), None),
            P(("groups", "dp"), None),
            P(("groups", "dp"), None),
            P(("groups", "dp")),
            P(("groups", "dp")),
        ),
        out_specs=P(("groups", "dp"), None),
        check_vma=False,
    )
```

```python
import functools
import math

import jax
import jax.numpy as jnp
import numpy as np
from jax import lax
from jax.experimental import pallas as pl
from jax.experimental.pallas import tpu as pltpu
from jax.sharding import PartitionSpec as P

RANK = 32
LEN = 80
F32 = jnp.float32
VMEM = 52 << 20


def ring_of(chips):
    cols = max([d for d in range(1, math.isqrt(chips) + 1) if chips % d == 0 and d % 2 == 0] or [1])
    rows = chips // cols
    if cols == 1 or rows % 2:
        return list(range(chips))
    walk = []
    for r in range(rows):
        line = range(1, cols) if r % 2 == 0 else range(cols - 1, 0, -1)
        walk += [r * cols + c for c in line]
    return walk + [r * cols for r in reversed(range(rows))]


def block_orders(chips):
    ring = ring_of(chips)
    order = np.zeros((2 * chips, chips), np.int32)
    for p, chip in enumerate(ring):
        for s in range(chips):
            order[2 * chip, s] = 2 * ring[(p - s) % chips]
            order[2 * chip + 1, s] = 2 * ring[(p + s) % chips] + 1
    return order


def ring_pairs(chips):
    ring = ring_of(chips)
    pairs = []
    for p, chip in enumerate(ring):
        pairs.append((2 * chip, 2 * ring[(p + 1) % chips]))
        pairs.append((2 * chip + 1, 2 * ring[(p - 1) % chips] + 1))
    return pairs


def dot(a, b):
    return jnp.dot(a, b, preferred_element_type=F32)


def call(kernel, order, windows, whole, scalars, out_shape, flops, name):
    in_specs = [pl.BlockSpec((x.shape[0], w), at) for x, w, at in windows]
    in_specs += [pl.BlockSpec(x.shape, lambda i, o: (0, 0)) for x in whole]
    in_specs += [pl.BlockSpec(memory_space=pltpu.SMEM) for _ in scalars]
    size = sum(2 * x.shape[0] * w for x, w, _ in windows)
    size += sum(x.size * x.dtype.itemsize for x in list(whole) + list(out_shape))
    return pl.pallas_call(
        kernel,
        grid_spec=pltpu.PrefetchScalarGridSpec(
            num_scalar_prefetch=1,
            grid=(1,),
            in_specs=in_specs,
            out_specs=[pl.BlockSpec(x.shape, lambda i, o: (0, 0)) for x in out_shape],
        ),
        out_shape=out_shape,
        cost_estimate=pl.CostEstimate(flops=flops, bytes_accessed=size, transcendentals=0),
        compiler_params=pltpu.CompilerParams(vmem_limit_bytes=VMEM),
        name=name,
    )(order, *[x for x, _, _ in windows], *whole, *scalars)


def step_kernel(pieces, kinds, count, summed, order_ref, *refs):
    windows = {kind: refs[2 * i:2 * i + 2] for i, kind in enumerate(kinds)}
    blocks, refs = refs[2 * len(kinds):2 * len(kinds) + count], refs[2 * len(kinds) + count:]
    tokens = windows[kinds[0]][0].shape[0]
    for i, kind in enumerate(kinds):
        for k in range(2):
            at = pl.ds(k * tokens, tokens)
            total = refs[i][at] if summed else 0.0
            for which, row, height, of, column in pieces:
                if of == kind:
                    window = windows[kind][k][:, column:column + height]
                    total += dot(window, blocks[which][row:row + height])
            refs[i - len(kinds)][at] = total


def step(order, tokens_of, blocks, pieces, totals, s):
    kinds = sorted({piece[3] for piece in pieces})
    windows = []
    for kind in kinds:
        own, sib, width = tokens_of[kind]
        windows += [(x, width, lambda i, o: (0, o[s])) for x in (own, sib)]
    tokens, columns = windows[0][0].shape[0], blocks[0].shape[1]
    summed = all(kind in totals for kind in kinds)
    shape = jax.ShapeDtypeStruct((2 * tokens, columns), F32)
    out = call(
        functools.partial(step_kernel, pieces, kinds, len(blocks), summed),
        order, windows, list(blocks) + ([totals[k] for k in kinds] if summed else []), [],
        [shape] * len(kinds), 4 * tokens * sum(p[2] for p in pieces) * columns, "step",
    )
    return {**totals, **dict(zip(kinds, out))}


def window_kernel(lead, order_ref, own_ref, sib_ref, out_ref):
    tokens = own_ref.shape[0]
    out_ref[:tokens] = own_ref[:, :lead]
    out_ref[tokens:] = sib_ref[:, :lead]


TILE = 8
EXTRA = 8


def turned_kernel(count, order_ref, *refs):
    windows, blocks = refs[:2 * count], refs[2 * count:3 * count]
    total_ref, seq_ref, len_ref, out_ref = refs[3 * count:]
    tokens = windows[0].shape[0]
    for k in range(2):
        at = pl.ds(k * tokens, tokens)
        total = total_ref[at]
        for w in range(count):
            total += dot(windows[2 * w + k][...], blocks[w][...])
        out_ref[at] = total
    held = seq_ref.shape[0]
    lane = lax.broadcasted_iota(jnp.int32, (EXTRA, out_ref.shape[1]), 1)
    numbers = jnp.zeros(lane.shape, F32)
    for i in range(held):
        numbers = jnp.where(lane == i, seq_ref[i].astype(F32), numbers)
        numbers = jnp.where(lane == held + i, len_ref[i].astype(F32), numbers)
    out_ref[2 * tokens:] = numbers


def masked_kernel(order_ref, own_ref, got_ref, out_ref):
    tokens = (own_ref.shape[0] - EXTRA) // 2
    columns = own_ref.shape[1]
    held = tokens // LEN
    position = lax.broadcasted_iota(jnp.int32, (LEN, columns), 0).astype(F32)
    for k, (mine, other) in enumerate(((own_ref, got_ref), (got_ref, own_ref))):
        for i in range(held):
            at, across = pl.ds(i * LEN, LEN), pl.ds(tokens + i * LEN, LEN)
            length = mine[2 * tokens:2 * tokens + 1, held + i:held + i + 1]
            out_ref[pl.ds(k * tokens + i * LEN, LEN)] = jnp.where(
                position < length, mine[at] + other[across], 0.0
            )
    lane = lax.broadcasted_iota(jnp.int32, (EXTRA, columns), 1)
    numbers = jnp.zeros(lane.shape, F32)
    for k, ref in enumerate((own_ref, got_ref)):
        for i in range(held):
            slot = ref[2 * tokens:2 * tokens + 1, i:i + 1]
            numbers = jnp.where(lane == k * held + i, slot, numbers)
    out_ref[2 * tokens:] = numbers


def score_kernel(per_device, window_ref, block_ref, total_ref, inn_ref, table_ref):
    height, columns = total_ref.shape
    lanes = table_ref.shape[1]
    column = lax.broadcasted_iota(jnp.int32, (columns, lanes), 0) // RANK
    query = lax.broadcasted_iota(jnp.int32, (columns, lanes), 1)
    fold = (column == query).astype(F32)
    at = lax.broadcasted_iota(jnp.int32, table_ref.shape, 0)
    within = lax.rem(at, TILE)
    row = jnp.where(within < per_device, lax.div(at, TILE) * per_device + within, -1).astype(F32)
    contrib = (total_ref[...] + dot(window_ref[...], block_ref[...])) * inn_ref[:height]
    count = height // LEN
    sums = [jnp.sum(contrib[i * LEN:(i + 1) * LEN], axis=0, keepdims=True) for i in range(count)]
    scores = jnp.dot(
        jnp.concatenate(sums), fold, precision=lax.Precision.HIGHEST, preferred_element_type=F32
    ) * (1.0 / math.sqrt(RANK * LEN))
    table = jnp.zeros(table_ref.shape, F32)
    for i in range(count):
        slot = inn_ref[height:height + 1, i:i + 1]
        table = jnp.where(row == slot, scores[i:i + 1], table)
    table_ref[...] = table


def score_table(arrays, per_device, devices):
    vmem = pl.BlockSpec(memory_space=pltpu.VMEM)
    window, block = arrays[:2]
    size = sum(x.size * x.dtype.itemsize for x in arrays)
    return pl.pallas_call(
        functools.partial(score_kernel, per_device),
        in_specs=[vmem] * len(arrays),
        out_specs=vmem,
        out_shape=jax.ShapeDtypeStruct((devices * TILE, 128), F32),
        cost_estimate=pl.CostEstimate(
            flops=2 * window.size * block.shape[1], bytes_accessed=size, transcendentals=0
        ),
        compiler_params=pltpu.CompilerParams(vmem_limit_bytes=16 << 20),
        name="score",
    )(*arrays)


def shards(acts, grads, out_factors, in_factors, seq_slot, lengths):
    devices = lax.axis_size("dp")
    chips = devices // 2
    me = lax.axis_index("dp")
    tokens = grads.shape[0]
    rows, columns = out_factors.shape
    rows_in = in_factors.shape[0]
    orders = jnp.asarray(block_orders(chips))
    mine = lax.dynamic_index_in_dim(orders, me, keepdims=False)
    pairs = ring_pairs(chips)
    swap = [(d, d ^ 1) for d in range(devices)]

    send = lambda x: lax.ppermute(x, "dp", pairs)
    across = lambda x: lax.ppermute(x, "dp", swap)

    every = None
    if rows_in % 128:
        every = lax.all_gather(in_factors, "dp", axis=0, tiled=True)
        rows_in = 0
    lead = (rows - rows_in) // 2
    tokens_of = {"out": (grads, across(grads), rows)}
    if rows_in:
        tokens_of["in"] = (acts, across(acts), rows_in)

    inside = [(1, 0, rows_in, "in", 0)] if rows_in else []
    held = [[out_factors] + [in_factors] * (rows_in > 0)]
    pieces = [[(0, 0, rows, "out", 0)] + inside]
    came = send(out_factors)
    late, early = came[lead:], came[:lead]
    if rows_in:
        came, turned = lax.optimization_barrier((came, in_factors))
        turned = lax.ppermute(turned, "dp", [(j, i) for i, j in pairs])
        late, early = came[lead:], came[:lead]
        inner, turned = lax.optimization_barrier((send(in_factors), turned))
        early = jnp.concatenate([inner, early])
    totals, summed, last = {}, 0, chips - 1

    def sum_to(k, totals, summed):
        for j in range(summed, k):
            totals = step(mine, tokens_of, held[j], pieces[j], totals, j)
        return totals, max(k, summed)

    for s in range(1, chips):
        held.append([late, early])
        pieces.append([(0, 0, rows - lead, "out", lead), (1, rows_in, lead, "out", 0)] + inside)
        if s == last:
            break
        if s >= 4:
            totals, summed = sum_to(min(2 * s - 6, s), totals, summed)
            late, totals = lax.optimization_barrier((late, totals))
            early, totals = lax.optimization_barrier((early, totals))
        late = send(late)
        early = send(early if s < last - 1 else early[rows_in:])

    window = call(
        functools.partial(window_kernel, lead), mine,
        [(x, rows, lambda i, o: (0, o[last])) for x in tokens_of["out"][:2]], [], [],
        [jax.ShapeDtypeStruct((2 * tokens, lead), grads.dtype)], 0, "window",
    )[0]
    totals, window = lax.optimization_barrier((totals, window))
    totals, summed = sum_to(last, totals, summed)
    slots = lengths.shape[0]
    height = (2 * tokens + EXTRA, columns)
    if rows_in:
        inn = call(
            functools.partial(turned_kernel, 1), mine,
            [(x, rows_in, lambda i, o: (0, o[last])) for x in tokens_of["in"][:2]],
            [turned, totals["in"]], [seq_slot, lengths],
            [jax.ShapeDtypeStruct(height, F32)], 4 * tokens * rows_in * columns, "turned",
        )[0]
    else:
        numbers = jnp.concatenate([seq_slot, lengths]).astype(F32)
        inn = jnp.zeros(height, F32).at[:tokens].set(dot(acts, every))
        inn = inn.at[2 * tokens, :2 * slots].set(numbers)
    inn = call(
        masked_kernel, mine, [], [inn, across(inn)], [],
        [jax.ShapeDtypeStruct(height, F32)], 0, "masked",
    )[0]
    totals = step(mine, tokens_of, [late], pieces[last][:1], totals, last)

    queries = columns // RANK
    table = score_table([window, early, totals["out"], inn], slots, devices)
    got = lax.all_to_all(table.reshape(devices, TILE, -1), "dp", 0, 0, tiled=True)
    return jnp.sum(got[:, :slots, :queries], axis=0)


def solution(mesh):
    return jax.shard_map(
        shards,
        mesh=mesh,
        in_specs=(
            P(("groups", "dp"), None),
            P(("groups", "dp"), None),
            P(("groups", "dp"), None),
            P(("groups", "dp"), None),
            P(("groups", "dp")),
            P(("groups", "dp")),
        ),
        out_specs=P(("groups", "dp"), None),
        check_vma=False,
    )
```

```python
import functools
import math

import jax
import jax.numpy as jnp
import numpy as np
from jax import lax
from jax.experimental import pallas as pl
from jax.experimental.pallas import tpu as pltpu
from jax.sharding import PartitionSpec as P

RANK = 32
LEN = 80
F32 = jnp.float32
VMEM = 52 << 20


def ring_of(chips):
    cols = max([d for d in range(1, math.isqrt(chips) + 1) if chips % d == 0 and d % 2 == 0] or [1])
    rows = chips // cols
    if cols == 1 or rows % 2:
        return list(range(chips))
    walk = []
    for r in range(rows):
        line = range(1, cols) if r % 2 == 0 else range(cols - 1, 0, -1)
        walk += [r * cols + c for c in line]
    return walk + [r * cols for r in reversed(range(rows))]


def block_orders(chips):
    ring = ring_of(chips)
    order = np.zeros((2 * chips, chips), np.int32)
    for p, chip in enumerate(ring):
        for s in range(chips):
            order[2 * chip, s] = 2 * ring[(p - s) % chips]
            order[2 * chip + 1, s] = 2 * ring[(p + s) % chips] + 1
    return order


def ring_pairs(chips):
    ring = ring_of(chips)
    pairs = []
    for p, chip in enumerate(ring):
        pairs.append((2 * chip, 2 * ring[(p + 1) % chips]))
        pairs.append((2 * chip + 1, 2 * ring[(p - 1) % chips] + 1))
    return pairs


def dot(a, b):
    return jnp.dot(a, b, preferred_element_type=F32)


def call(kernel, order, windows, whole, scalars, out_shape, flops, name):
    in_specs = [pl.BlockSpec((x.shape[0], w), at) for x, w, at in windows]
    in_specs += [pl.BlockSpec(x.shape, lambda i, o: (0, 0)) for x in whole]
    in_specs += [pl.BlockSpec(memory_space=pltpu.SMEM) for _ in scalars]
    size = sum(2 * x.shape[0] * w for x, w, _ in windows)
    size += sum(x.size * x.dtype.itemsize for x in list(whole) + list(out_shape))
    return pl.pallas_call(
        kernel,
        grid_spec=pltpu.PrefetchScalarGridSpec(
            num_scalar_prefetch=1,
            grid=(1,),
            in_specs=in_specs,
            out_specs=[pl.BlockSpec(x.shape, lambda i, o: (0, 0)) for x in out_shape],
        ),
        out_shape=out_shape,
        cost_estimate=pl.CostEstimate(flops=flops, bytes_accessed=size, transcendentals=0),
        compiler_params=pltpu.CompilerParams(vmem_limit_bytes=VMEM),
        name=name,
    )(order, *[x for x, _, _ in windows], *whole, *scalars)


def step_kernel(pieces, kinds, count, summed, order_ref, *refs):
    windows = {kind: refs[2 * i:2 * i + 2] for i, kind in enumerate(kinds)}
    blocks, refs = refs[2 * len(kinds):2 * len(kinds) + count], refs[2 * len(kinds) + count:]
    tokens = windows[kinds[0]][0].shape[0]
    for i, kind in enumerate(kinds):
        for k in range(2):
            at = pl.ds(k * tokens, tokens)
            total = refs[i][at] if summed else 0.0
            for which, row, height, of, column in pieces:
                if of == kind:
                    window = windows[kind][k][:, column:column + height]
                    total += dot(window, blocks[which][row:row + height])
            refs[i - len(kinds)][at] = total


def step(order, tokens_of, blocks, pieces, totals, s):
    kinds = sorted({piece[3] for piece in pieces})
    windows = []
    for kind in kinds:
        own, sib, width = tokens_of[kind]
        windows += [(x, width, lambda i, o: (0, o[s])) for x in (own, sib)]
    tokens, columns = windows[0][0].shape[0], blocks[0].shape[1]
    summed = all(kind in totals for kind in kinds)
    shape = jax.ShapeDtypeStruct((2 * tokens, columns), F32)
    out = call(
        functools.partial(step_kernel, pieces, kinds, len(blocks), summed),
        order, windows, list(blocks) + ([totals[k] for k in kinds] if summed else []), [],
        [shape] * len(kinds), 4 * tokens * sum(p[2] for p in pieces) * columns, "step",
    )
    return {**totals, **dict(zip(kinds, out))}


def window_kernel(lead, order_ref, own_ref, sib_ref, out_ref):
    tokens = own_ref.shape[0]
    out_ref[:tokens] = own_ref[:, :lead]
    out_ref[tokens:] = sib_ref[:, :lead]


EXTRA = 8


def turned_kernel(count, order_ref, *refs):
    windows, blocks = refs[:2 * count], refs[2 * count:3 * count]
    total_ref, seq_ref, len_ref, out_ref = refs[3 * count:]
    tokens = windows[0].shape[0]
    for k in range(2):
        at = pl.ds(k * tokens, tokens)
        total = total_ref[at]
        for w in range(count):
            total += dot(windows[2 * w + k][...], blocks[w][...])
        out_ref[at] = total
    held = seq_ref.shape[0]
    lane = lax.broadcasted_iota(jnp.int32, (EXTRA, out_ref.shape[1]), 1)
    numbers = jnp.zeros(lane.shape, F32)
    for i in range(held):
        numbers = jnp.where(lane == i, seq_ref[i].astype(F32), numbers)
        numbers = jnp.where(lane == held + i, len_ref[i].astype(F32), numbers)
    out_ref[2 * tokens:] = numbers


def masked_kernel(order_ref, own_ref, got_ref, out_ref):
    tokens = (own_ref.shape[0] - EXTRA) // 2
    columns = own_ref.shape[1]
    held = tokens // LEN
    position = lax.broadcasted_iota(jnp.int32, (LEN, columns), 0).astype(F32)
    for k, (mine, other) in enumerate(((own_ref, got_ref), (got_ref, own_ref))):
        for i in range(held):
            at, across = pl.ds(i * LEN, LEN), pl.ds(tokens + i * LEN, LEN)
            length = mine[2 * tokens:2 * tokens + 1, held + i:held + i + 1]
            out_ref[pl.ds(k * tokens + i * LEN, LEN)] = jnp.where(
                position < length, mine[at] + other[across], 0.0
            )
    lane = lax.broadcasted_iota(jnp.int32, (EXTRA, columns), 1)
    numbers = jnp.zeros(lane.shape, F32)
    for k, ref in enumerate((own_ref, got_ref)):
        for i in range(held):
            slot = ref[2 * tokens:2 * tokens + 1, i:i + 1]
            numbers = jnp.where(lane == k * held + i, slot, numbers)
    out_ref[2 * tokens:] = numbers


def score_kernel(per_device, window_ref, block_ref, total_ref, inn_ref, table_ref):
    height, columns = total_ref.shape
    queries = columns // RANK
    column = lax.broadcasted_iota(jnp.int32, (columns, queries), 0) // RANK
    query = lax.broadcasted_iota(jnp.int32, (columns, queries), 1)
    fold = (column == query).astype(F32)
    row = lax.broadcasted_iota(jnp.int32, table_ref.shape, 0)
    owner = table_ref.shape[0] // per_device - 1 - lax.div(row, per_device)
    row = (owner * per_device + lax.rem(row, per_device)).astype(F32)
    contrib = (total_ref[...] + dot(window_ref[...], block_ref[...])) * inn_ref[:height]
    count = height // LEN
    sums = [jnp.sum(contrib[i * LEN:(i + 1) * LEN], axis=0, keepdims=True) for i in range(count)]
    scores = jnp.dot(
        jnp.concatenate(sums), fold, precision=lax.Precision.HIGHEST, preferred_element_type=F32
    ) * (1.0 / math.sqrt(RANK * LEN))
    table = jnp.zeros(table_ref.shape, F32)
    for i in range(count):
        slot = inn_ref[height:height + 1, i:i + 1]
        table = jnp.where(row == slot, scores[i:i + 1], table)
    table_ref[...] = table


def score_table(arrays, per_device, rows, queries):
    vmem = pl.BlockSpec(memory_space=pltpu.VMEM)
    window, block = arrays[:2]
    size = sum(x.size * x.dtype.itemsize for x in arrays)
    return pl.pallas_call(
        functools.partial(score_kernel, per_device),
        in_specs=[vmem] * len(arrays),
        out_specs=vmem,
        out_shape=jax.ShapeDtypeStruct((rows, queries), F32),
        cost_estimate=pl.CostEstimate(
            flops=2 * window.size * block.shape[1], bytes_accessed=size, transcendentals=0
        ),
        compiler_params=pltpu.CompilerParams(vmem_limit_bytes=16 << 20),
        name="score",
    )(*arrays)


def shards(acts, grads, out_factors, in_factors, seq_slot, lengths):
    devices = lax.axis_size("dp")
    chips = devices // 2
    me = lax.axis_index("dp")
    tokens = grads.shape[0]
    rows, columns = out_factors.shape
    rows_in = in_factors.shape[0]
    orders = jnp.asarray(block_orders(chips))
    mine = lax.dynamic_index_in_dim(orders, me, keepdims=False)
    pairs = ring_pairs(chips)
    swap = [(d, d ^ 1) for d in range(devices)]

    send = lambda x: lax.ppermute(x, "dp", pairs)
    across = lambda x: lax.ppermute(x, "dp", swap)

    every = None
    if rows_in % 128:
        every = lax.all_gather(in_factors, "dp", axis=0, tiled=True)
        rows_in = 0
    lead = (rows - rows_in) // 2
    tokens_of = {"out": (grads, across(grads), rows)}
    if rows_in:
        tokens_of["in"] = (acts, across(acts), rows_in)

    inside = [(1, 0, rows_in, "in", 0)] if rows_in else []
    held = [[out_factors] + [in_factors] * (rows_in > 0)]
    pieces = [[(0, 0, rows, "out", 0)] + inside]
    came = send(out_factors)
    late, early = came[lead:], came[:lead]
    if rows_in:
        came, turned = lax.optimization_barrier((came, in_factors))
        turned = lax.ppermute(turned, "dp", [(j, i) for i, j in pairs])
        late, early = came[lead:], came[:lead]
        inner, turned = lax.optimization_barrier((send(in_factors), turned))
        early = jnp.concatenate([inner, early])
    totals, summed, last = {}, 0, chips - 1

    def sum_to(k, totals, summed):
        for j in range(summed, k):
            totals = step(mine, tokens_of, held[j], pieces[j], totals, j)
        return totals, max(k, summed)

    for s in range(1, chips):
        held.append([late, early])
        pieces.append([(0, 0, rows - lead, "out", lead), (1, rows_in, lead, "out", 0)] + inside)
        if s == last:
            break
        if s >= 4:
            totals, summed = sum_to(min(2 * s - 6, s), totals, summed)
            late, totals = lax.optimization_barrier((late, totals))
            early, totals = lax.optimization_barrier((early, totals))
        late = send(late)
        early = send(early if s < last - 1 else early[rows_in:])

    window = call(
        functools.partial(window_kernel, lead), mine,
        [(x, rows, lambda i, o: (0, o[last])) for x in tokens_of["out"][:2]], [], [],
        [jax.ShapeDtypeStruct((2 * tokens, lead), grads.dtype)], 0, "window",
    )[0]
    totals, window = lax.optimization_barrier((totals, window))
    totals, summed = sum_to(last, totals, summed)
    slots = lengths.shape[0]
    height = (2 * tokens + EXTRA, columns)
    if rows_in:
        inn = call(
            functools.partial(turned_kernel, 1), mine,
            [(x, rows_in, lambda i, o: (0, o[last])) for x in tokens_of["in"][:2]],
            [turned, totals["in"]], [seq_slot, lengths],
            [jax.ShapeDtypeStruct(height, F32)], 4 * tokens * rows_in * columns, "turned",
        )[0]
    else:
        numbers = jnp.concatenate([seq_slot, lengths]).astype(F32)
        inn = jnp.zeros(height, F32).at[:tokens].set(dot(acts, every))
        inn = inn.at[2 * tokens, :2 * slots].set(numbers)
    inn = call(
        masked_kernel, mine, [], [inn, across(inn)], [],
        [jax.ShapeDtypeStruct(height, F32)], 0, "masked",
    )[0]
    totals = step(mine, tokens_of, [late], pieces[last][:1], totals, last)

    queries = columns // RANK
    table = score_table([window, early, totals["out"], inn], slots, slots * devices, queries)
    groups = [list(reversed(range(devices)))]
    got = lax.all_to_all(
        table.reshape(devices, slots, queries), "dp", 0, 0, axis_index_groups=groups, tiled=True
    )
    return jnp.sum(got, axis=0)


def solution(mesh):
    return jax.shard_map(
        shards,
        mesh=mesh,
        in_specs=(
            P(("groups", "dp"), None),
            P(("groups", "dp"), None),
            P(("groups", "dp"), None),
            P(("groups", "dp"), None),
            P(("groups", "dp")),
            P(("groups", "dp")),
        ),
        out_specs=P(("groups", "dp"), None),
        check_vma=False,
    )
```

```python
import functools
import math

import jax
import jax.numpy as jnp
import numpy as np
from jax import lax
from jax.experimental import pallas as pl
from jax.experimental.pallas import tpu as pltpu
from jax.sharding import PartitionSpec as P

RANK = 32
LEN = 80
F32 = jnp.float32
VMEM = 52 << 20


def ring_of(chips):
    cols = max([d for d in range(1, math.isqrt(chips) + 1) if chips % d == 0 and d % 2 == 0] or [1])
    rows = chips // cols
    if cols == 1 or rows % 2:
        return list(range(chips))
    walk = []
    for r in range(rows):
        line = range(1, cols) if r % 2 == 0 else range(cols - 1, 0, -1)
        walk += [r * cols + c for c in line]
    return walk + [r * cols for r in reversed(range(rows))]


def block_orders(chips):
    ring = ring_of(chips)
    order = np.zeros((2 * chips, chips), np.int32)
    for p, chip in enumerate(ring):
        for s in range(chips):
            order[2 * chip, s] = 2 * ring[(p - s) % chips]
            order[2 * chip + 1, s] = 2 * ring[(p + s) % chips] + 1
    return order


def ring_pairs(chips):
    ring = ring_of(chips)
    pairs = []
    for p, chip in enumerate(ring):
        pairs.append((2 * chip, 2 * ring[(p + 1) % chips]))
        pairs.append((2 * chip + 1, 2 * ring[(p - 1) % chips] + 1))
    return pairs


def dot(a, b):
    return jnp.dot(a, b, preferred_element_type=F32)


def call(kernel, order, windows, whole, scalars, out_shape, flops, name):
    in_specs = [pl.BlockSpec((x.shape[0], w), at) for x, w, at in windows]
    in_specs += [pl.BlockSpec(x.shape, lambda i, o: (0, 0)) for x in whole]
    in_specs += [pl.BlockSpec(memory_space=pltpu.SMEM) for _ in scalars]
    size = sum(2 * x.shape[0] * w for x, w, _ in windows)
    size += sum(x.size * x.dtype.itemsize for x in list(whole) + list(out_shape))
    return pl.pallas_call(
        kernel,
        grid_spec=pltpu.PrefetchScalarGridSpec(
            num_scalar_prefetch=1,
            grid=(1,),
            in_specs=in_specs,
            out_specs=[pl.BlockSpec(x.shape, lambda i, o: (0, 0)) for x in out_shape],
        ),
        out_shape=out_shape,
        cost_estimate=pl.CostEstimate(flops=flops, bytes_accessed=size, transcendentals=0),
        compiler_params=pltpu.CompilerParams(vmem_limit_bytes=VMEM),
        name=name,
    )(order, *[x for x, _, _ in windows], *whole, *scalars)


def step_kernel(pieces, kinds, count, summed, order_ref, *refs):
    windows = {kind: refs[2 * i:2 * i + 2] for i, kind in enumerate(kinds)}
    blocks, refs = refs[2 * len(kinds):2 * len(kinds) + count], refs[2 * len(kinds) + count:]
    tokens = windows[kinds[0]][0].shape[0]
    for i, kind in enumerate(kinds):
        for k in range(2):
            at = pl.ds(k * tokens, tokens)
            total = refs[i][at] if summed else 0.0
            for which, row, height, of, column in pieces:
                if of == kind:
                    window = windows[kind][k][:, column:column + height]
                    total += dot(window, blocks[which][row:row + height])
            refs[i - len(kinds)][at] = total


def step(order, tokens_of, blocks, pieces, totals, s):
    kinds = sorted({piece[3] for piece in pieces})
    windows = []
    for kind in kinds:
        own, sib, width = tokens_of[kind]
        windows += [(x, width, lambda i, o: (0, o[s])) for x in (own, sib)]
    tokens, columns = windows[0][0].shape[0], blocks[0].shape[1]
    summed = all(kind in totals for kind in kinds)
    shape = jax.ShapeDtypeStruct((2 * tokens, columns), F32)
    out = call(
        functools.partial(step_kernel, pieces, kinds, len(blocks), summed),
        order, windows, list(blocks) + ([totals[k] for k in kinds] if summed else []), [],
        [shape] * len(kinds), 4 * tokens * sum(p[2] for p in pieces) * columns, "step",
    )
    return {**totals, **dict(zip(kinds, out))}


def window_kernel(lead, order_ref, own_ref, sib_ref, out_ref):
    tokens = own_ref.shape[0]
    out_ref[:tokens] = own_ref[:, :lead]
    out_ref[tokens:] = sib_ref[:, :lead]


EXTRA = 8


def turned_kernel(count, order_ref, *refs):
    windows, blocks = refs[:2 * count], refs[2 * count:3 * count]
    total_ref, seq_ref, len_ref, out_ref = refs[3 * count:]
    tokens = windows[0].shape[0]
    for k in range(2):
        at = pl.ds(k * tokens, tokens)
        total = total_ref[at]
        for w in range(count):
            total += dot(windows[2 * w + k][...], blocks[w][...])
        out_ref[at] = total
    held = seq_ref.shape[0]
    lane = lax.broadcasted_iota(jnp.int32, (EXTRA, out_ref.shape[1]), 1)
    numbers = jnp.zeros(lane.shape, F32)
    for i in range(held):
        numbers = jnp.where(lane == i, seq_ref[i].astype(F32), numbers)
        numbers = jnp.where(lane == held + i, len_ref[i].astype(F32), numbers)
    out_ref[2 * tokens:] = numbers


def masked_kernel(order_ref, own_ref, got_ref, out_ref):
    tokens = (own_ref.shape[0] - EXTRA) // 2
    columns = own_ref.shape[1]
    held = tokens // LEN
    position = lax.broadcasted_iota(jnp.int32, (LEN, columns), 0).astype(F32)
    for k, (mine, other) in enumerate(((own_ref, got_ref), (got_ref, own_ref))):
        for i in range(held):
            at, across = pl.ds(i * LEN, LEN), pl.ds(tokens + i * LEN, LEN)
            length = mine[2 * tokens:2 * tokens + 1, held + i:held + i + 1]
            out_ref[pl.ds(k * tokens + i * LEN, LEN)] = jnp.where(
                position < length, mine[at] + other[across], 0.0
            )
    lane = lax.broadcasted_iota(jnp.int32, (EXTRA, columns), 1)
    numbers = jnp.zeros(lane.shape, F32)
    for k, ref in enumerate((own_ref, got_ref)):
        for i in range(held):
            slot = ref[2 * tokens:2 * tokens + 1, i:i + 1]
            numbers = jnp.where(lane == k * held + i, slot, numbers)
    out_ref[2 * tokens:] = numbers


def score_kernel(per_device, window_ref, block_ref, total_ref, inn_ref, table_ref):
    height, columns = total_ref.shape
    queries = columns // RANK
    column = lax.broadcasted_iota(jnp.int32, (columns, queries), 0) // RANK
    query = lax.broadcasted_iota(jnp.int32, (columns, queries), 1)
    fold = (column == query).astype(F32)
    row = lax.broadcasted_iota(jnp.int32, table_ref.shape, 0)
    owner = table_ref.shape[0] // per_device - 1 - lax.div(row, per_device)
    row = (owner * per_device + lax.rem(row, per_device)).astype(F32)
    contrib = (total_ref[...] + dot(window_ref[...], block_ref[...])) * inn_ref[:height]
    count = height // LEN
    sums = [jnp.sum(contrib[i * LEN:(i + 1) * LEN], axis=0, keepdims=True) for i in range(count)]
    scores = jnp.dot(
        jnp.concatenate(sums), fold, precision=lax.Precision.HIGHEST, preferred_element_type=F32
    ) * (1.0 / math.sqrt(RANK * LEN))
    table = jnp.zeros(table_ref.shape, F32)
    for i in range(count):
        slot = inn_ref[height:height + 1, i:i + 1]
        table = jnp.where(row == slot, scores[i:i + 1], table)
    table_ref[...] = table


def score_table(arrays, per_device, rows, queries):
    vmem = pl.BlockSpec(memory_space=pltpu.VMEM)
    window, block = arrays[:2]
    size = sum(x.size * x.dtype.itemsize for x in arrays)
    return pl.pallas_call(
        functools.partial(score_kernel, per_device),
        in_specs=[vmem] * len(arrays),
        out_specs=vmem,
        out_shape=jax.ShapeDtypeStruct((rows, queries), F32),
        cost_estimate=pl.CostEstimate(
            flops=2 * window.size * block.shape[1], bytes_accessed=size, transcendentals=0
        ),
        compiler_params=pltpu.CompilerParams(vmem_limit_bytes=16 << 20),
        name="score",
    )(*arrays)


def shards(acts, grads, out_factors, in_factors, seq_slot, lengths):
    devices = lax.axis_size("dp")
    chips = devices // 2
    me = lax.axis_index("dp")
    tokens = grads.shape[0]
    rows, columns = out_factors.shape
    rows_in = in_factors.shape[0]
    orders = jnp.asarray(block_orders(chips))
    mine = lax.dynamic_index_in_dim(orders, me, keepdims=False)
    pairs = ring_pairs(chips)
    swap = [(d, d ^ 1) for d in range(devices)]

    send = lambda x: lax.ppermute(x, "dp", pairs)
    across = lambda x: lax.ppermute(x, "dp", swap)

    every = None
    if rows_in % 128:
        every = lax.all_gather(in_factors, "dp", axis=0, tiled=True)
        rows_in = 0
    lead = (rows - rows_in) // 2
    tokens_of = {"out": (grads, across(grads), rows)}
    if rows_in:
        tokens_of["in"] = (acts, across(acts), rows_in)

    inside = [(1, 0, rows_in, "in", 0)] if rows_in else []
    held = [[out_factors] + [in_factors] * (rows_in > 0)]
    pieces = [[(0, 0, rows, "out", 0)] + inside]
    came = send(out_factors)
    late, early = came[lead:], came[:lead]
    if rows_in:
        came, turned = lax.optimization_barrier((came, in_factors))
        turned = lax.ppermute(turned, "dp", [(j, i) for i, j in pairs])
        late, early = came[lead:], came[:lead]
        inner, turned = lax.optimization_barrier((send(in_factors), turned))
        early = jnp.concatenate([inner, early])
        backward = [(j, i) for i, j in pairs]
        turned = [turned, lax.ppermute(turned, "dp", backward)]
    totals, summed, last = {}, 0, chips - 1

    def sum_to(k, totals, summed):
        for j in range(summed, k):
            totals = step(mine, tokens_of, held[j], pieces[j], totals, j)
        return totals, max(k, summed)

    for s in range(1, chips):
        held.append([late, early])
        top = rows_in if s < last - 1 else 0
        pieces.append([(0, 0, rows - lead, "out", lead), (1, top, lead, "out", 0)])
        pieces[s] += inside if top else []
        if s == last:
            break
        if s >= 4:
            totals, summed = sum_to(min(2 * s - 6, s), totals, summed)
            late, totals = lax.optimization_barrier((late, totals))
            early, totals = lax.optimization_barrier((early, totals))
        if s == 3 and rows_in:
            early, turned = lax.optimization_barrier((early, turned))
        late = send(late)
        early = send(early[rows_in:] if s == last - 2 else early)

    window = call(
        functools.partial(window_kernel, lead), mine,
        [(x, rows, lambda i, o: (0, o[last])) for x in tokens_of["out"][:2]], [], [],
        [jax.ShapeDtypeStruct((2 * tokens, lead), grads.dtype)], 0, "window",
    )[0]
    totals, window = lax.optimization_barrier((totals, window))
    totals, summed = sum_to(last, totals, summed)
    slots = lengths.shape[0]
    height = (2 * tokens + EXTRA, columns)
    if rows_in:
        inn = call(
            functools.partial(turned_kernel, 2), mine,
            [
                (x, rows_in, functools.partial(lambda i, o, k: (0, o[k]), k=last - k))
                for k in (0, 1) for x in tokens_of["in"][:2]
            ],
            turned + [totals["in"]], [seq_slot, lengths],
            [jax.ShapeDtypeStruct(height, F32)], 8 * tokens * rows_in * columns, "turned",
        )[0]
    else:
        numbers = jnp.concatenate([seq_slot, lengths]).astype(F32)
        inn = jnp.zeros(height, F32).at[:tokens].set(dot(acts, every))
        inn = inn.at[2 * tokens, :2 * slots].set(numbers)
    inn = call(
        masked_kernel, mine, [], [inn, across(inn)], [],
        [jax.ShapeDtypeStruct(height, F32)], 0, "masked",
    )[0]
    totals = step(mine, tokens_of, [late], pieces[last][:1], totals, last)

    queries = columns // RANK
    table = score_table([window, early, totals["out"], inn], slots, slots * devices, queries)
    groups = [list(reversed(range(devices)))]
    got = lax.all_to_all(
        table.reshape(devices, slots, queries), "dp", 0, 0, axis_index_groups=groups, tiled=True
    )
    return jnp.sum(got, axis=0)


def solution(mesh):
    return jax.shard_map(
        shards,
        mesh=mesh,
        in_specs=(
            P(("groups", "dp"), None),
            P(("groups", "dp"), None),
            P(("groups", "dp"), None),
            P(("groups", "dp"), None),
            P(("groups", "dp")),
            P(("groups", "dp")),
        ),
        out_specs=P(("groups", "dp"), None),
        check_vma=False,
    )
```

```python
import functools
import math

import jax
import jax.numpy as jnp
import numpy as np
from jax import lax
from jax.experimental import pallas as pl
from jax.experimental.pallas import tpu as pltpu
from jax.sharding import PartitionSpec as P

RANK = 32
LEN = 80
F32 = jnp.float32
VMEM = 52 << 20


def ring_of(chips):
    cols = max([d for d in range(1, math.isqrt(chips) + 1) if chips % d == 0 and d % 2 == 0] or [1])
    rows = chips // cols
    if cols == 1 or rows % 2:
        return list(range(chips))
    walk = []
    for r in range(rows):
        line = range(1, cols) if r % 2 == 0 else range(cols - 1, 0, -1)
        walk += [r * cols + c for c in line]
    return walk + [r * cols for r in reversed(range(rows))]


def block_orders(chips):
    ring = ring_of(chips)
    order = np.zeros((2 * chips, chips), np.int32)
    for p, chip in enumerate(ring):
        for s in range(chips):
            order[2 * chip, s] = 2 * ring[(p - s) % chips]
            order[2 * chip + 1, s] = 2 * ring[(p + s) % chips] + 1
    return order


def ring_pairs(chips):
    ring = ring_of(chips)
    pairs = []
    for p, chip in enumerate(ring):
        pairs.append((2 * chip, 2 * ring[(p + 1) % chips]))
        pairs.append((2 * chip + 1, 2 * ring[(p - 1) % chips] + 1))
    return pairs


def dot(a, b):
    return jnp.dot(a, b, preferred_element_type=F32)


def call(kernel, order, windows, whole, scalars, out_shape, flops, name):
    in_specs = [pl.BlockSpec((x.shape[0], w), at) for x, w, at in windows]
    in_specs += [pl.BlockSpec(x.shape, lambda i, o: (0, 0)) for x in whole]
    in_specs += [pl.BlockSpec(memory_space=pltpu.SMEM) for _ in scalars]
    size = sum(2 * x.shape[0] * w for x, w, _ in windows)
    size += sum(x.size * x.dtype.itemsize for x in list(whole) + list(out_shape))
    return pl.pallas_call(
        kernel,
        grid_spec=pltpu.PrefetchScalarGridSpec(
            num_scalar_prefetch=1,
            grid=(1,),
            in_specs=in_specs,
            out_specs=[pl.BlockSpec(x.shape, lambda i, o: (0, 0)) for x in out_shape],
        ),
        out_shape=out_shape,
        cost_estimate=pl.CostEstimate(flops=flops, bytes_accessed=size, transcendentals=0),
        compiler_params=pltpu.CompilerParams(vmem_limit_bytes=VMEM),
        name=name,
    )(order, *[x for x, _, _ in windows], *whole, *scalars)


def step_kernel(pieces, kinds, count, summed, order_ref, *refs):
    windows = {kind: refs[2 * i:2 * i + 2] for i, kind in enumerate(kinds)}
    blocks, refs = refs[2 * len(kinds):2 * len(kinds) + count], refs[2 * len(kinds) + count:]
    tokens = windows[kinds[0]][0].shape[0]
    for i, kind in enumerate(kinds):
        for k in range(2):
            at = pl.ds(k * tokens, tokens)
            total = refs[i][at] if summed else 0.0
            for which, row, height, of, column in pieces:
                if of == kind:
                    window = windows[kind][k][:, column:column + height]
                    total += dot(window, blocks[which][row:row + height])
            refs[i - len(kinds)][at] = total


def step(order, tokens_of, blocks, pieces, totals, s):
    kinds = sorted({piece[3] for piece in pieces})
    windows = []
    for kind in kinds:
        own, sib, width = tokens_of[kind]
        windows += [(x, width, lambda i, o: (0, o[s])) for x in (own, sib)]
    tokens, columns = windows[0][0].shape[0], blocks[0].shape[1]
    summed = all(kind in totals for kind in kinds)
    shape = jax.ShapeDtypeStruct((2 * tokens, columns), F32)
    out = call(
        functools.partial(step_kernel, pieces, kinds, len(blocks), summed),
        order, windows, list(blocks) + ([totals[k] for k in kinds] if summed else []), [],
        [shape] * len(kinds), 4 * tokens * sum(p[2] for p in pieces) * columns, "step",
    )
    return {**totals, **dict(zip(kinds, out))}


def window_kernel(lead, order_ref, own_ref, sib_ref, out_ref):
    tokens = own_ref.shape[0]
    out_ref[:tokens] = own_ref[:, :lead]
    out_ref[tokens:] = sib_ref[:, :lead]


EXTRA = 8


def turned_kernel(count, order_ref, *refs):
    windows, blocks = refs[:2 * count], refs[2 * count:3 * count]
    total_ref, seq_ref, len_ref, out_ref = refs[3 * count:]
    tokens = windows[0].shape[0]
    for k in range(2):
        at = pl.ds(k * tokens, tokens)
        total = total_ref[at]
        for w in range(count):
            total += dot(windows[2 * w + k][...], blocks[w][...])
        out_ref[at] = total
    held = seq_ref.shape[0]
    lane = lax.broadcasted_iota(jnp.int32, (EXTRA, out_ref.shape[1]), 1)
    numbers = jnp.zeros(lane.shape, F32)
    for i in range(held):
        numbers = jnp.where(lane == i, seq_ref[i].astype(F32), numbers)
        numbers = jnp.where(lane == held + i, len_ref[i].astype(F32), numbers)
    out_ref[2 * tokens:] = numbers


def masked_kernel(order_ref, own_ref, got_ref, out_ref):
    tokens = (own_ref.shape[0] - EXTRA) // 2
    columns = own_ref.shape[1]
    held = tokens // LEN
    position = lax.broadcasted_iota(jnp.int32, (LEN, columns), 0).astype(F32)
    for k, (mine, other) in enumerate(((own_ref, got_ref), (got_ref, own_ref))):
        for i in range(held):
            at, across = pl.ds(i * LEN, LEN), pl.ds(tokens + i * LEN, LEN)
            length = mine[2 * tokens:2 * tokens + 1, held + i:held + i + 1]
            out_ref[pl.ds(k * tokens + i * LEN, LEN)] = jnp.where(
                position < length, mine[at] + other[across], 0.0
            )
    lane = lax.broadcasted_iota(jnp.int32, (EXTRA, columns), 1)
    numbers = jnp.zeros(lane.shape, F32)
    for k, ref in enumerate((own_ref, got_ref)):
        for i in range(held):
            slot = ref[2 * tokens:2 * tokens + 1, i:i + 1]
            numbers = jnp.where(lane == k * held + i, slot, numbers)
    out_ref[2 * tokens:] = numbers


def score_kernel(per_device, window_ref, block_ref, total_ref, inn_ref, table_ref):
    height, columns = total_ref.shape
    queries = columns // RANK
    column = lax.broadcasted_iota(jnp.int32, (columns, queries), 0) // RANK
    query = lax.broadcasted_iota(jnp.int32, (columns, queries), 1)
    fold = (column == query).astype(F32)
    row = lax.broadcasted_iota(jnp.int32, table_ref.shape, 0)
    owner = table_ref.shape[0] // per_device - 1 - lax.div(row, per_device)
    row = (owner * per_device + lax.rem(row, per_device)).astype(F32)
    contrib = (total_ref[...] + dot(window_ref[...], block_ref[...])) * inn_ref[:height]
    count = height // LEN
    sums = [jnp.sum(contrib[i * LEN:(i + 1) * LEN], axis=0, keepdims=True) for i in range(count)]
    scores = jnp.dot(
        jnp.concatenate(sums), fold, precision=lax.Precision.HIGHEST, preferred_element_type=F32
    ) * (1.0 / math.sqrt(RANK * LEN))
    table = jnp.zeros(table_ref.shape, F32)
    for i in range(count):
        slot = inn_ref[height:height + 1, i:i + 1]
        table = jnp.where(row == slot, scores[i:i + 1], table)
    table_ref[...] = table


def score_table(arrays, per_device, rows, queries):
    vmem = pl.BlockSpec(memory_space=pltpu.VMEM)
    window, block = arrays[:2]
    size = sum(x.size * x.dtype.itemsize for x in arrays)
    return pl.pallas_call(
        functools.partial(score_kernel, per_device),
        in_specs=[vmem] * len(arrays),
        out_specs=vmem,
        out_shape=jax.ShapeDtypeStruct((rows, queries), F32),
        cost_estimate=pl.CostEstimate(
            flops=2 * window.size * block.shape[1], bytes_accessed=size, transcendentals=0
        ),
        compiler_params=pltpu.CompilerParams(vmem_limit_bytes=16 << 20),
        name="score",
    )(*arrays)


def shards(acts, grads, out_factors, in_factors, seq_slot, lengths):
    devices = lax.axis_size("dp")
    chips = devices // 2
    me = lax.axis_index("dp")
    tokens = grads.shape[0]
    rows, columns = out_factors.shape
    rows_in = in_factors.shape[0]
    orders = jnp.asarray(block_orders(chips))
    mine = lax.dynamic_index_in_dim(orders, me, keepdims=False)
    pairs = ring_pairs(chips)
    swap = [(d, d ^ 1) for d in range(devices)]

    send = lambda x: lax.ppermute(x, "dp", pairs)
    across = lambda x: lax.ppermute(x, "dp", swap)

    every = None
    if rows_in % 128:
        every = lax.all_gather(in_factors, "dp", axis=0, tiled=True)
        rows_in = 0
    lead = (rows - rows_in) // 2
    tokens_of = {"out": (grads, across(grads), rows)}
    if rows_in:
        tokens_of["in"] = (acts, across(acts), rows_in)

    inside = [(1, 0, rows_in, "in", 0)] if rows_in else []
    held = [[out_factors] + [in_factors] * (rows_in > 0)]
    pieces = [[(0, 0, rows, "out", 0)] + inside]
    came = send(out_factors)
    late, early = came[lead:], came[:lead]
    if rows_in:
        came, turned = lax.optimization_barrier((came, in_factors))
        turned = lax.ppermute(turned, "dp", [(j, i) for i, j in pairs])
        late, early = came[lead:], came[:lead]
        inner, turned = lax.optimization_barrier((send(in_factors), turned))
        early = jnp.concatenate([inner, early])
        backward = [(j, i) for i, j in pairs]
        turned = [turned, lax.ppermute(turned, "dp", backward)]
    totals, summed, last = {}, 0, chips - 1

    def sum_to(k, totals, summed):
        for j in range(summed, k):
            totals = step(mine, tokens_of, held[j], pieces[j], totals, j)
        return totals, max(k, summed)

    window = call(
        functools.partial(window_kernel, lead), mine,
        [(x, rows, lambda i, o: (0, o[last])) for x in tokens_of["out"][:2]], [], [],
        [jax.ShapeDtypeStruct((2 * tokens, lead), grads.dtype)], 0, "window",
    )[0]

    for s in range(1, chips):
        held.append([late, early])
        top = rows_in if s < last - 1 else 0
        pieces.append([(0, 0, rows - lead, "out", lead), (1, top, lead, "out", 0)])
        pieces[s] += inside if top else []
        if s == last:
            break
        if s >= 4:
            totals, summed = sum_to(min(2 * s - 6, s), totals, summed)
            late, totals = lax.optimization_barrier((late, totals))
            early, totals = lax.optimization_barrier((early, totals))
        if s == 3 and rows_in:
            early, turned = lax.optimization_barrier((early, turned))
        late = send(late)
        if s == last - 1:
            early, window = lax.optimization_barrier((early, window))
        early = send(early[rows_in:] if s == last - 2 else early)

    totals, summed = sum_to(last, totals, summed)
    slots = lengths.shape[0]
    height = (2 * tokens + EXTRA, columns)
    if rows_in:
        inn = call(
            functools.partial(turned_kernel, 2), mine,
            [
                (x, rows_in, functools.partial(lambda i, o, k: (0, o[k]), k=last - k))
                for k in (0, 1) for x in tokens_of["in"][:2]
            ],
            turned + [totals["in"]], [seq_slot, lengths],
            [jax.ShapeDtypeStruct(height, F32)], 8 * tokens * rows_in * columns, "turned",
        )[0]
    else:
        numbers = jnp.concatenate([seq_slot, lengths]).astype(F32)
        inn = jnp.zeros(height, F32).at[:tokens].set(dot(acts, every))
        inn = inn.at[2 * tokens, :2 * slots].set(numbers)
    inn = call(
        masked_kernel, mine, [], [inn, across(inn)], [],
        [jax.ShapeDtypeStruct(height, F32)], 0, "masked",
    )[0]
    totals = step(mine, tokens_of, [late], pieces[last][:1], totals, last)

    queries = columns // RANK
    table = score_table([window, early, totals["out"], inn], slots, slots * devices, queries)
    groups = [list(reversed(range(devices)))]
    got = lax.all_to_all(
        table.reshape(devices, slots, queries), "dp", 0, 0, axis_index_groups=groups, tiled=True
    )
    return jnp.sum(got, axis=0)


def solution(mesh):
    return jax.shard_map(
        shards,
        mesh=mesh,
        in_specs=(
            P(("groups", "dp"), None),
            P(("groups", "dp"), None),
            P(("groups", "dp"), None),
            P(("groups", "dp"), None),
            P(("groups", "dp")),
            P(("groups", "dp")),
        ),
        out_specs=P(("groups", "dp"), None),
        check_vma=False,
    )
```

```python
import functools
import math

import jax
import jax.numpy as jnp
import numpy as np
from jax import lax
from jax.experimental import pallas as pl
from jax.experimental.pallas import tpu as pltpu
from jax.sharding import PartitionSpec as P

RANK = 32
LEN = 80
F32 = jnp.float32
VMEM = 52 << 20


def ring_of(chips):
    cols = max([d for d in range(1, math.isqrt(chips) + 1) if chips % d == 0 and d % 2 == 0] or [1])
    rows = chips // cols
    if cols == 1 or rows % 2:
        return list(range(chips))
    walk = []
    for r in range(rows):
        line = range(1, cols) if r % 2 == 0 else range(cols - 1, 0, -1)
        walk += [r * cols + c for c in line]
    return walk + [r * cols for r in reversed(range(rows))]


def block_orders(chips):
    ring = ring_of(chips)
    order = np.zeros((2 * chips, chips), np.int32)
    for p, chip in enumerate(ring):
        for s in range(chips):
            order[2 * chip, s] = 2 * ring[(p - s) % chips]
            order[2 * chip + 1, s] = 2 * ring[(p + s) % chips] + 1
    return order


def ring_pairs(chips):
    ring = ring_of(chips)
    pairs = []
    for p, chip in enumerate(ring):
        pairs.append((2 * chip, 2 * ring[(p + 1) % chips]))
        pairs.append((2 * chip + 1, 2 * ring[(p - 1) % chips] + 1))
    return pairs


def dot(a, b):
    return jnp.dot(a, b, preferred_element_type=F32)


def call(kernel, order, windows, whole, scalars, out_shape, flops, name):
    in_specs = [pl.BlockSpec((x.shape[0], w), at) for x, w, at in windows]
    in_specs += [pl.BlockSpec(x.shape, lambda i, o: (0, 0)) for x in whole]
    in_specs += [pl.BlockSpec(memory_space=pltpu.SMEM) for _ in scalars]
    size = sum(2 * x.shape[0] * w for x, w, _ in windows)
    size += sum(x.size * x.dtype.itemsize for x in list(whole) + list(out_shape))
    return pl.pallas_call(
        kernel,
        grid_spec=pltpu.PrefetchScalarGridSpec(
            num_scalar_prefetch=1,
            grid=(1,),
            in_specs=in_specs,
            out_specs=[pl.BlockSpec(x.shape, lambda i, o: (0, 0)) for x in out_shape],
        ),
        out_shape=out_shape,
        cost_estimate=pl.CostEstimate(flops=flops, bytes_accessed=size, transcendentals=0),
        compiler_params=pltpu.CompilerParams(vmem_limit_bytes=VMEM),
        name=name,
    )(order, *[x for x, _, _ in windows], *whole, *scalars)


def step_kernel(pieces, kinds, count, summed, order_ref, *refs):
    windows = {kind: refs[2 * i:2 * i + 2] for i, kind in enumerate(kinds)}
    blocks, refs = refs[2 * len(kinds):2 * len(kinds) + count], refs[2 * len(kinds) + count:]
    tokens = windows[kinds[0]][0].shape[0]
    for i, kind in enumerate(kinds):
        for k in range(2):
            at = pl.ds(k * tokens, tokens)
            total = refs[i][at] if summed else 0.0
            for which, row, height, of, column in pieces:
                if of == kind:
                    window = windows[kind][k][:, column:column + height]
                    total += dot(window, blocks[which][row:row + height])
            refs[i - len(kinds)][at] = total


def step(order, tokens_of, blocks, pieces, totals, s):
    kinds = sorted({piece[3] for piece in pieces})
    windows = []
    for kind in kinds:
        own, sib, width = tokens_of[kind]
        windows += [(x, width, lambda i, o: (0, o[s])) for x in (own, sib)]
    tokens, columns = windows[0][0].shape[0], blocks[0].shape[1]
    summed = all(kind in totals for kind in kinds)
    shape = jax.ShapeDtypeStruct((2 * tokens, columns), F32)
    out = call(
        functools.partial(step_kernel, pieces, kinds, len(blocks), summed),
        order, windows, list(blocks) + ([totals[k] for k in kinds] if summed else []), [],
        [shape] * len(kinds), 4 * tokens * sum(p[2] for p in pieces) * columns, "step",
    )
    return {**totals, **dict(zip(kinds, out))}


def window_kernel(lead, order_ref, own_ref, sib_ref, out_ref):
    tokens = own_ref.shape[0]
    out_ref[:tokens] = own_ref[:, :lead]
    out_ref[tokens:] = sib_ref[:, :lead]


EXTRA = 8


def turned_kernel(count, order_ref, *refs):
    windows, blocks = refs[:2 * count], refs[2 * count:3 * count]
    total_ref, seq_ref, len_ref, out_ref = refs[3 * count:]
    tokens = windows[0].shape[0]
    for k in range(2):
        at = pl.ds(k * tokens, tokens)
        total = total_ref[at]
        for w in range(count):
            total += dot(windows[2 * w + k][...], blocks[w][...])
        out_ref[at] = total
    held = seq_ref.shape[0]
    lane = lax.broadcasted_iota(jnp.int32, (EXTRA, out_ref.shape[1]), 1)
    numbers = jnp.zeros(lane.shape, F32)
    for i in range(held):
        numbers = jnp.where(lane == i, seq_ref[i].astype(F32), numbers)
        numbers = jnp.where(lane == held + i, len_ref[i].astype(F32), numbers)
    out_ref[2 * tokens:] = numbers


def masked_kernel(order_ref, own_ref, got_ref, out_ref):
    tokens = (own_ref.shape[0] - EXTRA) // 2
    columns = own_ref.shape[1]
    held = tokens // LEN
    position = lax.broadcasted_iota(jnp.int32, (LEN, columns), 0).astype(F32)
    for k, (mine, other) in enumerate(((own_ref, got_ref), (got_ref, own_ref))):
        for i in range(held):
            at, across = pl.ds(i * LEN, LEN), pl.ds(tokens + i * LEN, LEN)
            length = mine[2 * tokens:2 * tokens + 1, held + i:held + i + 1]
            out_ref[pl.ds(k * tokens + i * LEN, LEN)] = jnp.where(
                position < length, mine[at] + other[across], 0.0
            )
    lane = lax.broadcasted_iota(jnp.int32, (EXTRA, columns), 1)
    numbers = jnp.zeros(lane.shape, F32)
    for k, ref in enumerate((own_ref, got_ref)):
        for i in range(held):
            slot = ref[2 * tokens:2 * tokens + 1, i:i + 1]
            numbers = jnp.where(lane == k * held + i, slot, numbers)
    out_ref[2 * tokens:] = numbers


def score_kernel(per_device, window_ref, block_ref, total_ref, inn_ref, table_ref):
    height, columns = total_ref.shape
    queries = columns // RANK
    column = lax.broadcasted_iota(jnp.int32, (columns, queries), 0) // RANK
    query = lax.broadcasted_iota(jnp.int32, (columns, queries), 1)
    fold = (column == query).astype(F32)
    row = lax.broadcasted_iota(jnp.int32, table_ref.shape, 0)
    owner = table_ref.shape[0] // per_device - 1 - lax.div(row, per_device)
    row = (owner * per_device + lax.rem(row, per_device)).astype(F32)
    contrib = (total_ref[...] + dot(window_ref[...], block_ref[...])) * inn_ref[:height]
    count = height // LEN
    sums = [jnp.sum(contrib[i * LEN:(i + 1) * LEN], axis=0, keepdims=True) for i in range(count)]
    scores = jnp.dot(
        jnp.concatenate(sums), fold, precision=lax.Precision.HIGHEST, preferred_element_type=F32
    ) * (1.0 / math.sqrt(RANK * LEN))
    table = jnp.zeros(table_ref.shape, F32)
    for i in range(count):
        slot = inn_ref[height:height + 1, i:i + 1]
        table = jnp.where(row == slot, scores[i:i + 1], table)
    table_ref[...] = table


def score_table(arrays, per_device, rows, queries):
    vmem = pl.BlockSpec(memory_space=pltpu.VMEM)
    window, block = arrays[:2]
    size = sum(x.size * x.dtype.itemsize for x in arrays)
    return pl.pallas_call(
        functools.partial(score_kernel, per_device),
        in_specs=[vmem] * len(arrays),
        out_specs=vmem,
        out_shape=jax.ShapeDtypeStruct((rows, queries), F32),
        cost_estimate=pl.CostEstimate(
            flops=2 * window.size * block.shape[1], bytes_accessed=size, transcendentals=0
        ),
        compiler_params=pltpu.CompilerParams(vmem_limit_bytes=16 << 20),
        name="score",
    )(*arrays)


def shards(acts, grads, out_factors, in_factors, seq_slot, lengths):
    devices = lax.axis_size("dp")
    chips = devices // 2
    me = lax.axis_index("dp")
    tokens = grads.shape[0]
    rows, columns = out_factors.shape
    rows_in = in_factors.shape[0]
    orders = jnp.asarray(block_orders(chips))
    mine = lax.dynamic_index_in_dim(orders, me, keepdims=False)
    pairs = ring_pairs(chips)
    swap = [(d, d ^ 1) for d in range(devices)]

    send = lambda x: lax.ppermute(x, "dp", pairs)
    across = lambda x: lax.ppermute(x, "dp", swap)

    every = None
    if rows_in % 128:
        every = lax.all_gather(in_factors, "dp", axis=0, tiled=True)
        rows_in = 0
    lead = (rows - rows_in) // 2
    tokens_of = {"out": (grads, across(grads), rows)}
    if rows_in:
        tokens_of["in"] = (acts, across(acts), rows_in)

    inside = [(1, 0, rows_in, "in", 0)] if rows_in else []
    held = [[out_factors] + [in_factors] * (rows_in > 0)]
    pieces = [[(0, 0, rows, "out", 0)] + inside]
    came = send(out_factors)
    late, early = came[lead:], came[:lead]
    if rows_in:
        came, turned = lax.optimization_barrier((came, in_factors))
        turned = lax.ppermute(turned, "dp", [(j, i) for i, j in pairs])
        late, early = came[lead:], came[:lead]
        inner, turned = lax.optimization_barrier((send(in_factors), turned))
        early = jnp.concatenate([inner, early])
        backward = [(j, i) for i, j in pairs]
        turned = [turned, lax.ppermute(turned, "dp", backward)]
    totals, summed, last = {}, 0, chips - 1

    def sum_to(k, totals, summed):
        for j in range(summed, k):
            totals = step(mine, tokens_of, held[j], pieces[j], totals, j)
        return totals, max(k, summed)

    window = call(
        functools.partial(window_kernel, lead), mine,
        [(x, rows, lambda i, o: (0, o[last])) for x in tokens_of["out"][:2]], [], [],
        [jax.ShapeDtypeStruct((2 * tokens, lead), grads.dtype)], 0, "window",
    )[0]

    for s in range(1, chips):
        held.append([late, early])
        top = rows_in if s < last - 1 else 0
        pieces.append([(0, 0, rows - lead, "out", lead), (1, top, lead, "out", 0)])
        pieces[s] += inside if top else []
        if s == last:
            break
        if s >= 4:
            totals, summed = sum_to(min(2 * s - 6, s), totals, summed)
            late, totals = lax.optimization_barrier((late, totals))
            early, totals = lax.optimization_barrier((early, totals))
        if s == 4 and rows_in:
            early, turned = lax.optimization_barrier((early, turned))
        late = send(late)
        if s == last - 1:
            early, window = lax.optimization_barrier((early, window))
        early = send(early[rows_in:] if s == last - 2 else early)

    totals, summed = sum_to(last, totals, summed)
    slots = lengths.shape[0]
    height = (2 * tokens + EXTRA, columns)
    if rows_in:
        inn = call(
            functools.partial(turned_kernel, 2), mine,
            [
                (x, rows_in, functools.partial(lambda i, o, k: (0, o[k]), k=last - k))
                for k in (0, 1) for x in tokens_of["in"][:2]
            ],
            turned + [totals["in"]], [seq_slot, lengths],
            [jax.ShapeDtypeStruct(height, F32)], 8 * tokens * rows_in * columns, "turned",
        )[0]
    else:
        numbers = jnp.concatenate([seq_slot, lengths]).astype(F32)
        inn = jnp.zeros(height, F32).at[:tokens].set(dot(acts, every))
        inn = inn.at[2 * tokens, :2 * slots].set(numbers)
    inn = call(
        masked_kernel, mine, [], [inn, across(inn)], [],
        [jax.ShapeDtypeStruct(height, F32)], 0, "masked",
    )[0]
    totals = step(mine, tokens_of, [late], pieces[last][:1], totals, last)

    queries = columns // RANK
    table = score_table([window, early, totals["out"], inn], slots, slots * devices, queries)
    groups = [list(reversed(range(devices)))]
    got = lax.all_to_all(
        table.reshape(devices, slots, queries), "dp", 0, 0, axis_index_groups=groups, tiled=True
    )
    return jnp.sum(got, axis=0)


def solution(mesh):
    return jax.shard_map(
        shards,
        mesh=mesh,
        in_specs=(
            P(("groups", "dp"), None),
            P(("groups", "dp"), None),
            P(("groups", "dp"), None),
            P(("groups", "dp"), None),
            P(("groups", "dp")),
            P(("groups", "dp")),
        ),
        out_specs=P(("groups", "dp"), None),
        check_vma=False,
    )
```

```python
import functools
import math

import jax
import jax.numpy as jnp
import numpy as np
from jax import lax
from jax.experimental import pallas as pl
from jax.experimental.pallas import tpu as pltpu
from jax.sharding import PartitionSpec as P

RANK = 32
LEN = 80
F32 = jnp.float32
VMEM = 52 << 20


def ring_of(chips):
    cols = max([d for d in range(1, math.isqrt(chips) + 1) if chips % d == 0 and d % 2 == 0] or [1])
    rows = chips // cols
    if cols == 1 or rows % 2:
        return list(range(chips))
    walk = []
    for r in range(rows):
        line = range(1, cols) if r % 2 == 0 else range(cols - 1, 0, -1)
        walk += [r * cols + c for c in line]
    return walk + [r * cols for r in reversed(range(rows))]


def block_orders(chips):
    ring = ring_of(chips)
    order = np.zeros((2 * chips, chips), np.int32)
    for p, chip in enumerate(ring):
        for s in range(chips):
            order[2 * chip, s] = 2 * ring[(p - s) % chips]
            order[2 * chip + 1, s] = 2 * ring[(p + s) % chips] + 1
    return order


def ring_pairs(chips):
    ring = ring_of(chips)
    pairs = []
    for p, chip in enumerate(ring):
        pairs.append((2 * chip, 2 * ring[(p + 1) % chips]))
        pairs.append((2 * chip + 1, 2 * ring[(p - 1) % chips] + 1))
    return pairs


def dot(a, b):
    return jnp.dot(a, b, preferred_element_type=F32)


def call(kernel, order, windows, whole, scalars, out_shape, flops, name):
    in_specs = [pl.BlockSpec((x.shape[0], w), at) for x, w, at in windows]
    in_specs += [pl.BlockSpec(x.shape, lambda i, o: (0, 0)) for x in whole]
    in_specs += [pl.BlockSpec(memory_space=pltpu.SMEM) for _ in scalars]
    size = sum(2 * x.shape[0] * w for x, w, _ in windows)
    size += sum(x.size * x.dtype.itemsize for x in list(whole) + list(out_shape))
    return pl.pallas_call(
        kernel,
        grid_spec=pltpu.PrefetchScalarGridSpec(
            num_scalar_prefetch=1,
            grid=(1,),
            in_specs=in_specs,
            out_specs=[pl.BlockSpec(x.shape, lambda i, o: (0, 0)) for x in out_shape],
        ),
        out_shape=out_shape,
        cost_estimate=pl.CostEstimate(flops=flops, bytes_accessed=size, transcendentals=0),
        compiler_params=pltpu.CompilerParams(vmem_limit_bytes=VMEM),
        name=name,
    )(order, *[x for x, _, _ in windows], *whole, *scalars)


def step_kernel(pieces, kinds, count, summed, order_ref, *refs):
    windows = {kind: refs[2 * i:2 * i + 2] for i, kind in enumerate(kinds)}
    blocks, refs = refs[2 * len(kinds):2 * len(kinds) + count], refs[2 * len(kinds) + count:]
    tokens = windows[kinds[0]][0].shape[0]
    for i, kind in enumerate(kinds):
        for k in range(2):
            at = pl.ds(k * tokens, tokens)
            total = refs[i][at] if summed else 0.0
            for which, row, height, of, column in pieces:
                if of == kind:
                    window = windows[kind][k][:, column:column + height]
                    total += dot(window, blocks[which][row:row + height])
            refs[i - len(kinds)][at] = total


def step(order, tokens_of, blocks, pieces, totals, s):
    kinds = sorted({piece[3] for piece in pieces})
    windows = []
    for kind in kinds:
        own, sib, width = tokens_of[kind]
        windows += [(x, width, lambda i, o: (0, o[s])) for x in (own, sib)]
    tokens, columns = windows[0][0].shape[0], blocks[0].shape[1]
    summed = all(kind in totals for kind in kinds)
    shape = jax.ShapeDtypeStruct((2 * tokens, columns), F32)
    out = call(
        functools.partial(step_kernel, pieces, kinds, len(blocks), summed),
        order, windows, list(blocks) + ([totals[k] for k in kinds] if summed else []), [],
        [shape] * len(kinds), 4 * tokens * sum(p[2] for p in pieces) * columns, "step",
    )
    return {**totals, **dict(zip(kinds, out))}


def window_kernel(lead, order_ref, own_ref, sib_ref, out_ref):
    tokens = own_ref.shape[0]
    out_ref[:tokens] = own_ref[:, :lead]
    out_ref[tokens:] = sib_ref[:, :lead]


EXTRA = 8


def turned_kernel(count, order_ref, *refs):
    windows, blocks = refs[:2 * count], refs[2 * count:3 * count]
    total_ref, seq_ref, len_ref, out_ref = refs[3 * count:]
    tokens = windows[0].shape[0]
    for k in range(2):
        at = pl.ds(k * tokens, tokens)
        total = total_ref[at]
        for w in range(count):
            total += dot(windows[2 * w + k][...], blocks[w][...])
        out_ref[at] = total
    held = seq_ref.shape[0]
    lane = lax.broadcasted_iota(jnp.int32, (EXTRA, out_ref.shape[1]), 1)
    numbers = jnp.zeros(lane.shape, F32)
    for i in range(held):
        numbers = jnp.where(lane == i, seq_ref[i].astype(F32), numbers)
        numbers = jnp.where(lane == held + i, len_ref[i].astype(F32), numbers)
    out_ref[2 * tokens:] = numbers


def masked_kernel(order_ref, own_ref, got_ref, out_ref):
    tokens = (own_ref.shape[0] - EXTRA) // 2
    columns = own_ref.shape[1]
    held = tokens // LEN
    position = lax.broadcasted_iota(jnp.int32, (LEN, columns), 0).astype(F32)
    for k, (mine, other) in enumerate(((own_ref, got_ref), (got_ref, own_ref))):
        for i in range(held):
            at, across = pl.ds(i * LEN, LEN), pl.ds(tokens + i * LEN, LEN)
            length = mine[2 * tokens:2 * tokens + 1, held + i:held + i + 1]
            out_ref[pl.ds(k * tokens + i * LEN, LEN)] = jnp.where(
                position < length, mine[at] + other[across], 0.0
            )
    lane = lax.broadcasted_iota(jnp.int32, (EXTRA, columns), 1)
    numbers = jnp.zeros(lane.shape, F32)
    for k, ref in enumerate((own_ref, got_ref)):
        for i in range(held):
            slot = ref[2 * tokens:2 * tokens + 1, i:i + 1]
            numbers = jnp.where(lane == k * held + i, slot, numbers)
    out_ref[2 * tokens:] = numbers


def score_kernel(per_device, window_ref, block_ref, total_ref, inn_ref, table_ref):
    height, columns = total_ref.shape
    queries = columns // RANK
    column = lax.broadcasted_iota(jnp.int32, (columns, queries), 0) // RANK
    query = lax.broadcasted_iota(jnp.int32, (columns, queries), 1)
    fold = (column == query).astype(F32)
    row = lax.broadcasted_iota(jnp.int32, table_ref.shape, 0)
    count = table_ref.shape[0] // per_device
    owner = lax.rem(count - lax.div(row, per_device), count)
    row = (owner * per_device + lax.rem(row, per_device)).astype(F32)
    contrib = (total_ref[...] + dot(window_ref[...], block_ref[...])) * inn_ref[:height]
    count = height // LEN
    sums = [jnp.sum(contrib[i * LEN:(i + 1) * LEN], axis=0, keepdims=True) for i in range(count)]
    scores = jnp.dot(
        jnp.concatenate(sums), fold, precision=lax.Precision.HIGHEST, preferred_element_type=F32
    ) * (1.0 / math.sqrt(RANK * LEN))
    table = jnp.zeros(table_ref.shape, F32)
    for i in range(count):
        slot = inn_ref[height:height + 1, i:i + 1]
        table = jnp.where(row == slot, scores[i:i + 1], table)
    table_ref[...] = table


def score_table(arrays, per_device, rows, queries):
    vmem = pl.BlockSpec(memory_space=pltpu.VMEM)
    window, block = arrays[:2]
    size = sum(x.size * x.dtype.itemsize for x in arrays)
    return pl.pallas_call(
        functools.partial(score_kernel, per_device),
        in_specs=[vmem] * len(arrays),
        out_specs=vmem,
        out_shape=jax.ShapeDtypeStruct((rows, queries), F32),
        cost_estimate=pl.CostEstimate(
            flops=2 * window.size * block.shape[1], bytes_accessed=size, transcendentals=0
        ),
        compiler_params=pltpu.CompilerParams(vmem_limit_bytes=16 << 20),
        name="score",
    )(*arrays)


def shards(acts, grads, out_factors, in_factors, seq_slot, lengths):
    devices = lax.axis_size("dp")
    chips = devices // 2
    me = lax.axis_index("dp")
    tokens = grads.shape[0]
    rows, columns = out_factors.shape
    rows_in = in_factors.shape[0]
    orders = jnp.asarray(block_orders(chips))
    mine = lax.dynamic_index_in_dim(orders, me, keepdims=False)
    pairs = ring_pairs(chips)
    swap = [(d, d ^ 1) for d in range(devices)]

    send = lambda x: lax.ppermute(x, "dp", pairs)
    across = lambda x: lax.ppermute(x, "dp", swap)

    every = None
    if rows_in % 128:
        every = lax.all_gather(in_factors, "dp", axis=0, tiled=True)
        rows_in = 0
    lead = (rows - rows_in) // 2
    tokens_of = {"out": (grads, across(grads), rows)}
    if rows_in:
        tokens_of["in"] = (acts, across(acts), rows_in)

    inside = [(1, 0, rows_in, "in", 0)] if rows_in else []
    held = [[out_factors] + [in_factors] * (rows_in > 0)]
    pieces = [[(0, 0, rows, "out", 0)] + inside]
    came = send(out_factors)
    late, early = came[lead:], came[:lead]
    if rows_in:
        came, turned = lax.optimization_barrier((came, in_factors))
        turned = lax.ppermute(turned, "dp", [(j, i) for i, j in pairs])
        late, early = came[lead:], came[:lead]
        inner, turned = lax.optimization_barrier((send(in_factors), turned))
        early = jnp.concatenate([inner, early])
        backward = [(j, i) for i, j in pairs]
        turned = [turned, lax.ppermute(turned, "dp", backward)]
    totals, summed, last = {}, 0, chips - 1

    def sum_to(k, totals, summed):
        for j in range(summed, k):
            totals = step(mine, tokens_of, held[j], pieces[j], totals, j)
        return totals, max(k, summed)

    window = call(
        functools.partial(window_kernel, lead), mine,
        [(x, rows, lambda i, o: (0, o[last])) for x in tokens_of["out"][:2]], [], [],
        [jax.ShapeDtypeStruct((2 * tokens, lead), grads.dtype)], 0, "window",
    )[0]

    for s in range(1, chips):
        held.append([late, early])
        top = rows_in if s < last - 1 else 0
        pieces.append([(0, 0, rows - lead, "out", lead), (1, top, lead, "out", 0)])
        pieces[s] += inside if top else []
        if s == last:
            break
        if s >= 4:
            totals, summed = sum_to(min(2 * s - 6, s), totals, summed)
            late, totals = lax.optimization_barrier((late, totals))
            early, totals = lax.optimization_barrier((early, totals))
        if s == 4 and rows_in:
            early, turned = lax.optimization_barrier((early, turned))
        late = send(late)
        if s == last - 1:
            early, window = lax.optimization_barrier((early, window))
        early = send(early[rows_in:] if s == last - 2 else early)

    totals, summed = sum_to(last, totals, summed)
    slots = lengths.shape[0]
    height = (2 * tokens + EXTRA, columns)
    if rows_in:
        inn = call(
            functools.partial(turned_kernel, 2), mine,
            [
                (x, rows_in, functools.partial(lambda i, o, k: (0, o[k]), k=last - k))
                for k in (0, 1) for x in tokens_of["in"][:2]
            ],
            turned + [totals["in"]], [seq_slot, lengths],
            [jax.ShapeDtypeStruct(height, F32)], 8 * tokens * rows_in * columns, "turned",
        )[0]
    else:
        numbers = jnp.concatenate([seq_slot, lengths]).astype(F32)
        inn = jnp.zeros(height, F32).at[:tokens].set(dot(acts, every))
        inn = inn.at[2 * tokens, :2 * slots].set(numbers)
    inn = call(
        masked_kernel, mine, [], [inn, across(inn)], [],
        [jax.ShapeDtypeStruct(height, F32)], 0, "masked",
    )[0]
    totals = step(mine, tokens_of, [late], pieces[last][:1], totals, last)

    queries = columns // RANK
    table = score_table([window, early, totals["out"], inn], slots, slots * devices, queries)
    groups = [[0] + list(range(devices - 1, 0, -1))]
    got = lax.all_to_all(
        table.reshape(devices, slots, queries), "dp", 0, 0, axis_index_groups=groups, tiled=True
    )
    return jnp.sum(got, axis=0)


def solution(mesh):
    return jax.shard_map(
        shards,
        mesh=mesh,
        in_specs=(
            P(("groups", "dp"), None),
            P(("groups", "dp"), None),
            P(("groups", "dp"), None),
            P(("groups", "dp"), None),
            P(("groups", "dp")),
            P(("groups", "dp")),
        ),
        out_specs=P(("groups", "dp"), None),
        check_vma=False,
    )
```

```python
import functools
import math

import jax
import jax.numpy as jnp
import numpy as np
from jax import lax
from jax.experimental import pallas as pl
from jax.experimental.pallas import tpu as pltpu
from jax.sharding import PartitionSpec as P

RANK = 32
LEN = 80
F32 = jnp.float32
VMEM = 52 << 20


def ring_of(chips):
    cols = max([d for d in range(1, math.isqrt(chips) + 1) if chips % d == 0 and d % 2 == 0] or [1])
    rows = chips // cols
    if cols == 1 or rows % 2:
        return list(range(chips))
    walk = []
    for r in range(rows):
        line = range(1, cols) if r % 2 == 0 else range(cols - 1, 0, -1)
        walk += [r * cols + c for c in line]
    return walk + [r * cols for r in reversed(range(rows))]


def block_orders(chips):
    ring = ring_of(chips)
    order = np.zeros((2 * chips, chips), np.int32)
    for p, chip in enumerate(ring):
        for s in range(chips):
            order[2 * chip, s] = 2 * ring[(p - s) % chips]
            order[2 * chip + 1, s] = 2 * ring[(p + s) % chips] + 1
    return order


def ring_pairs(chips):
    ring = ring_of(chips)
    pairs = []
    for p, chip in enumerate(ring):
        pairs.append((2 * chip, 2 * ring[(p + 1) % chips]))
        pairs.append((2 * chip + 1, 2 * ring[(p - 1) % chips] + 1))
    return pairs


def dot(a, b):
    return jnp.dot(a, b, preferred_element_type=F32)


def call(kernel, order, windows, whole, scalars, out_shape, flops, name):
    in_specs = [pl.BlockSpec((x.shape[0], w), at) for x, w, at in windows]
    in_specs += [pl.BlockSpec(x.shape, lambda i, o: (0, 0)) for x in whole]
    in_specs += [pl.BlockSpec(memory_space=pltpu.SMEM) for _ in scalars]
    size = sum(2 * x.shape[0] * w for x, w, _ in windows)
    size += sum(x.size * x.dtype.itemsize for x in list(whole) + list(out_shape))
    return pl.pallas_call(
        kernel,
        grid_spec=pltpu.PrefetchScalarGridSpec(
            num_scalar_prefetch=1,
            grid=(1,),
            in_specs=in_specs,
            out_specs=[pl.BlockSpec(x.shape, lambda i, o: (0, 0)) for x in out_shape],
        ),
        out_shape=out_shape,
        cost_estimate=pl.CostEstimate(flops=flops, bytes_accessed=size, transcendentals=0),
        compiler_params=pltpu.CompilerParams(vmem_limit_bytes=VMEM),
        name=name,
    )(order, *[x for x, _, _ in windows], *whole, *scalars)


def step_kernel(pieces, kinds, count, summed, order_ref, *refs):
    windows = {kind: refs[2 * i:2 * i + 2] for i, kind in enumerate(kinds)}
    blocks, refs = refs[2 * len(kinds):2 * len(kinds) + count], refs[2 * len(kinds) + count:]
    tokens = windows[kinds[0]][0].shape[0]
    for i, kind in enumerate(kinds):
        for k in range(2):
            at = pl.ds(k * tokens, tokens)
            total = refs[i][at] if summed else 0.0
            for which, row, height, of, column in pieces:
                if of == kind:
                    window = windows[kind][k][:, column:column + height]
                    total += dot(window, blocks[which][row:row + height])
            refs[i - len(kinds)][at] = total


def step(order, tokens_of, blocks, pieces, totals, s):
    kinds = sorted({piece[3] for piece in pieces})
    windows = []
    for kind in kinds:
        own, sib, width = tokens_of[kind]
        windows += [(x, width, lambda i, o: (0, o[s])) for x in (own, sib)]
    tokens, columns = windows[0][0].shape[0], blocks[0].shape[1]
    summed = all(kind in totals for kind in kinds)
    shape = jax.ShapeDtypeStruct((2 * tokens, columns), F32)
    out = call(
        functools.partial(step_kernel, pieces, kinds, len(blocks), summed),
        order, windows, list(blocks) + ([totals[k] for k in kinds] if summed else []), [],
        [shape] * len(kinds), 4 * tokens * sum(p[2] for p in pieces) * columns, "step",
    )
    return {**totals, **dict(zip(kinds, out))}


def window_kernel(lead, order_ref, own_ref, sib_ref, out_ref):
    tokens = own_ref.shape[0]
    out_ref[:tokens] = own_ref[:, :lead]
    out_ref[tokens:] = sib_ref[:, :lead]


EXTRA = 8


def turned_kernel(count, order_ref, *refs):
    windows, blocks = refs[:2 * count], refs[2 * count:3 * count]
    total_ref, seq_ref, len_ref, out_ref = refs[3 * count:]
    tokens = windows[0].shape[0]
    for k in range(2):
        at = pl.ds(k * tokens, tokens)
        total = total_ref[at]
        for w in range(count):
            total += dot(windows[2 * w + k][...], blocks[w][...])
        out_ref[at] = total
    held = seq_ref.shape[0]
    lane = lax.broadcasted_iota(jnp.int32, (EXTRA, out_ref.shape[1]), 1)
    numbers = jnp.zeros(lane.shape, F32)
    for i in range(held):
        numbers = jnp.where(lane == i, seq_ref[i].astype(F32), numbers)
        numbers = jnp.where(lane == held + i, len_ref[i].astype(F32), numbers)
    out_ref[2 * tokens:] = numbers


def masked_kernel(order_ref, own_ref, got_ref, out_ref):
    tokens = (own_ref.shape[0] - EXTRA) // 2
    columns = own_ref.shape[1]
    held = tokens // LEN
    position = lax.broadcasted_iota(jnp.int32, (LEN, columns), 0).astype(F32)
    for k, (mine, other) in enumerate(((own_ref, got_ref), (got_ref, own_ref))):
        for i in range(held):
            at, across = pl.ds(i * LEN, LEN), pl.ds(tokens + i * LEN, LEN)
            length = mine[2 * tokens:2 * tokens + 1, held + i:held + i + 1]
            out_ref[pl.ds(k * tokens + i * LEN, LEN)] = jnp.where(
                position < length, mine[at] + other[across], 0.0
            )
    lane = lax.broadcasted_iota(jnp.int32, (EXTRA, columns), 1)
    numbers = jnp.zeros(lane.shape, F32)
    for k, ref in enumerate((own_ref, got_ref)):
        for i in range(held):
            slot = ref[2 * tokens:2 * tokens + 1, i:i + 1]
            numbers = jnp.where(lane == k * held + i, slot, numbers)
    out_ref[2 * tokens:] = numbers


def score_kernel(per_device, window_ref, block_ref, total_ref, inn_ref, table_ref):
    height, columns = total_ref.shape
    queries = columns // RANK
    column = lax.broadcasted_iota(jnp.int32, (columns, queries), 0) // RANK
    query = lax.broadcasted_iota(jnp.int32, (columns, queries), 1)
    fold = (column == query).astype(F32)
    row = lax.broadcasted_iota(jnp.int32, table_ref.shape, 0)
    count = table_ref.shape[0] // per_device
    owner = lax.rem(count + 3 * count // 4 - 1 - lax.div(row, per_device), count)
    row = (owner * per_device + lax.rem(row, per_device)).astype(F32)
    contrib = (total_ref[...] + dot(window_ref[...], block_ref[...])) * inn_ref[:height]
    count = height // LEN
    sums = [jnp.sum(contrib[i * LEN:(i + 1) * LEN], axis=0, keepdims=True) for i in range(count)]
    scores = jnp.dot(
        jnp.concatenate(sums), fold, precision=lax.Precision.HIGHEST, preferred_element_type=F32
    ) * (1.0 / math.sqrt(RANK * LEN))
    table = jnp.zeros(table_ref.shape, F32)
    for i in range(count):
        slot = inn_ref[height:height + 1, i:i + 1]
        table = jnp.where(row == slot, scores[i:i + 1], table)
    table_ref[...] = table


def score_table(arrays, per_device, rows, queries):
    vmem = pl.BlockSpec(memory_space=pltpu.VMEM)
    window, block = arrays[:2]
    size = sum(x.size * x.dtype.itemsize for x in arrays)
    return pl.pallas_call(
        functools.partial(score_kernel, per_device),
        in_specs=[vmem] * len(arrays),
        out_specs=vmem,
        out_shape=jax.ShapeDtypeStruct((rows, queries), F32),
        cost_estimate=pl.CostEstimate(
            flops=2 * window.size * block.shape[1], bytes_accessed=size, transcendentals=0
        ),
        compiler_params=pltpu.CompilerParams(vmem_limit_bytes=16 << 20),
        name="score",
    )(*arrays)


def shards(acts, grads, out_factors, in_factors, seq_slot, lengths):
    devices = lax.axis_size("dp")
    chips = devices // 2
    me = lax.axis_index("dp")
    tokens = grads.shape[0]
    rows, columns = out_factors.shape
    rows_in = in_factors.shape[0]
    orders = jnp.asarray(block_orders(chips))
    mine = lax.dynamic_index_in_dim(orders, me, keepdims=False)
    pairs = ring_pairs(chips)
    swap = [(d, d ^ 1) for d in range(devices)]

    send = lambda x: lax.ppermute(x, "dp", pairs)
    across = lambda x: lax.ppermute(x, "dp", swap)

    every = None
    if rows_in % 128:
        every = lax.all_gather(in_factors, "dp", axis=0, tiled=True)
        rows_in = 0
    lead = (rows - rows_in) // 2
    tokens_of = {"out": (grads, across(grads), rows)}
    if rows_in:
        tokens_of["in"] = (acts, across(acts), rows_in)

    inside = [(1, 0, rows_in, "in", 0)] if rows_in else []
    held = [[out_factors] + [in_factors] * (rows_in > 0)]
    pieces = [[(0, 0, rows, "out", 0)] + inside]
    came = send(out_factors)
    late, early = came[lead:], came[:lead]
    if rows_in:
        came, turned = lax.optimization_barrier((came, in_factors))
        turned = lax.ppermute(turned, "dp", [(j, i) for i, j in pairs])
        late, early = came[lead:], came[:lead]
        inner, turned = lax.optimization_barrier((send(in_factors), turned))
        early = jnp.concatenate([inner, early])
        backward = [(j, i) for i, j in pairs]
        turned = [turned, lax.ppermute(turned, "dp", backward)]
    totals, summed, last = {}, 0, chips - 1

    def sum_to(k, totals, summed):
        for j in range(summed, k):
            totals = step(mine, tokens_of, held[j], pieces[j], totals, j)
        return totals, max(k, summed)

    window = call(
        functools.partial(window_kernel, lead), mine,
        [(x, rows, lambda i, o: (0, o[last])) for x in tokens_of["out"][:2]], [], [],
        [jax.ShapeDtypeStruct((2 * tokens, lead), grads.dtype)], 0, "window",
    )[0]

    for s in range(1, chips):
        held.append([late, early])
        top = rows_in if s < last - 1 else 0
        pieces.append([(0, 0, rows - lead, "out", lead), (1, top, lead, "out", 0)])
        pieces[s] += inside if top else []
        if s == last:
            break
        if s >= 4:
            totals, summed = sum_to(min(2 * s - 6, s), totals, summed)
            late, totals = lax.optimization_barrier((late, totals))
            early, totals = lax.optimization_barrier((early, totals))
        if s == 4 and rows_in:
            early, turned = lax.optimization_barrier((early, turned))
        late = send(late)
        if s == last - 1:
            early, window = lax.optimization_barrier((early, window))
        early = send(early[rows_in:] if s == last - 2 else early)

    totals, summed = sum_to(last, totals, summed)
    slots = lengths.shape[0]
    height = (2 * tokens + EXTRA, columns)
    if rows_in:
        inn = call(
            functools.partial(turned_kernel, 2), mine,
            [
                (x, rows_in, functools.partial(lambda i, o, k: (0, o[k]), k=last - k))
                for k in (0, 1) for x in tokens_of["in"][:2]
            ],
            turned + [totals["in"]], [seq_slot, lengths],
            [jax.ShapeDtypeStruct(height, F32)], 8 * tokens * rows_in * columns, "turned",
        )[0]
    else:
        numbers = jnp.concatenate([seq_slot, lengths]).astype(F32)
        inn = jnp.zeros(height, F32).at[:tokens].set(dot(acts, every))
        inn = inn.at[2 * tokens, :2 * slots].set(numbers)
    inn = call(
        masked_kernel, mine, [], [inn, across(inn)], [],
        [jax.ShapeDtypeStruct(height, F32)], 0, "masked",
    )[0]
    totals = step(mine, tokens_of, [late], pieces[last][:1], totals, last)

    queries = columns // RANK
    table = score_table([window, early, totals["out"], inn], slots, slots * devices, queries)
    groups = [[(3 * devices // 4 - 1 - k) % devices for k in range(devices)]]
    got = lax.all_to_all(
        table.reshape(devices, slots, queries), "dp", 0, 0, axis_index_groups=groups, tiled=True
    )
    return jnp.sum(got, axis=0)


def solution(mesh):
    return jax.shard_map(
        shards,
        mesh=mesh,
        in_specs=(
            P(("groups", "dp"), None),
            P(("groups", "dp"), None),
            P(("groups", "dp"), None),
            P(("groups", "dp"), None),
            P(("groups", "dp")),
            P(("groups", "dp")),
        ),
        out_specs=P(("groups", "dp"), None),
        check_vma=False,
    )
```

```python
import functools
import math

import jax
import jax.numpy as jnp
import numpy as np
from jax import lax
from jax.experimental import pallas as pl
from jax.experimental.pallas import tpu as pltpu
from jax.sharding import PartitionSpec as P

RANK = 32
LEN = 80
F32 = jnp.float32
VMEM = 52 << 20


def ring_of(chips):
    cols = max([d for d in range(1, math.isqrt(chips) + 1) if chips % d == 0 and d % 2 == 0] or [1])
    rows = chips // cols
    if cols == 1 or rows % 2:
        return list(range(chips))
    walk = []
    for r in range(rows):
        line = range(1, cols) if r % 2 == 0 else range(cols - 1, 0, -1)
        walk += [r * cols + c for c in line]
    return walk + [r * cols for r in reversed(range(rows))]


def block_orders(chips):
    ring = ring_of(chips)
    order = np.zeros((2 * chips, chips), np.int32)
    for p, chip in enumerate(ring):
        for s in range(chips):
            order[2 * chip, s] = 2 * ring[(p - s) % chips]
            order[2 * chip + 1, s] = 2 * ring[(p + s) % chips] + 1
    return order


def ring_pairs(chips):
    ring = ring_of(chips)
    pairs = []
    for p, chip in enumerate(ring):
        pairs.append((2 * chip, 2 * ring[(p + 1) % chips]))
        pairs.append((2 * chip + 1, 2 * ring[(p - 1) % chips] + 1))
    return pairs


def dot(a, b):
    return jnp.dot(a, b, preferred_element_type=F32)


def call(kernel, order, windows, whole, scalars, out_shape, flops, name):
    in_specs = [pl.BlockSpec((x.shape[0], w), at) for x, w, at in windows]
    in_specs += [pl.BlockSpec(x.shape, lambda i, o: (0, 0)) for x in whole]
    in_specs += [pl.BlockSpec(memory_space=pltpu.SMEM) for _ in scalars]
    size = sum(2 * x.shape[0] * w for x, w, _ in windows)
    size += sum(x.size * x.dtype.itemsize for x in list(whole) + list(out_shape))
    return pl.pallas_call(
        kernel,
        grid_spec=pltpu.PrefetchScalarGridSpec(
            num_scalar_prefetch=1,
            grid=(1,),
            in_specs=in_specs,
            out_specs=[pl.BlockSpec(x.shape, lambda i, o: (0, 0)) for x in out_shape],
        ),
        out_shape=out_shape,
        cost_estimate=pl.CostEstimate(flops=flops, bytes_accessed=size, transcendentals=0),
        compiler_params=pltpu.CompilerParams(vmem_limit_bytes=VMEM),
        name=name,
    )(order, *[x for x, _, _ in windows], *whole, *scalars)


def step_kernel(pieces, kinds, count, summed, order_ref, *refs):
    windows = {kind: refs[2 * i:2 * i + 2] for i, kind in enumerate(kinds)}
    blocks, refs = refs[2 * len(kinds):2 * len(kinds) + count], refs[2 * len(kinds) + count:]
    tokens = windows[kinds[0]][0].shape[0]
    for i, kind in enumerate(kinds):
        for k in range(2):
            at = pl.ds(k * tokens, tokens)
            total = refs[i][at] if summed else 0.0
            for which, row, height, of, column in pieces:
                if of == kind:
                    window = windows[kind][k][:, column:column + height]
                    total += dot(window, blocks[which][row:row + height])
            refs[i - len(kinds)][at] = total


def step(order, tokens_of, blocks, pieces, totals, s):
    kinds = sorted({piece[3] for piece in pieces})
    windows = []
    for kind in kinds:
        own, sib, width = tokens_of[kind]
        windows += [(x, width, lambda i, o: (0, o[s])) for x in (own, sib)]
    tokens, columns = windows[0][0].shape[0], blocks[0].shape[1]
    summed = all(kind in totals for kind in kinds)
    shape = jax.ShapeDtypeStruct((2 * tokens, columns), F32)
    out = call(
        functools.partial(step_kernel, pieces, kinds, len(blocks), summed),
        order, windows, list(blocks) + ([totals[k] for k in kinds] if summed else []), [],
        [shape] * len(kinds), 4 * tokens * sum(p[2] for p in pieces) * columns, "step",
    )
    return {**totals, **dict(zip(kinds, out))}


def window_kernel(lead, order_ref, own_ref, sib_ref, out_ref):
    tokens = own_ref.shape[0]
    out_ref[:tokens] = own_ref[:, :lead]
    out_ref[tokens:] = sib_ref[:, :lead]


EXTRA = 8


def turned_kernel(count, order_ref, *refs):
    windows, blocks = refs[:2 * count], refs[2 * count:3 * count]
    total_ref, seq_ref, len_ref, out_ref = refs[3 * count:]
    tokens = windows[0].shape[0]
    for k in range(2):
        at = pl.ds(k * tokens, tokens)
        total = total_ref[at]
        for w in range(count):
            total += dot(windows[2 * w + k][...], blocks[w][...])
        out_ref[at] = total
    held = seq_ref.shape[0]
    lane = lax.broadcasted_iota(jnp.int32, (EXTRA, out_ref.shape[1]), 1)
    numbers = jnp.zeros(lane.shape, F32)
    for i in range(held):
        numbers = jnp.where(lane == i, seq_ref[i].astype(F32), numbers)
        numbers = jnp.where(lane == held + i, len_ref[i].astype(F32), numbers)
    out_ref[2 * tokens:] = numbers


def masked_kernel(order_ref, own_ref, got_ref, out_ref):
    tokens = (own_ref.shape[0] - EXTRA) // 2
    columns = own_ref.shape[1]
    held = tokens // LEN
    position = lax.broadcasted_iota(jnp.int32, (LEN, columns), 0).astype(F32)
    for k, (mine, other) in enumerate(((own_ref, got_ref), (got_ref, own_ref))):
        for i in range(held):
            at, across = pl.ds(i * LEN, LEN), pl.ds(tokens + i * LEN, LEN)
            length = mine[2 * tokens:2 * tokens + 1, held + i:held + i + 1]
            out_ref[pl.ds(k * tokens + i * LEN, LEN)] = jnp.where(
                position < length, mine[at] + other[across], 0.0
            )
    lane = lax.broadcasted_iota(jnp.int32, (EXTRA, columns), 1)
    numbers = jnp.zeros(lane.shape, F32)
    for k, ref in enumerate((own_ref, got_ref)):
        for i in range(held):
            slot = ref[2 * tokens:2 * tokens + 1, i:i + 1]
            numbers = jnp.where(lane == k * held + i, slot, numbers)
    out_ref[2 * tokens:] = numbers


def score_kernel(per_device, window_ref, block_ref, total_ref, inn_ref, table_ref):
    height, columns = total_ref.shape
    queries = columns // RANK
    column = lax.broadcasted_iota(jnp.int32, (columns, queries), 0) // RANK
    query = lax.broadcasted_iota(jnp.int32, (columns, queries), 1)
    fold = (column == query).astype(F32)
    row = lax.broadcasted_iota(jnp.int32, table_ref.shape, 0)
    count = table_ref.shape[0] // per_device
    owner = lax.rem(2 * count - 3 - lax.div(row, per_device), count)
    row = (owner * per_device + lax.rem(row, per_device)).astype(F32)
    contrib = (total_ref[...] + dot(window_ref[...], block_ref[...])) * inn_ref[:height]
    count = height // LEN
    sums = [jnp.sum(contrib[i * LEN:(i + 1) * LEN], axis=0, keepdims=True) for i in range(count)]
    scores = jnp.dot(
        jnp.concatenate(sums), fold, precision=lax.Precision.HIGHEST, preferred_element_type=F32
    ) * (1.0 / math.sqrt(RANK * LEN))
    table = jnp.zeros(table_ref.shape, F32)
    for i in range(count):
        slot = inn_ref[height:height + 1, i:i + 1]
        table = jnp.where(row == slot, scores[i:i + 1], table)
    table_ref[...] = table


def score_table(arrays, per_device, rows, queries):
    vmem = pl.BlockSpec(memory_space=pltpu.VMEM)
    window, block = arrays[:2]
    size = sum(x.size * x.dtype.itemsize for x in arrays)
    return pl.pallas_call(
        functools.partial(score_kernel, per_device),
        in_specs=[vmem] * len(arrays),
        out_specs=vmem,
        out_shape=jax.ShapeDtypeStruct((rows, queries), F32),
        cost_estimate=pl.CostEstimate(
            flops=2 * window.size * block.shape[1], bytes_accessed=size, transcendentals=0
        ),
        compiler_params=pltpu.CompilerParams(vmem_limit_bytes=16 << 20),
        name="score",
    )(*arrays)


def shards(acts, grads, out_factors, in_factors, seq_slot, lengths):
    devices = lax.axis_size("dp")
    chips = devices // 2
    me = lax.axis_index("dp")
    tokens = grads.shape[0]
    rows, columns = out_factors.shape
    rows_in = in_factors.shape[0]
    orders = jnp.asarray(block_orders(chips))
    mine = lax.dynamic_index_in_dim(orders, me, keepdims=False)
    pairs = ring_pairs(chips)
    swap = [(d, d ^ 1) for d in range(devices)]

    send = lambda x: lax.ppermute(x, "dp", pairs)
    across = lambda x: lax.ppermute(x, "dp", swap)

    every = None
    if rows_in % 128:
        every = lax.all_gather(in_factors, "dp", axis=0, tiled=True)
        rows_in = 0
    lead = (rows - rows_in) // 2
    tokens_of = {"out": (grads, across(grads), rows)}
    if rows_in:
        tokens_of["in"] = (acts, across(acts), rows_in)

    inside = [(1, 0, rows_in, "in", 0)] if rows_in else []
    held = [[out_factors] + [in_factors] * (rows_in > 0)]
    pieces = [[(0, 0, rows, "out", 0)] + inside]
    came = send(out_factors)
    late, early = came[lead:], came[:lead]
    if rows_in:
        came, turned = lax.optimization_barrier((came, in_factors))
        turned = lax.ppermute(turned, "dp", [(j, i) for i, j in pairs])
        late, early = came[lead:], came[:lead]
        inner, turned = lax.optimization_barrier((send(in_factors), turned))
        early = jnp.concatenate([inner, early])
        backward = [(j, i) for i, j in pairs]
        turned = [turned, lax.ppermute(turned, "dp", backward)]
    totals, summed, last = {}, 0, chips - 1

    def sum_to(k, totals, summed):
        for j in range(summed, k):
            totals = step(mine, tokens_of, held[j], pieces[j], totals, j)
        return totals, max(k, summed)

    window = call(
        functools.partial(window_kernel, lead), mine,
        [(x, rows, lambda i, o: (0, o[last])) for x in tokens_of["out"][:2]], [], [],
        [jax.ShapeDtypeStruct((2 * tokens, lead), grads.dtype)], 0, "window",
    )[0]

    for s in range(1, chips):
        held.append([late, early])
        top = rows_in if s < last - 1 else 0
        pieces.append([(0, 0, rows - lead, "out", lead), (1, top, lead, "out", 0)])
        pieces[s] += inside if top else []
        if s == last:
            break
        if s >= 4:
            totals, summed = sum_to(min(2 * s - 6, s), totals, summed)
            late, totals = lax.optimization_barrier((late, totals))
            early, totals = lax.optimization_barrier((early, totals))
        if s == 4 and rows_in:
            early, turned = lax.optimization_barrier((early, turned))
        late = send(late)
        if s == last - 1:
            early, window = lax.optimization_barrier((early, window))
        early = send(early[rows_in:] if s == last - 2 else early)

    totals, summed = sum_to(last, totals, summed)
    slots = lengths.shape[0]
    height = (2 * tokens + EXTRA, columns)
    if rows_in:
        inn = call(
            functools.partial(turned_kernel, 2), mine,
            [
                (x, rows_in, functools.partial(lambda i, o, k: (0, o[k]), k=last - k))
                for k in (0, 1) for x in tokens_of["in"][:2]
            ],
            turned + [totals["in"]], [seq_slot, lengths],
            [jax.ShapeDtypeStruct(height, F32)], 8 * tokens * rows_in * columns, "turned",
        )[0]
    else:
        numbers = jnp.concatenate([seq_slot, lengths]).astype(F32)
        inn = jnp.zeros(height, F32).at[:tokens].set(dot(acts, every))
        inn = inn.at[2 * tokens, :2 * slots].set(numbers)
    inn = call(
        masked_kernel, mine, [], [inn, across(inn)], [],
        [jax.ShapeDtypeStruct(height, F32)], 0, "masked",
    )[0]
    totals = step(mine, tokens_of, [late], pieces[last][:1], totals, last)

    queries = columns // RANK
    table = score_table([window, early, totals["out"], inn], slots, slots * devices, queries)
    groups = [[(devices - 3 - k) % devices for k in range(devices)]]
    got = lax.all_to_all(
        table.reshape(devices, slots, queries), "dp", 0, 0, axis_index_groups=groups, tiled=True
    )
    return jnp.sum(got, axis=0)


def solution(mesh):
    return jax.shard_map(
        shards,
        mesh=mesh,
        in_specs=(
            P(("groups", "dp"), None),
            P(("groups", "dp"), None),
            P(("groups", "dp"), None),
            P(("groups", "dp"), None),
            P(("groups", "dp")),
            P(("groups", "dp")),
        ),
        out_specs=P(("groups", "dp"), None),
        check_vma=False,
    )
```

```python
import functools
import math

import jax
import jax.numpy as jnp
import numpy as np
from jax import lax
from jax.experimental import pallas as pl
from jax.experimental.pallas import tpu as pltpu
from jax.sharding import PartitionSpec as P

RANK = 32
LEN = 80
F32 = jnp.float32
VMEM = 52 << 20


def ring_of(chips):
    cols = max([d for d in range(1, math.isqrt(chips) + 1) if chips % d == 0 and d % 2 == 0] or [1])
    rows = chips // cols
    if cols == 1 or rows % 2:
        return list(range(chips))
    walk = []
    for r in range(rows):
        line = range(1, cols) if r % 2 == 0 else range(cols - 1, 0, -1)
        walk += [r * cols + c for c in line]
    return walk + [r * cols for r in reversed(range(rows))]


def block_orders(chips):
    ring = ring_of(chips)
    order = np.zeros((2 * chips, chips), np.int32)
    for p, chip in enumerate(ring):
        for s in range(chips):
            order[2 * chip, s] = 2 * ring[(p - s) % chips]
            order[2 * chip + 1, s] = 2 * ring[(p + s) % chips] + 1
    return order


def ring_pairs(chips):
    ring = ring_of(chips)
    pairs = []
    for p, chip in enumerate(ring):
        pairs.append((2 * chip, 2 * ring[(p + 1) % chips]))
        pairs.append((2 * chip + 1, 2 * ring[(p - 1) % chips] + 1))
    return pairs


def dot(a, b):
    return jnp.dot(a, b, preferred_element_type=F32)


def call(kernel, order, windows, whole, scalars, out_shape, flops, name):
    in_specs = [pl.BlockSpec((x.shape[0], w), at) for x, w, at in windows]
    in_specs += [pl.BlockSpec(x.shape, lambda i, o: (0, 0)) for x in whole]
    in_specs += [pl.BlockSpec(memory_space=pltpu.SMEM) for _ in scalars]
    size = sum(2 * x.shape[0] * w for x, w, _ in windows)
    size += sum(x.size * x.dtype.itemsize for x in list(whole) + list(out_shape))
    return pl.pallas_call(
        kernel,
        grid_spec=pltpu.PrefetchScalarGridSpec(
            num_scalar_prefetch=1,
            grid=(1,),
            in_specs=in_specs,
            out_specs=[pl.BlockSpec(x.shape, lambda i, o: (0, 0)) for x in out_shape],
        ),
        out_shape=out_shape,
        cost_estimate=pl.CostEstimate(flops=flops, bytes_accessed=size, transcendentals=0),
        compiler_params=pltpu.CompilerParams(vmem_limit_bytes=VMEM),
        name=name,
    )(order, *[x for x, _, _ in windows], *whole, *scalars)


def step_kernel(pieces, kinds, count, summed, order_ref, *refs):
    windows = {kind: refs[2 * i:2 * i + 2] for i, kind in enumerate(kinds)}
    blocks, refs = refs[2 * len(kinds):2 * len(kinds) + count], refs[2 * len(kinds) + count:]
    tokens = windows[kinds[0]][0].shape[0]
    for i, kind in enumerate(kinds):
        for k in range(2):
            at = pl.ds(k * tokens, tokens)
            total = refs[i][at] if summed else 0.0
            for which, row, height, of, column in pieces:
                if of == kind:
                    window = windows[kind][k][:, column:column + height]
                    total += dot(window, blocks[which][row:row + height])
            refs[i - len(kinds)][at] = total


def step(order, tokens_of, blocks, pieces, totals, s):
    kinds = sorted({piece[3] for piece in pieces})
    windows = []
    for kind in kinds:
        own, sib, width = tokens_of[kind]
        windows += [(x, width, lambda i, o: (0, o[s])) for x in (own, sib)]
    tokens, columns = windows[0][0].shape[0], blocks[0].shape[1]
    summed = all(kind in totals for kind in kinds)
    shape = jax.ShapeDtypeStruct((2 * tokens, columns), F32)
    out = call(
        functools.partial(step_kernel, pieces, kinds, len(blocks), summed),
        order, windows, list(blocks) + ([totals[k] for k in kinds] if summed else []), [],
        [shape] * len(kinds), 4 * tokens * sum(p[2] for p in pieces) * columns, "step",
    )
    return {**totals, **dict(zip(kinds, out))}


def window_kernel(lead, order_ref, own_ref, sib_ref, out_ref):
    tokens = own_ref.shape[0]
    out_ref[:tokens] = own_ref[:, :lead]
    out_ref[tokens:] = sib_ref[:, :lead]


EXTRA = 8


def turned_kernel(count, order_ref, *refs):
    windows, blocks = refs[:2 * count], refs[2 * count:3 * count]
    total_ref, seq_ref, len_ref, out_ref = refs[3 * count:]
    tokens = windows[0].shape[0]
    for k in range(2):
        at = pl.ds(k * tokens, tokens)
        total = total_ref[at]
        for w in range(count):
            total += dot(windows[2 * w + k][...], blocks[w][...])
        out_ref[at] = total
    held = seq_ref.shape[0]
    lane = lax.broadcasted_iota(jnp.int32, (EXTRA, out_ref.shape[1]), 1)
    numbers = jnp.zeros(lane.shape, F32)
    for i in range(held):
        numbers = jnp.where(lane == i, seq_ref[i].astype(F32), numbers)
        numbers = jnp.where(lane == held + i, len_ref[i].astype(F32), numbers)
    out_ref[2 * tokens:] = numbers


def masked_kernel(order_ref, own_ref, got_ref, out_ref):
    tokens = (own_ref.shape[0] - EXTRA) // 2
    columns = own_ref.shape[1]
    held = tokens // LEN
    position = lax.broadcasted_iota(jnp.int32, (LEN, columns), 0).astype(F32)
    for k, (mine, other) in enumerate(((own_ref, got_ref), (got_ref, own_ref))):
        for i in range(held):
            at, across = pl.ds(i * LEN, LEN), pl.ds(tokens + i * LEN, LEN)
            length = mine[2 * tokens:2 * tokens + 1, held + i:held + i + 1]
            out_ref[pl.ds(k * tokens + i * LEN, LEN)] = jnp.where(
                position < length, mine[at] + other[across], 0.0
            )
    lane = lax.broadcasted_iota(jnp.int32, (EXTRA, columns), 1)
    numbers = jnp.zeros(lane.shape, F32)
    for k, ref in enumerate((own_ref, got_ref)):
        for i in range(held):
            slot = ref[2 * tokens:2 * tokens + 1, i:i + 1]
            numbers = jnp.where(lane == k * held + i, slot, numbers)
    out_ref[2 * tokens:] = numbers


def score_kernel(per_device, window_ref, block_ref, total_ref, inn_ref, table_ref):
    height, columns = total_ref.shape
    queries = columns // RANK
    column = lax.broadcasted_iota(jnp.int32, (columns, queries), 0) // RANK
    query = lax.broadcasted_iota(jnp.int32, (columns, queries), 1)
    fold = (column == query).astype(F32)
    row = lax.broadcasted_iota(jnp.int32, table_ref.shape, 0)
    count = table_ref.shape[0] // per_device
    owner = lax.rem(2 * count - 2 - lax.div(row, per_device), count)
    row = (owner * per_device + lax.rem(row, per_device)).astype(F32)
    contrib = (total_ref[...] + dot(window_ref[...], block_ref[...])) * inn_ref[:height]
    count = height // LEN
    sums = [jnp.sum(contrib[i * LEN:(i + 1) * LEN], axis=0, keepdims=True) for i in range(count)]
    scores = jnp.dot(
        jnp.concatenate(sums), fold, precision=lax.Precision.HIGHEST, preferred_element_type=F32
    ) * (1.0 / math.sqrt(RANK * LEN))
    table = jnp.zeros(table_ref.shape, F32)
    for i in range(count):
        slot = inn_ref[height:height + 1, i:i + 1]
        table = jnp.where(row == slot, scores[i:i + 1], table)
    table_ref[...] = table


def score_table(arrays, per_device, rows, queries):
    vmem = pl.BlockSpec(memory_space=pltpu.VMEM)
    window, block = arrays[:2]
    size = sum(x.size * x.dtype.itemsize for x in arrays)
    return pl.pallas_call(
        functools.partial(score_kernel, per_device),
        in_specs=[vmem] * len(arrays),
        out_specs=vmem,
        out_shape=jax.ShapeDtypeStruct((rows, queries), F32),
        cost_estimate=pl.CostEstimate(
            flops=2 * window.size * block.shape[1], bytes_accessed=size, transcendentals=0
        ),
        compiler_params=pltpu.CompilerParams(vmem_limit_bytes=16 << 20),
        name="score",
    )(*arrays)


def shards(acts, grads, out_factors, in_factors, seq_slot, lengths):
    devices = lax.axis_size("dp")
    chips = devices // 2
    me = lax.axis_index("dp")
    tokens = grads.shape[0]
    rows, columns = out_factors.shape
    rows_in = in_factors.shape[0]
    orders = jnp.asarray(block_orders(chips))
    mine = lax.dynamic_index_in_dim(orders, me, keepdims=False)
    pairs = ring_pairs(chips)
    swap = [(d, d ^ 1) for d in range(devices)]

    send = lambda x: lax.ppermute(x, "dp", pairs)
    across = lambda x: lax.ppermute(x, "dp", swap)

    every = None
    if rows_in % 128:
        every = lax.all_gather(in_factors, "dp", axis=0, tiled=True)
        rows_in = 0
    lead = (rows - rows_in) // 2
    tokens_of = {"out": (grads, across(grads), rows)}
    if rows_in:
        tokens_of["in"] = (acts, across(acts), rows_in)

    inside = [(1, 0, rows_in, "in", 0)] if rows_in else []
    held = [[out_factors] + [in_factors] * (rows_in > 0)]
    pieces = [[(0, 0, rows, "out", 0)] + inside]
    came = send(out_factors)
    late, early = came[lead:], came[:lead]
    if rows_in:
        came, turned = lax.optimization_barrier((came, in_factors))
        turned = lax.ppermute(turned, "dp", [(j, i) for i, j in pairs])
        late, early = came[lead:], came[:lead]
        inner, turned = lax.optimization_barrier((send(in_factors), turned))
        early = jnp.concatenate([inner, early])
        backward = [(j, i) for i, j in pairs]
        turned = [turned, lax.ppermute(turned, "dp", backward)]
    totals, summed, last = {}, 0, chips - 1

    def sum_to(k, totals, summed):
        for j in range(summed, k):
            totals = step(mine, tokens_of, held[j], pieces[j], totals, j)
        return totals, max(k, summed)

    window = call(
        functools.partial(window_kernel, lead), mine,
        [(x, rows, lambda i, o: (0, o[last])) for x in tokens_of["out"][:2]], [], [],
        [jax.ShapeDtypeStruct((2 * tokens, lead), grads.dtype)], 0, "window",
    )[0]

    for s in range(1, chips):
        held.append([late, early])
        top = rows_in if s < last - 1 else 0
        pieces.append([(0, 0, rows - lead, "out", lead), (1, top, lead, "out", 0)])
        pieces[s] += inside if top else []
        if s == last:
            break
        if s >= 4:
            totals, summed = sum_to(min(2 * s - 6, s), totals, summed)
            late, totals = lax.optimization_barrier((late, totals))
            early, totals = lax.optimization_barrier((early, totals))
        if s == 4 and rows_in:
            early, turned = lax.optimization_barrier((early, turned))
        late = send(late)
        if s == last - 1:
            early, window = lax.optimization_barrier((early, window))
        early = send(early[rows_in:] if s == last - 2 else early)

    totals, summed = sum_to(last, totals, summed)
    slots = lengths.shape[0]
    height = (2 * tokens + EXTRA, columns)
    if rows_in:
        inn = call(
            functools.partial(turned_kernel, 2), mine,
            [
                (x, rows_in, functools.partial(lambda i, o, k: (0, o[k]), k=last - k))
                for k in (0, 1) for x in tokens_of["in"][:2]
            ],
            turned + [totals["in"]], [seq_slot, lengths],
            [jax.ShapeDtypeStruct(height, F32)], 8 * tokens * rows_in * columns, "turned",
        )[0]
    else:
        numbers = jnp.concatenate([seq_slot, lengths]).astype(F32)
        inn = jnp.zeros(height, F32).at[:tokens].set(dot(acts, every))
        inn = inn.at[2 * tokens, :2 * slots].set(numbers)
    inn = call(
        masked_kernel, mine, [], [inn, across(inn)], [],
        [jax.ShapeDtypeStruct(height, F32)], 0, "masked",
    )[0]
    totals = step(mine, tokens_of, [late], pieces[last][:1], totals, last)

    queries = columns // RANK
    table = score_table([window, early, totals["out"], inn], slots, slots * devices, queries)
    groups = [[(devices - 2 - k) % devices for k in range(devices)]]
    got = lax.all_to_all(
        table.reshape(devices, slots, queries), "dp", 0, 0, axis_index_groups=groups, tiled=True
    )
    return jnp.sum(got, axis=0)


def solution(mesh):
    return jax.shard_map(
        shards,
        mesh=mesh,
        in_specs=(
            P(("groups", "dp"), None),
            P(("groups", "dp"), None),
            P(("groups", "dp"), None),
            P(("groups", "dp"), None),
            P(("groups", "dp")),
            P(("groups", "dp")),
        ),
        out_specs=P(("groups", "dp"), None),
        check_vma=False,
    )
```
